128 devices in a mesh: ctx: 16 (over y, z_hi, core), fsdp: 8 (over x, z_lo).
Axes of the slice: x: 4, y: 4, z: 4 (z_hi: 2, z_lo: 2; z = z_hi * 2 + z_lo), core: 2. Of those that a mesh axis runs over, the one named last changes fastest.
Arguments:
- hidden_in: bfloat16 [8, 2048, 1024], P('fsdp', 'ctx'), may hold values from -6 to 6
- cotangent: bfloat16 [8, 2048, 1024], P('fsdp', 'ctx'), may hold values from -6 to 6
- block_deal: int32 [32], replicated, may hold values from 0 to 31, as said below
- routes: int32 [8, 2048, 8], P('fsdp', 'ctx'), may hold values from 0 to 31, all different within a row; in each aligned block of 128 rows (0 to 127, 128 to 255, ..., all dimensions but the last counted through in order) at most 40 rows name the same one
- query_key_value_weight: bfloat16 [4, 1024, 512], P(None, ('ctx', 'fsdp')), may hold values from -0.09375 to 0.09375
- output_weight_matrix: bfloat16 [2, 1024, 512], P(None, ('ctx', 'fsdp')), may hold values from -1.5 to 1.5
- router_weights: bfloat16 [1024, 32], P(('ctx', 'fsdp')), may hold values from -0.125 to 0.125
- norm_gains: bfloat16 [2, 1024], P(None, ('ctx', 'fsdp')), may hold values from 0.5 to 7.5
- expert_in: bfloat16 [32, 2, 1024, 512], P('ctx', None, 'fsdp'), may hold values from -0.1875 to 0.1875
- expert_out: bfloat16 [32, 1024, 512], P('ctx', 'fsdp'), may hold values from -0.1875 to 0.1875
- query_key_value_momentum: float32 [4, 1024, 512], P(None, ('ctx', 'fsdp')), may hold values from -2048 to 2048
- output_momentum: float32 [2, 1024, 512], P(None, ('ctx', 'fsdp')), may hold values from -112 to 112
- router_moment: float32 [1024, 32], P(('ctx', 'fsdp')), may hold values from -1792 to 1792
- gain_moment: float32 [2, 1024], P(None, ('ctx', 'fsdp')), may hold values from -56 to 56
- in_moment: float32 [32, 2, 1024, 512], P('ctx', None, 'fsdp'), may hold values from -128 to 128
- down_moment: float32 [32, 1024, 512], P('ctx', 'fsdp'), may hold values from -160 to 160
Outputs:
- hidden_out: bfloat16 [8, 2048, 1024], P('fsdp', 'ctx')
- input_grad: float32 [8, 2048, 1024], P('fsdp', 'ctx')
- qkv_grad: float32 [4, 1024, 512], P(None, ('ctx', 'fsdp'))
- out_grad: float32 [2, 1024, 512], P(None, ('ctx', 'fsdp'))
- router_grad: float32 [1024, 32], P(('ctx', 'fsdp'))
- gain_grad: float32 [2, 1024], P(None, ('ctx', 'fsdp'))
- in_grad: float32 [32, 2, 1024, 512], P('ctx', None, 'fsdp')
- down_grad: float32 [32, 1024, 512], P('ctx', 'fsdp')
- qkv_moment_new: float32 [4, 1024, 512], P(None, ('ctx', 'fsdp'))
- out_moment_new: float32 [2, 1024, 512], P(None, ('ctx', 'fsdp'))
- router_moment_new: float32 [1024, 32], P(('ctx', 'fsdp'))
- gain_moment_new: float32 [2, 1024], P(None, ('ctx', 'fsdp'))
- in_moment_new: float32 [32, 2, 1024, 512], P('ctx', None, 'fsdp')
- down_moment_new: float32 [32, 1024, 512], P('ctx', 'fsdp')
- qkv_new: float32 [4, 1024, 512], P(None, ('ctx', 'fsdp'))
- out_new: float32 [2, 1024, 512], P(None, ('ctx', 'fsdp'))
- router_new: float32 [1024, 32], P(('ctx', 'fsdp'))
- gains_new: float32 [2, 1024], P(None, ('ctx', 'fsdp'))
- in_new: float32 [32, 2, 1024, 512], P('ctx', None, 'fsdp')
- down_new: float32 [32, 1024, 512], P('ctx', 'fsdp')
The draws below stay inside these ranges and needn't reach their ends.
Inputs may be any that keep to these rules, and one draw needn't show every extreme that they name: block_deal names each of the 32 blocks once, and entries 2c and 2c + 1 name two blocks whose numbers sum to 31. `routes`: each token names 8 different experts. In each aligned block of 128 rows of a sequence no expert is named by more than 40 rows, a bound that some block reaches.
All inputs are finite; a program needn't handle non-finite values.
Results may differ from the reference program's by a relative error of at most 0.024.
Values may be sent and summed in bfloat16 or wider, within the bound.
A program may use at most 192 MiB of HBM per device.

```python
import math
import jax
import jax.numpy as jnp
import numpy as np
from jax import lax

MODEL_WIDTH = 1024
QUERY_HEADS = 16
KEY_VALUE_HEADS = 8
HEAD_WIDTH = 64
E = 32
FF = 512
TOP = 8
SEQUENCE_LENGTH = 2048
SCHULZ_STEPS = 2
BLOCKS = 32
TOK_DEV = 128
MOST = 40
SEQUENCE_COUNT = 8


def draw_block_deal(key, part):
    key = jax.random.fold_in(key, 11)
    pairs = BLOCKS // 2
    order = jax.random.permutation(key, pairs).astype(jnp.int32)
    flips = jax.random.randint(jax.random.fold_in(key, 5), (pairs,), 0, 2).astype(jnp.int32)
    mirror = BLOCKS - 1 - order
    leading = jnp.where(flips == 1, mirror, order)
    trailing = jnp.where(flips == 1, order, mirror)
    return jnp.stack([leading, trailing], 1).reshape(BLOCKS).astype(jnp.int32)


def draw_norm_gains(key, part):
    key = jax.random.fold_in(key, 23)
    fraction = jnp.arange(MODEL_WIDTH).astype(jnp.float32) / (MODEL_WIDTH - 1)
    rising = 1.0 + 2.0 * fraction
    factor = jnp.exp(jax.random.uniform(key, (2, MODEL_WIDTH), jnp.float32, -0.5, 0.33))
    return (rising[None, :] * factor).astype(jnp.bfloat16)


def block_levels(stream_key, shape, pieces, smallest, largest):
    factor_of = 1.0
    for axis_at, blocks in pieces:
        heights = jax.random.uniform(jax.random.fold_in(jax.random.fold_in(stream_key, 6), axis_at), (blocks,), jnp.float32, smallest / len(pieces), largest / len(pieces))
        factor_of = factor_of * jnp.repeat(jnp.exp(heights), shape[axis_at] // blocks).reshape((-1,) + (1,) * (len(shape) - 1 - axis_at))
    return factor_of


def routed_block(rng, own, number, rows, count, top, most, lean):
    ranking = jax.random.permutation(rng, count)
    crowded, common = portions_of(count, rows * top, most, lean, True), portions_of(count, rows * top, most, lean, False)
    places = jnp.arange(count)

    def named(lengths, offset_by):
        used = int((lengths > 0).sum())
        fixed = max(1, used // 4)
        moved = fixed + (places - fixed + offset_by * (used - fixed)) % max(1, count - fixed)
        return jnp.zeros((count,), jnp.int32).at[ranking[jnp.where(places < fixed, places, moved)]].set(jnp.asarray(lengths, jnp.int32))

    lengths = jnp.where(number % 4 == 0, named(crowded, number // 4), named(common, number - number // 4 - 1))
    mixed = jax.random.permutation(jax.random.fold_in(own, 3), count)
    donor, receiver = mixed[0:count // 2 * 2:2], mixed[1:count // 2 * 2:2]
    room = jnp.minimum(lengths[donor] - 1, most - lengths[receiver]) // 2
    room = jnp.where((donor == ranking[0]) | (receiver == ranking[0]) | (lengths[receiver] == 0), 0, jnp.maximum(room, 0))
    moved = jax.random.randint(jax.random.fold_in(own, 4), (count // 2,), 0, 1 << 20) % (room + 1)
    lengths = lengths.at[donor].add(-moved).at[receiver].add(moved)
    members = jnp.searchsorted(jnp.cumsum(lengths), jnp.arange(rows * top), side="right").astype(jnp.int32)
    listing = members.reshape(top, rows).T
    listing = listing[jax.random.permutation(jax.random.fold_in(own, 1), rows)]
    offset_by = jax.random.randint(jax.random.fold_in(own, 2), (rows, 1), 0, top)
    return jnp.take_along_axis(listing, (jnp.arange(top)[None, :] + offset_by) % top, axis=1)


def portions_of(number_of, total, limit, slope, full):
    weights = [(1 << 20) // math.isqrt(rank ** slope) + 1 for rank in range(1, number_of + 1)]
    largest = limit if full else min(limit, max(-(-total // number_of), total * weights[0] // sum(weights)))
    least = 1 if total - largest >= number_of - 1 else 0
    holding, surplus = [largest] + [least] * (number_of - 1), total - largest - least * (number_of - 1)
    while surplus > 0:
        free = [i for i in range(1, number_of) if holding[i] < largest] or [i for i in range(1, number_of) if holding[i] < limit]
        pool, budget = sum([weights[i] for i in free]), surplus
        for i in free:
            extra = min(limit - holding[i], max(1, budget * weights[i] // pool), surplus)
            holding[i] = holding[i] + extra
            surplus = surplus - extra
    return np.array(holding)


def gaussian(own_key, shape, deviation, most, pieces=(), kind=jnp.bfloat16):
    factor_of = block_levels(own_key, shape, pieces, -0.22, 0.18) if pieces else 1.0
    drawn = jax.random.normal(own_key, shape, jnp.float32) * deviation * factor_of
    return jnp.minimum(jnp.maximum(drawn, -most), most).astype(kind)


def setup_inputs(seed: int = 0) -> dict:
    keys = jax.random.split(jax.random.key(seed), 17)
    hidden_in = gaussian(keys[0], (SEQUENCE_COUNT, SEQUENCE_LENGTH, MODEL_WIDTH), 1.0, 6.0, ((0, 8), (1, 16)))
    cotangent = gaussian(keys[1], (SEQUENCE_COUNT, SEQUENCE_LENGTH, MODEL_WIDTH), 1.0, 6.0, ((0, 8), (1, 16)))
    block_deal = draw_block_deal(jax.random.fold_in(keys[16], 71), 0)
    routes_keys = jax.random.split(jax.random.fold_in(keys[3], 1), SEQUENCE_COUNT * SEQUENCE_LENGTH // TOK_DEV)
    routes_turns = jax.random.permutation(jax.random.fold_in(keys[3], 3), SEQUENCE_COUNT * SEQUENCE_LENGTH // TOK_DEV)
    routes = jax.vmap(lambda own, number: routed_block(jax.random.fold_in(keys[3], 2), own, number, TOK_DEV, E, TOP, MOST, 1))(routes_keys, routes_turns).reshape((SEQUENCE_COUNT, SEQUENCE_LENGTH, TOP))
    query_key_value_weight = gaussian(keys[4], (4, MODEL_WIDTH, KEY_VALUE_HEADS * HEAD_WIDTH), (4 * MODEL_WIDTH) ** -0.5, 0.09375, ((1, 128),))
    output_weight_matrix = gaussian(keys[5], (2, MODEL_WIDTH, KEY_VALUE_HEADS * HEAD_WIDTH), (max(QUERY_HEADS * HEAD_WIDTH // 64, 4)) ** -0.5, 1.5, ((1, 128),))
    router_weights = gaussian(keys[6], (MODEL_WIDTH, E), (0.25 * MODEL_WIDTH ** -0.5), 0.125, ((0, 128),))
    norm_gains = draw_norm_gains(jax.random.fold_in(keys[16], 71), 0)
    expert_in = gaussian(keys[8], (E, 2, MODEL_WIDTH, FF), MODEL_WIDTH ** -0.5, 0.1875, ((0, 16), (2, 8)))
    expert_out = gaussian(keys[9], (E, MODEL_WIDTH, FF), MODEL_WIDTH ** -0.5, 0.1875, ((0, 16), (1, 8)))
    query_key_value_momentum = gaussian(keys[10], (4, MODEL_WIDTH, KEY_VALUE_HEADS * HEAD_WIDTH), (2.5 * (SEQUENCE_COUNT * SEQUENCE_LENGTH) ** 0.5), 2048.0, ((1, 128),), jnp.float32)
    output_momentum = gaussian(keys[11], (2, MODEL_WIDTH, KEY_VALUE_HEADS * HEAD_WIDTH), (0.15 * (SEQUENCE_COUNT * SEQUENCE_LENGTH) ** 0.5), 112.0, ((1, 128),), jnp.float32)
    router_moment = gaussian(keys[12], (MODEL_WIDTH, E), (2.2 * (SEQUENCE_COUNT * SEQUENCE_LENGTH) ** 0.5), 1792.0, ((0, 128),), jnp.float32)
    gain_moment = gaussian(keys[13], (2, MODEL_WIDTH), (0.07 * (SEQUENCE_COUNT * SEQUENCE_LENGTH) ** 0.5), 56.0, ((1, 128),), jnp.float32)
    in_moment = gaussian(keys[14], (E, 2, MODEL_WIDTH, FF), (0.35 * (SEQUENCE_COUNT * SEQUENCE_LENGTH * TOP // E) ** 0.5), 128.0, ((0, 16), (2, 8)), jnp.float32)
    down_moment = gaussian(keys[15], (E, MODEL_WIDTH, FF), (0.45 * (SEQUENCE_COUNT * SEQUENCE_LENGTH * TOP // E) ** 0.5), 160.0, ((0, 16), (1, 8)), jnp.float32)
    return {"hidden_in": hidden_in, "cotangent": cotangent, "block_deal": block_deal, "routes": routes, "query_key_value_weight": query_key_value_weight, "output_weight_matrix": output_weight_matrix, "router_weights": router_weights, "norm_gains": norm_gains, "expert_in": expert_in, "expert_out": expert_out, "query_key_value_momentum": query_key_value_momentum, "output_momentum": output_momentum, "router_moment": router_moment, "gain_moment": gain_moment, "in_moment": in_moment, "down_moment": down_moment}


PRECISE = lax.Precision.HIGHEST
EPSILON = 1e-06
ROTARY_BASE = 10000.0
MOMENTUM_DECAY = 0.95
AVERAGE_DECAY = 0.9
SCHULZ_LINEAR = 3.4445
SCHULZ_SQUARE = -4.775
SCHULZ_CUBIC = 2.0315
WEIGHT_DECAY = 0.1
RATE_INPUT = 0.016
RATE_OUTPUT = 0.25
RATE_EXPERT = 0.031
RATE_DOWN = 0.031
RATE_GAIN = 0.5
RATE_ROUTER = 0.008
MASKED = -1e+30

@jax.custom_vjp
def lower_bound(v):
    return lax.optimization_barrier(v.astype(jnp.bfloat16)).astype(jnp.float32)

@jax.custom_vjp
def low_back(v):
    return v

def low_keep(v):
    return (lower_bound(v), None)

def low_pass(kept, grad):
    return (grad,)

def back_keep(v):
    return (v, None)

def back_low(kept, grad):
    return (lower_bound(grad),)
lower_bound.defvjp(low_keep, low_pass)
low_back.defvjp(back_keep, back_low)

def lower_both(value):
    return lower_bound(low_back(value))

def rotary_tables(token_positions, head_size):
    half_size = head_size // 2
    powers = jnp.arange(half_size).astype(jnp.float32) * (2.0 / head_size)
    frequency = jnp.exp(-math.log(ROTARY_BASE) * powers)
    angles = token_positions.astype(jnp.float32)[:, None] * frequency[None, :]
    return (jnp.cos(angles), jnp.sin(angles))

def apply_rotation(tensor, cosine_values, sine_lookup):
    half_size = tensor.shape[-1] // 2
    leading = tensor[..., :half_size]
    trailing = tensor[..., half_size:]
    table_shape = (tensor.shape[0],) + (1,) * (tensor.ndim - 2) + (half_size,)
    cosine_values = cosine_values.reshape(table_shape)
    sine_lookup = sine_lookup.reshape(table_shape)
    return jnp.concatenate([leading * cosine_values - trailing * sine_lookup, trailing * cosine_values + leading * sine_lookup], -1)

def orthogonal(matrix):
    scaled = matrix / (jnp.sqrt(jnp.sum(matrix * matrix)) + 1e-07)
    for sweep_index in range(SCHULZ_STEPS):
        gram_matrix = jnp.einsum('dw,dv->wv', scaled, scaled, precision=PRECISE)
        polynomial = SCHULZ_SQUARE * gram_matrix + SCHULZ_CUBIC * jnp.einsum('wv,vu->wu', gram_matrix, gram_matrix, precision=PRECISE)
        scaled = SCHULZ_LINEAR * scaled + jnp.einsum('dw,wv->dv', scaled, polynomial, precision=PRECISE)
    return scaled * math.sqrt(max(matrix.shape))

def layer_forward(tokens, weights_in, routed, token_positions, cosine_values, sine_lookup):
    qkv_full, out_full, router_full, gains_full, gateup_full, down_full = weights_in
    length_total = tokens.shape[0]
    block_width = qkv_full.shape[2]
    inverse_first = lax.rsqrt(lax.optimization_barrier(jnp.mean(tokens * tokens, -1, keepdims=True)) + EPSILON)
    normed = lower_bound(tokens * inverse_first * gains_full[0])
    project_rows = low_back(jnp.einsum('td,jdw->tjw', normed, qkv_full, precision=PRECISE))
    split_heads = project_rows.reshape(length_total, 4, KEY_VALUE_HEADS, HEAD_WIDTH)
    query_matrix = lower_bound(apply_rotation(split_heads[:, :2], cosine_values, sine_lookup)).reshape(length_total, KEY_VALUE_HEADS, QUERY_HEADS // KEY_VALUE_HEADS, HEAD_WIDTH)
    keys_rot = lower_bound(apply_rotation(split_heads[:, 2], cosine_values, sine_lookup))
    every_value = lower_bound(split_heads[:, 3])
    score_scale = 1.0 / math.sqrt(HEAD_WIDTH)
    block_of_queries = 512 if length_total % 512 == 0 else length_total
    block_total = length_total // block_of_queries

    def attend_over_block(packed):
        query_rows, query_pos = packed
        scores = low_back(jnp.einsum('qgrd,kgd->grqk', query_rows, keys_rot, precision=PRECISE) * score_scale)
        allowed = token_positions[None, :] <= query_pos[:, None]
        scores = jnp.where(allowed[None, None], scores, MASKED)
        weights = jax.nn.softmax(scores, axis=-1)
        return jnp.einsum('grqk,kgd->qgrd', lower_bound(weights), every_value, precision=PRECISE)
    mixture_output = lax.map(jax.checkpoint(attend_over_block), (query_matrix.reshape(block_total, block_of_queries, KEY_VALUE_HEADS, QUERY_HEADS // KEY_VALUE_HEADS, HEAD_WIDTH), token_positions.reshape(block_total, block_of_queries)))
    mixture_output = lower_both(mixture_output.reshape(length_total, 2, block_width))
    attention = low_back(jnp.einsum('tjw,jdw->td', mixture_output, out_full, precision=PRECISE))
    residual = tokens + attention
    inverse_second = lax.rsqrt(lax.optimization_barrier(jnp.mean(residual * residual, -1, keepdims=True)) + EPSILON)
    normed_second = lower_bound(residual * inverse_second * gains_full[1])
    logits = low_back(jnp.dot(normed_second, router_full, precision=PRECISE))
    gate_weights = jax.nn.softmax(jnp.take_along_axis(logits, routed, axis=1), axis=-1)
    flat_ids = routed.reshape(-1)
    onehot = (flat_ids[:, None] == jnp.arange(E, dtype=jnp.int32)[None, :]).astype(jnp.int32)
    slot_ranks = lax.optimization_barrier(jnp.sum(onehot * (jnp.cumsum(onehot, 0) - 1), -1))
    capacity = length_total // TOK_DEV * MOST
    assigns = length_total * TOP
    slot_table = jnp.full((E, capacity), assigns, jnp.int32).at[flat_ids, slot_ranks].set(jnp.arange(assigns, dtype=jnp.int32))
    padded = jnp.concatenate([normed_second, jnp.zeros((1, MODEL_WIDTH), jnp.float32)], 0)
    expert_rows = low_back(padded[slot_table // TOP])
    gate_up = low_back(jnp.einsum('ecd,ejdf->ejcf', expert_rows, gateup_full, precision=PRECISE))
    hidden = lower_bound(jax.nn.silu(gate_up[:, 0]) * gate_up[:, 1])
    outputs = lower_both(jnp.einsum('ecf,edf->ecd', hidden, down_full, precision=PRECISE))
    slot_index = flat_ids * capacity + slot_ranks
    returned = outputs.reshape(E * capacity, MODEL_WIDTH)[slot_index].reshape(length_total, TOP, MODEL_WIDTH)
    blended = lax.optimization_barrier(jnp.sum(gate_weights[:, :, None] * returned, 1))
    return residual + blended

def reference(hidden_in, cotangent, block_deal, routes, query_key_value_weight, output_weight_matrix, router_weights, norm_gains, expert_in, expert_out, query_key_value_momentum, output_momentum, router_moment, gain_moment, in_moment, down_moment):
    row_ids = jnp.arange(SEQUENCE_LENGTH, dtype=jnp.int32)
    block_rows = SEQUENCE_LENGTH // BLOCKS
    token_positions = block_deal[row_ids // block_rows] * block_rows + row_ids % block_rows
    cosine_values, sine_lookup = rotary_tables(token_positions, HEAD_WIDTH)
    params = (query_key_value_weight.astype(jnp.float32), output_weight_matrix.astype(jnp.float32), router_weights.astype(jnp.float32), norm_gains.astype(jnp.float32), expert_in.astype(jnp.float32), expert_out.astype(jnp.float32))

    def one_sequence(running, packed):
        tokens, cotan_rows, routed_rows = packed

        def forward(tokens_in, *weights_in):
            return layer_forward(tokens_in, weights_in, routed_rows, token_positions, cosine_values, sine_lookup)
        output_rows, pullback = jax.vjp(forward, tokens.astype(jnp.float32), *params)
        gradients = pullback(cotan_rows.astype(jnp.float32))
        running = tuple((running_sum + fresh_grad for running_sum, fresh_grad in zip(running, gradients[1:])))
        return (running, (output_rows.astype(jnp.bfloat16), gradients[0]))
    initial = tuple((jnp.zeros_like(param) for param in params))
    totals, (hidden_out, input_grad) = lax.scan(one_sequence, initial, (hidden_in, cotangent, routes))
    qkv_grad, out_grad, router_grad, gain_grad, in_grad, down_grad = totals
    qkv_f, out_f, router_f, gains_f, in_f, down_f = params
    many_orthogonal = jax.vmap(orthogonal)
    qkv_moment_new = MOMENTUM_DECAY * query_key_value_momentum + qkv_grad
    out_moment_new = MOMENTUM_DECAY * output_momentum + out_grad
    in_moment_new = MOMENTUM_DECAY * in_moment + in_grad
    down_moment_new = MOMENTUM_DECAY * down_moment + down_grad
    qkv_new = qkv_f * (1.0 - RATE_INPUT * WEIGHT_DECAY) - RATE_INPUT * many_orthogonal(qkv_moment_new)
    out_new = out_f * (1.0 - RATE_OUTPUT * WEIGHT_DECAY) - RATE_OUTPUT * many_orthogonal(out_moment_new)
    in_ortho = many_orthogonal(in_moment_new.reshape(E * 2, MODEL_WIDTH, FF)).reshape(E, 2, MODEL_WIDTH, FF)
    in_new = in_f * (1.0 - RATE_EXPERT * WEIGHT_DECAY) - RATE_EXPERT * in_ortho
    down_new = down_f * (1.0 - RATE_DOWN * WEIGHT_DECAY) - RATE_DOWN * many_orthogonal(down_moment_new)
    gain_moment_new = AVERAGE_DECAY * gain_moment + (1.0 - AVERAGE_DECAY) * gain_grad
    router_moment_new = AVERAGE_DECAY * router_moment + (1.0 - AVERAGE_DECAY) * router_grad
    gains_new = gains_f - RATE_GAIN * gain_moment_new * lax.rsqrt(lax.optimization_barrier(jnp.mean(gain_moment_new * gain_moment_new, -1, keepdims=True)) + EPSILON)
    router_new = router_f - RATE_ROUTER * router_moment_new * lax.rsqrt(jnp.mean(router_moment_new * router_moment_new) + EPSILON)
    return (hidden_out, input_grad, qkv_grad, out_grad, router_grad, gain_grad, in_grad, down_grad, qkv_moment_new, out_moment_new, router_moment_new, gain_moment_new, in_moment_new, down_moment_new, qkv_new, out_new, router_new, gains_new, in_new, down_new)
```

```python
import functools
import math

import jax
import jax.numpy as jnp
from jax import lax
from jax.experimental import pallas as pl
from jax.experimental.pallas import tpu as pltpu
from jax.sharding import PartitionSpec as P

MODEL_WIDTH = 1024
QUERY_HEADS = 16
KEY_VALUE_HEADS = 8
HEAD_WIDTH = 64
E = 32
TOP = 8
MOST = 40
SCHULZ_STEPS = 2


EPSILON = 1e-06
ROTARY_BASE = 10000.0
MOMENTUM_DECAY = 0.95
AVERAGE_DECAY = 0.9
SCHULZ_LINEAR = 3.4445
SCHULZ_SQUARE = -4.775
SCHULZ_CUBIC = 2.0315
WEIGHT_DECAY = 0.1
RATE_INPUT = 0.016
RATE_OUTPUT = 0.25
RATE_EXPERT = 0.031
RATE_DOWN = 0.031
RATE_GAIN = 0.5
RATE_ROUTER = 0.008
MASKED = -1e30

MESH = pl.DeviceIdType.MESH
RING = {"x": 4, "y": 4, "z": 4, "zh": 2, "zl": 2, "c": 2}
EVERY = ("y", "zh", "c", "x", "zl")
ALONG_CTX = ("y", "zh", "c")
ALONG_FSDP = ("x", "zl")


def place():
    ctx = lax.axis_index("ctx")
    fsdp = lax.axis_index("fsdp")
    at = {"y": ctx // 4, "zh": (ctx // 2) % 2, "c": ctx % 2, "x": fsdp // 2, "zl": fsdp % 2}
    at["z"] = at["zh"] * 2 + at["zl"]
    return at


def moved(at, dim, to):
    at = dict(at)
    at[dim] = to
    if dim == "z":
        at["zh"], at["zl"] = to // 2, to % 2
    return at


def device_at(at):
    return ((at["y"] * 2 + at["zh"]) * 2 + at["c"], at["x"] * 2 + at["zl"])


def greet(peers):
    barrier = pltpu.get_barrier_semaphore()
    for peer in peers:
        pl.semaphore_signal(barrier, inc=1, device_id=peer, device_id_type=MESH)
    pl.semaphore_wait(barrier, len(peers))


def network_dims(jobs):
    found = []
    for job in jobs:
        for piece in job[1]:
            for dim in piece[2]:
                if dim not in found:
                    found.append(dim)
        if "c" in job[0] and "c" not in found:
            found.append("c")
    return found


def gather_copies(jobs):
    total = 0
    for dims, pieces in jobs:
        shared = 1 if "c" in dims else 0
        for _, _, order in pieces:
            total += shared
            for dim in order:
                total += 1 + shared if RING[dim] == 2 else 4 + 3 * shared
    return total


def gather_kernel(jobs, *refs):
    n = len(jobs)
    sources, targets = refs[:n], refs[n : 2 * n]
    send_sems, recv_sems, local_sems = refs[2 * n :]
    me = place()
    peers = []
    for dim in network_dims(jobs):
        size = RING[dim]
        for step in (1,) if size == 2 else (1, 3):
            peers.append(device_at(moved(me, dim, (me[dim] + step) % size)))
    own = []
    for j, (dims, _) in enumerate(jobs):
        copy = pltpu.make_async_copy(
            sources[j], targets[j].at[tuple(me[d] for d in dims)], local_sems.at[j]
        )
        copy.start()
        own.append(copy)
    greet(peers)
    for copy in own:
        copy.wait()
    copies, to_other_core = [], []

    def flow(j, dims, first, rows, order):
        target = targets[j]
        columns = target.shape[-1]

        def view(sel, half):
            index = tuple(sel[d] for d in dims) + (pl.ds(first, rows),)
            if half is not None:
                index = index + (pl.ds(half * (columns // 2), columns // 2),)
            return target.at[index]

        def send(sel, dim, to, half=None):
            k = len(copies)
            part = view(sel, half)
            copy = pltpu.make_async_remote_copy(
                src_ref=part,
                dst_ref=part,
                send_sem=send_sems.at[k],
                recv_sem=recv_sems.at[k],
                device_id=device_at(moved(me, dim, to)),
                device_id_type=MESH,
            )
            copy.start()
            copies.append(copy)
            return copy

        def share(sel):
            if "c" in dims:
                to_other_core.append(send(sel, "c", 1 - me["c"]))

        def whole(sel, dim):
            if dim == "z":
                return dict(sel, zh=pl.ds(0, 2), zl=pl.ds(0, 2))
            return dict(sel, **{dim: pl.ds(0, RING[dim])})

        sel = dict(me)
        share(sel)
        for dim in order:
            if RING[dim] == 2:
                copy = send(sel, dim, 1 - me[dim])
                yield
                copy.wait_recv()
                share(moved(sel, dim, 1 - me[dim]))
            else:
                right, left = (me[dim] + 1) % 4, (me[dim] + 3) % 4
                up = send(sel, dim, right)
                down = send(sel, dim, left)
                yield
                up.wait_recv()
                on_up = send(moved(sel, dim, left), dim, right, 0)
                share(moved(sel, dim, left))
                down.wait_recv()
                on_down = send(moved(sel, dim, right), dim, left, 1)
                share(moved(sel, dim, right))
                yield
                on_up.wait_recv()
                on_down.wait_recv()
                share(moved(sel, dim, (me[dim] + 2) % 4))
            sel = whole(sel, dim)

    live = [flow(j, dims, *piece) for j, (dims, pieces) in enumerate(jobs) for piece in pieces]
    while live:
        live = [f for f in live if next(f, "end") != "end"]
    for copy in to_other_core:
        copy.wait_recv()
    for copy in copies:
        copy.wait_send()


def gather(jobs, blocks, collective_id):
    n = gather_copies(jobs)
    return pl.pallas_call(
        functools.partial(gather_kernel, jobs),
        out_shape=[
            jax.ShapeDtypeStruct(tuple(RING[d] for d in dims) + b.shape, b.dtype)
            for (dims, _), b in zip(jobs, blocks)
        ],
        in_specs=[pl.BlockSpec(memory_space=pl.ANY)] * len(jobs),
        out_specs=[pl.BlockSpec(memory_space=pl.ANY)] * len(jobs),
        scratch_shapes=[
            pltpu.SemaphoreType.DMA((n,)),
            pltpu.SemaphoreType.DMA((n,)),
            pltpu.SemaphoreType.DMA((len(jobs),)),
        ],
        compiler_params=pltpu.CompilerParams(collective_id=collective_id, has_side_effects=True),
        cost_estimate=pl.CostEstimate(flops=0, bytes_accessed=60_000_000, transcendentals=0),
    )(*blocks)


def dims_without(dims, dim):
    drop = ("zh", "zl") if dim == "z" else (dim,)
    return tuple(d for d in dims if d not in drop)


def scatter_buffers(jobs, shapes):
    buffers, sems = [], 0
    for (dims, pieces), shape in zip(jobs, shapes):
        for _, rows, order in pieces:
            left = dims
            for dim in order:
                left = dims_without(left, dim)
                block = tuple(RING[d] for d in left) + (rows, shape[-1])
                buffers.append(pltpu.VMEM((RING[dim] - 1,) + block, jnp.bfloat16))
                if left:
                    buffers.append(pltpu.VMEM(block, jnp.bfloat16))
                sems += RING[dim] - 1
    return buffers, sems


def scatter_kernel(jobs, *refs):
    n = len(jobs)
    sources, targets = refs[:n], refs[n : 2 * n]
    buffers = list(refs[2 * n : -2])
    send_sems, recv_sems = refs[-2:]
    me = place()
    peers = []
    for dim in network_dims(jobs):
        for step in range(1, RING[dim]):
            peers.append(device_at(moved(me, dim, (me[dim] + step) % RING[dim])))
    greet(peers)
    copies = []

    def run(j, dims, first, rows, order, held):
        current, left, span = sources[j], dims, pl.ds(first, rows)
        for (landing, total), dim in zip(held, order):
            size = RING[dim]
            rest = dims_without(left, dim)

            def pick(at, inner):
                return tuple(inner[d] if d in inner else at[d] for d in left) + (span,)

            every = {d: pl.ds(0, RING[d]) for d in rest}
            mine = []
            for step in range(1, size):
                other = moved(me, dim, (me[dim] + step) % size)
                k = len(copies)
                copy = pltpu.make_async_remote_copy(
                    src_ref=current.at[pick(other, every)],
                    dst_ref=landing.at[step - 1],
                    send_sem=send_sems.at[k],
                    recv_sem=recv_sems.at[k],
                    device_id=device_at(other),
                    device_id_type=MESH,
                )
                copy.start()
                copies.append(copy)
                mine.append(copy)
            yield
            for copy in mine:
                copy.wait_recv()
            blocks = math.prod(RING[d] for d in rest)
            out_span = pl.ds(0, rows) if rest else pl.ds(first, rows)

            def add(i, carry, current=current, landing=landing, total=total, rest=rest, pick=pick):
                inner, remains = {}, i
                for d in reversed(rest):
                    inner[d] = remains % RING[d]
                    remains = remains // RING[d]
                index = tuple(inner[d] for d in rest)
                value = current[pick(me, inner)].astype(jnp.float32)
                for step in range(size - 1):
                    value += landing[(step,) + index].astype(jnp.float32)
                total[index + (out_span,)] = value.astype(total.dtype)
                return carry

            if blocks == 1:
                add(0, 0)
            else:
                lax.fori_loop(0, blocks, add, 0)
            current, left, span = total, rest, pl.ds(0, rows)

    live = []
    for j, (dims, pieces) in enumerate(jobs):
        for first, rows, order in pieces:
            held, left = [], dims
            for dim in order:
                left = dims_without(left, dim)
                landing = buffers.pop(0)
                held.append((landing, buffers.pop(0) if left else targets[j]))
            live.append(run(j, dims, first, rows, order, held))
    while live:
        live = [f for f in live if next(f, "end") != "end"]
    for copy in copies:
        copy.wait_send()


def scatter(jobs, blocks, collective_id):
    buffers, n = scatter_buffers(jobs, [b.shape for b in blocks])
    return pl.pallas_call(
        functools.partial(scatter_kernel, jobs),
        out_shape=[jax.ShapeDtypeStruct(b.shape[-2:], jnp.float32) for b in blocks],
        in_specs=[pl.BlockSpec(memory_space=pltpu.VMEM)] * len(jobs),
        out_specs=[pl.BlockSpec(memory_space=pltpu.VMEM)] * len(jobs),
        scratch_shapes=buffers
        + [pltpu.SemaphoreType.DMA((n,)), pltpu.SemaphoreType.DMA((n,))],
        compiler_params=pltpu.CompilerParams(
            collective_id=collective_id, has_side_effects=True, vmem_limit_bytes=50 * 2**20
        ),
        cost_estimate=pl.CostEstimate(flops=0, bytes_accessed=60_000_000, transcendentals=0),
    )(*blocks)


def apply_rotation(tensor, cosine_values, sine_lookup):
    half_size = tensor.shape[-1] // 2
    leading = tensor[..., :half_size]
    trailing = tensor[..., half_size:]
    table_shape = (tensor.shape[0],) + (1,) * (tensor.ndim - 2) + (half_size,)
    cosine_values = cosine_values.reshape(table_shape)
    sine_lookup = sine_lookup.reshape(table_shape)
    return jnp.concatenate(
        [
            leading * cosine_values - trailing * sine_lookup,
            trailing * cosine_values + leading * sine_lookup,
        ],
        -1,
    )


def low(value):
    return value.astype(jnp.bfloat16)


def high(value):
    return value.astype(jnp.float32)


def product(spec, left, right):
    return jnp.einsum(spec, low(left), low(right), preferred_element_type=jnp.float32)


def orthogonal(matrix):
    scaled = matrix / (jnp.sqrt(jnp.sum(matrix * matrix)) + 1e-07)
    for sweep_index in range(SCHULZ_STEPS):
        gram_matrix = product("dw,dv->wv", scaled, scaled)
        polynomial = SCHULZ_SQUARE * gram_matrix + SCHULZ_CUBIC * product(
            "wv,vu->wu", gram_matrix, gram_matrix
        )
        scaled = SCHULZ_LINEAR * scaled + product("dw,wv->dv", scaled, polynomial)
    return scaled * math.sqrt(max(matrix.shape))


def norm_backward(values_in, inverse, gain_row, grad_normed):
    weighted = gain_row * grad_normed
    grad_values = inverse * weighted - values_in * inverse**3 * jnp.mean(
        weighted * values_in, -1, keepdims=True
    )
    grad_gain = jnp.sum(grad_normed * values_in * inverse, 0)
    return (grad_values, grad_gain)


def two_halves(value):
    upper = low(value)
    return upper, low(value - high(upper))


def slots_of(chosen):
    rows = chosen.shape[1]
    before = jnp.tril(jnp.ones((rows, rows), jnp.bfloat16), -1)
    rank = jnp.einsum("st,bte->bes", before, low(chosen), preferred_element_type=jnp.float32)
    taken = jnp.swapaxes(chosen, 1, 2)
    slot = jnp.arange(MOST, dtype=jnp.int32)[None, None, :, None]
    filled = (rank.astype(jnp.int32)[:, :, None, :] == slot) & (taken[:, :, None, :] > 0.5)
    return filled


ATTENTION_WEIGHTS = (
    (
        EVERY,
        (
            (48, 16, ("x", "y", "z")),
            (0, 16, ("x", "y", "z")),
            (16, 16, ("y", "z", "x")),
            (32, 16, ("z", "x", "y")),
        ),
    ),
)
ROWS_OF_CTX = ((ALONG_CTX, ((0, 64, ("zh", "y")), (64, 64, ("zh", "y")))),)
SUM_OF_CTX = ((ALONG_CTX, ((0, 64, ("c", "y", "zh")), (64, 64, ("c", "y", "zh")))),)
SUM_OF_ALL = (
    (
        EVERY,
        (
            (0, 16, ("c", "x", "y", "z")),
            (16, 16, ("c", "y", "z", "x")),
            (32, 16, ("c", "z", "x", "y")),
            (48, 16, ("c", "x", "y", "z")),
        ),
    ),
)


def on_device(
    hidden_in,
    cotangent,
    block_deal,
    routes,
    query_key_value_weight,
    output_weight_matrix,
    router_weights,
    norm_gains,
    expert_in,
    expert_out,
    query_key_value_momentum,
    output_momentum,
    router_moment,
    gain_moment,
    in_moment,
    down_moment,
):
    ctx_count = lax.axis_size("ctx")
    fsdp_count = lax.axis_size("fsdp")
    device_count = ctx_count * fsdp_count
    ctx_index = lax.axis_index("ctx")
    rows = hidden_in.shape[1]
    sequence_length = rows * ctx_count
    half_rows = rows // 2
    shard = query_key_value_weight.shape[1]
    width = query_key_value_weight.shape[2]
    group_width = QUERY_HEADS // KEY_VALUE_HEADS
    score_scale = 1.0 / math.sqrt(HEAD_WIDTH)

    steps = jnp.arange(half_rows, dtype=jnp.int32)[None, :]
    token_positions = (block_deal[:, None] * half_rows + steps).reshape(sequence_length)
    local_deal = lax.dynamic_slice_in_dim(block_deal, ctx_index * 2, 2)
    local_pos = (local_deal[:, None] * half_rows + steps).reshape(rows)
    half_size = HEAD_WIDTH // 2
    powers = jnp.arange(half_size).astype(jnp.float32) * (2.0 / HEAD_WIDTH)
    frequency = jnp.exp(-math.log(ROTARY_BASE) * powers)
    angles = local_pos.astype(jnp.float32)[:, None] * frequency[None, :]
    cosine_values, sine_lookup = jnp.cos(angles), jnp.sin(angles)
    allowed = token_positions[None, :] <= local_pos[:, None]

    spare = jnp.zeros((16, width), jnp.bfloat16)
    spare = spare.at[0, : shard * E].set(router_weights.reshape(-1))
    spare = spare.at[1, : 2 * shard].set(norm_gains.reshape(-1))
    packed = jnp.concatenate(
        [
            query_key_value_weight.reshape(4 * shard, width),
            output_weight_matrix.reshape(2 * shard, width),
            spare,
        ],
        0,
    )
    (weights,) = gather(ATTENTION_WEIGHTS, [packed], 1)
    weights = weights.reshape(device_count, 8 * shard, width)
    qkv_full = (
        weights[:, : 4 * shard]
        .reshape(device_count, 4, shard, width)
        .transpose(1, 0, 2, 3)
        .reshape(4, MODEL_WIDTH, width)
    )
    out_full = (
        weights[:, 4 * shard : 6 * shard]
        .reshape(device_count, 2, shard, width)
        .transpose(1, 0, 2, 3)
        .reshape(2, MODEL_WIDTH, width)
    )
    router_full = weights[:, 6 * shard, : shard * E].reshape(MODEL_WIDTH, E)
    gains_full = (
        weights[:, 6 * shard + 1, : 2 * shard]
        .reshape(device_count, 2, shard)
        .transpose(1, 0, 2)
        .reshape(2, MODEL_WIDTH)
    )

    part = expert_in.shape[2]
    experts_here = expert_in.shape[0]
    expert_block = jnp.concatenate([expert_in, expert_out[:, None]], 1).reshape(
        experts_here * 3 * part, width
    )
    expert_full = lax.all_gather(expert_block, "fsdp", axis=0)
    cotangent_all = lax.all_gather(cotangent[0], "ctx", axis=0)

    tokens = high(hidden_in[0])
    inverse_first = lax.rsqrt(jnp.mean(tokens * tokens, -1, keepdims=True) + EPSILON)
    gain_first = high(gains_full[0])
    normed = low(tokens * inverse_first * gain_first)
    project_rows = product("td,jdw->tjw", normed, qkv_full)
    split_heads = project_rows.reshape(rows, 4, KEY_VALUE_HEADS, HEAD_WIDTH)
    query_matrix = low(apply_rotation(split_heads[:, :2], cosine_values, sine_lookup))
    keys_local = low(apply_rotation(split_heads[:, 2], cosine_values, sine_lookup))
    values_local = low(split_heads[:, 3])
    (keys_values,) = gather(
        ROWS_OF_CTX,
        [jnp.concatenate([keys_local.reshape(rows, width), values_local.reshape(rows, width)], 1)],
        2,
    )
    keys_values = keys_values.reshape(sequence_length, 2, KEY_VALUE_HEADS, HEAD_WIDTH)
    every_key, every_value = keys_values[:, 0], keys_values[:, 1]
    heads_of_query = query_matrix.reshape(rows, KEY_VALUE_HEADS, group_width, HEAD_WIDTH)

    scores = product("qgrd,kgd->grqk", heads_of_query, every_key) * score_scale
    scores = jnp.where(allowed[None, None], scores, MASKED)
    row_peak = jnp.max(scores, -1, keepdims=True)
    exponent = jnp.exp(scores - row_peak)
    row_total = jnp.sum(exponent, -1, keepdims=True)
    log_total = row_peak + jnp.log(row_total)
    mixture_rows = low(product("grqk,kgd->qgrd", low(exponent / row_total), every_value)).reshape(
        rows, 2, width
    )
    residual = tokens + product("tjw,jdw->td", mixture_rows, out_full)
    inverse_second = lax.rsqrt(jnp.mean(residual * residual, -1, keepdims=True) + EPSILON)
    gain_second = high(gains_full[1])
    normed_second = low(residual * inverse_second * gain_second)
    logits = product("td,de->te", normed_second, router_full)
    routed = routes[0]
    chosen = jnp.sum(
        high(routed[:, :, None] == jnp.arange(E, dtype=jnp.int32)[None, None, :]), 1
    )
    peak = jnp.max(jnp.where(chosen > 0.5, logits, MASKED), -1, keepdims=True)
    weighed = jnp.where(chosen > 0.5, jnp.exp(jnp.minimum(logits - peak, 0.0)), 0.0)
    gates = weighed / jnp.sum(weighed, -1, keepdims=True)
    upstream = high(cotangent[0])

    gate_upper, gate_lower = two_halves(gates)
    (sent,) = gather(
        ROWS_OF_CTX,
        [
            jnp.concatenate(
                [normed_second, gate_upper, gate_lower, low(chosen), jnp.zeros_like(gate_upper)]
                + [jnp.zeros_like(gate_upper)] * 4,
                1,
            )
        ],
        3,
    )
    sent = sent.reshape(ctx_count, rows, MODEL_WIDTH + 8 * E)

    def mine(start):
        return lax.dynamic_slice_in_dim(
            sent, MODEL_WIDTH + start + ctx_index * experts_here, experts_here, 2
        )

    gates_mine = high(mine(0)) + high(mine(E))
    filled = slots_of(high(mine(2 * E)))
    picks = low(filled)
    capacity = ctx_count * MOST
    row_gates = jnp.sum(
        jnp.where(filled, jnp.swapaxes(gates_mine, 1, 2)[:, :, None, :], 0.0), -1
    ).transpose(1, 0, 2).reshape(experts_here, capacity, 1)

    def select(values):
        found = low(product("bert,btd->ebrd", picks, values))
        return found.reshape(experts_here, capacity, MODEL_WIDTH)

    expert_rows = select(sent[:, :, :MODEL_WIDTH])
    upstream_rows = high(select(cotangent_all))
    expert_full = expert_full.reshape(fsdp_count, experts_here, 3, part, width).transpose(
        1, 2, 0, 3, 4
    ).reshape(experts_here, 3, MODEL_WIDTH, width)
    gateup_full, down_full = expert_full[:, :2], expert_full[:, 2]
    gate_up = product("erd,ejdf->ejrf", expert_rows, gateup_full)
    upper_pre, lower_pre = gate_up[:, 0], gate_up[:, 1]
    sigmoid_up = jax.nn.sigmoid(upper_pre)
    hidden = low(upper_pre * sigmoid_up * lower_pre)
    outputs = high(low(product("erf,edf->erd", hidden, down_full)))
    row_grads = low(row_gates * upstream_rows)
    row_dgate = jnp.sum(upstream_rows * outputs, -1)
    grad_hidden = product("erd,edf->erf", row_grads, down_full)
    grad_upper = grad_hidden * lower_pre * sigmoid_up * (1.0 + upper_pre * (1.0 - sigmoid_up))
    grad_lower = grad_hidden * (upper_pre * sigmoid_up)
    grad_both = low(jnp.stack([grad_upper, grad_lower], 1))
    back_rows = low(product("ejrf,ejdf->erd", grad_both, gateup_full))

    def by_block(values):
        values = values.reshape(experts_here, ctx_count, MOST, values.shape[-1])
        return values.transpose(1, 0, 2, 3).reshape(ctx_count, experts_here * MOST, -1)

    dgate_upper, dgate_lower = two_halves(by_block(row_dgate[:, :, None])[:, :, 0])
    dgate_rows = jnp.stack([dgate_upper, dgate_lower], 1)
    dgate_rows = jnp.pad(
        dgate_rows, ((0, 0), (0, 6), (0, MODEL_WIDTH - experts_here * MOST))
    )
    back_sent = jnp.concatenate([by_block(back_rows), dgate_rows], 1)
    back_returned = lax.all_to_all(back_sent, "ctx", split_axis=0, concat_axis=0, tiled=True)
    blend_sent = by_block(low(row_gates * outputs))
    blend_sent, back_returned = lax.optimization_barrier((blend_sent, back_returned))
    blend_returned = lax.all_to_all(blend_sent, "ctx", split_axis=0, concat_axis=0, tiled=True)

    grad_experts = jnp.concatenate(
        [
            low(product("erd,ejrf->ejdf", expert_rows, grad_both)),
            low(product("erd,erf->edf", row_grads, hidden))[:, None],
        ],
        1,
    )
    grad_experts = (
        grad_experts.reshape(experts_here * 3, fsdp_count, part, width)
        .transpose(1, 0, 2, 3)
        .reshape(fsdp_count * experts_here * 3 * part, width)
    )
    expert_grad = lax.psum_scatter(grad_experts, "fsdp", scatter_dimension=0, tiled=True)

    own_filled = slots_of(chosen[None])[0]
    own_picks = low(own_filled).reshape(E * MOST, rows)
    back_values = back_returned[:, : experts_here * MOST].reshape(E * MOST, MODEL_WIDTH)
    back_sum = product("st,sd->td", own_picks, back_values)
    own_dgate = high(back_returned[:, experts_here * MOST, : experts_here * MOST]) + high(
        back_returned[:, experts_here * MOST + 1, : experts_here * MOST]
    )
    grad_gates = jnp.sum(
        jnp.where(own_filled, own_dgate.reshape(E, MOST, 1), 0.0), 1
    ).T
    grad_logits = low(gates * (grad_gates - jnp.sum(gates * grad_gates, -1, keepdims=True)))
    grad_router_part = product("td,te->de", normed_second, grad_logits)
    grad_normed_second = back_sum + product("te,de->td", grad_logits, router_full)
    grad_residual_norm, grad_gain_second = norm_backward(
        residual, inverse_second, gain_second, grad_normed_second
    )
    grad_residual = upstream + grad_residual_norm
    grad_attention = low(grad_residual)
    grad_out_part = product("td,tjw->jdw", grad_attention, mixture_rows)
    mixture_gradient = low(product("td,jdw->tjw", grad_attention, out_full))
    head_gradient = mixture_gradient.reshape(rows, KEY_VALUE_HEADS, group_width, HEAD_WIDTH)

    probabilities = jnp.exp(scores - log_total)
    grad_probs = product("qgrd,kgd->grqk", head_gradient, every_value)
    grad_scores = low(
        probabilities * (grad_probs - jnp.sum(probabilities * grad_probs, -1, keepdims=True))
    )
    query_gradient = product("grqk,kgd->qgrd", grad_scores, every_key) * score_scale
    grad_key = product("grqk,qgrd->kgd", grad_scores, heads_of_query) * score_scale
    grad_value = product("grqk,qgrd->kgd", probabilities, head_gradient)
    grad_keys_values = low(
        jnp.concatenate(
            [grad_key.reshape(sequence_length, width), grad_value.reshape(sequence_length, width)],
            1,
        )
    )
    (local_gradient,) = scatter(
        SUM_OF_CTX, [grad_keys_values.reshape(4, 2, 2, rows, 2 * width)], 4
    )
    query_row_gradient = apply_rotation(
        query_gradient.reshape(rows, 2, KEY_VALUE_HEADS, HEAD_WIDTH), cosine_values, -sine_lookup
    )
    key_row_gradient = apply_rotation(
        local_gradient[:, :width].reshape(rows, KEY_VALUE_HEADS, HEAD_WIDTH),
        cosine_values,
        -sine_lookup,
    )
    grad_project = low(
        jnp.concatenate(
            [
                query_row_gradient.reshape(rows, 2, width),
                key_row_gradient.reshape(rows, 1, width),
                local_gradient[:, width:].reshape(rows, 1, width),
            ],
            1,
        )
    )
    grad_qkv_part = product("td,tjw->jdw", normed, grad_project)
    grad_normed_first = product("tjw,jdw->td", grad_project, qkv_full)
    grad_tokens_norm, grad_gain_first = norm_backward(
        tokens, inverse_first, gain_first, grad_normed_first
    )
    input_grad = (grad_residual + grad_tokens_norm)[None]

    def by_device(values):
        values = low(values).reshape(values.shape[0], device_count, shard, width)
        return values.transpose(1, 0, 2, 3).reshape(device_count, -1, width)

    gains_part = jnp.stack([grad_gain_first, grad_gain_second], 0)
    gains_part = gains_part.reshape(2, device_count, shard).transpose(1, 0, 2)
    spare_part = jnp.concatenate(
        [
            jnp.pad(
                low(grad_router_part).reshape(device_count, 1, shard * E),
                ((0, 0), (0, 0), (0, width - shard * E)),
            ),
            jnp.pad(
                low(gains_part).reshape(device_count, 1, 2 * shard),
                ((0, 0), (0, 14), (0, width - 2 * shard)),
            ),
        ],
        1,
    )
    parts = jnp.concatenate([by_device(grad_qkv_part), by_device(grad_out_part), spare_part], 1)
    (summed,) = scatter(SUM_OF_ALL, [parts.reshape(4, 2, 2, 4, 2, 8 * shard, width)], 5)
    qkv_grad = summed[: 4 * shard].reshape(4, shard, width)
    out_grad = summed[4 * shard : 6 * shard].reshape(2, shard, width)
    router_grad = summed[6 * shard, : shard * E].reshape(shard, E)
    gain_grad = summed[6 * shard + 1, : 2 * shard].reshape(2, shard)

    expert_grad = high(expert_grad).reshape(experts_here, 3, part, width)
    in_grad, down_grad = expert_grad[:, :2], expert_grad[:, 2]
    in_moment_new = MOMENTUM_DECAY * in_moment + in_grad
    down_moment_new = MOMENTUM_DECAY * down_moment + down_grad
    expert_count = experts_here * 3
    expert_stack = low(jnp.concatenate([in_moment_new, down_moment_new[:, None]], 1)).reshape(
        expert_count, part, width
    )
    expert_stack = jnp.pad(expert_stack, ((0, fsdp_count - expert_count), (0, 0), (0, 0)))
    expert_part = lax.all_to_all(expert_stack, "fsdp", split_axis=0, concat_axis=0, tiled=True)
    expert_solved = low(orthogonal(high(expert_part).reshape(MODEL_WIDTH, width)))
    expert_ortho = lax.all_to_all(
        expert_solved.reshape(fsdp_count, part, width),
        "fsdp",
        split_axis=0,
        concat_axis=0,
        tiled=True,
    )
    expert_ortho = high(expert_ortho[:expert_count]).reshape(experts_here, 3, part, width)
    in_new = (
        high(expert_in) * (1.0 - RATE_EXPERT * WEIGHT_DECAY) - RATE_EXPERT * expert_ortho[:, :2]
    )
    down_new = (
        high(expert_out) * (1.0 - RATE_DOWN * WEIGHT_DECAY) - RATE_DOWN * expert_ortho[:, 2]
    )

    qkv_moment_new = MOMENTUM_DECAY * query_key_value_momentum + qkv_grad
    out_moment_new = MOMENTUM_DECAY * output_momentum + out_grad
    attn_stack = low(jnp.concatenate([qkv_moment_new, out_moment_new], 0))
    attn_stack = jnp.pad(attn_stack, ((0, ctx_count - 6), (0, 0), (0, 0)))
    attn_rows = lax.all_to_all(attn_stack, "ctx", split_axis=0, concat_axis=0, tiled=True)
    attn_rows = attn_rows.reshape(1, ctx_count * shard, width)
    attn_rows = jnp.pad(attn_rows, ((0, fsdp_count - 1), (0, 0), (0, 0)))
    attn_rows = lax.all_to_all(attn_rows, "fsdp", split_axis=0, concat_axis=0, tiled=True)
    attn_solved = low(orthogonal(high(attn_rows).reshape(MODEL_WIDTH, width)))
    attn_back = lax.all_to_all(
        attn_solved.reshape(fsdp_count, ctx_count * shard, width),
        "fsdp",
        split_axis=0,
        concat_axis=0,
        tiled=True,
    )
    attn_ortho = lax.all_to_all(
        attn_back[0].reshape(ctx_count, shard, width),
        "ctx",
        split_axis=0,
        concat_axis=0,
        tiled=True,
    )
    attn_ortho = high(attn_ortho[:6])
    qkv_new = (
        high(query_key_value_weight) * (1.0 - RATE_INPUT * WEIGHT_DECAY)
        - RATE_INPUT * attn_ortho[:4]
    )
    out_new = (
        high(output_weight_matrix) * (1.0 - RATE_OUTPUT * WEIGHT_DECAY)
        - RATE_OUTPUT * attn_ortho[4:6]
    )

    gain_moment_new = AVERAGE_DECAY * gain_moment + (1.0 - AVERAGE_DECAY) * gain_grad
    router_moment_new = AVERAGE_DECAY * router_moment + (1.0 - AVERAGE_DECAY) * router_grad
    squares = jnp.concatenate(
        [
            jnp.sum(gain_moment_new * gain_moment_new, 1),
            jnp.sum(router_moment_new * router_moment_new)[None],
            jnp.zeros((125,), jnp.float32),
        ]
    )
    for axis, count in (("ctx", ctx_count), ("fsdp", fsdp_count)):
        copies = jnp.broadcast_to(squares[None], (count, 128))
        squares = jnp.sum(
            lax.all_to_all(copies, axis, split_axis=0, concat_axis=0, tiled=True), 0
        )
    gains_new = (
        high(norm_gains)
        - RATE_GAIN * gain_moment_new * lax.rsqrt(squares[:2] / MODEL_WIDTH + EPSILON)[:, None]
    )
    router_new = high(router_weights) - RATE_ROUTER * router_moment_new * lax.rsqrt(
        squares[2] / (MODEL_WIDTH * E) + EPSILON
    )
    hidden_out = low(
        residual + product("st,sd->td", own_picks, blend_returned.reshape(E * MOST, MODEL_WIDTH))
    )[None]
    return (
        hidden_out,
        input_grad,
        qkv_grad,
        out_grad,
        router_grad,
        gain_grad,
        in_grad,
        down_grad,
        qkv_moment_new,
        out_moment_new,
        router_moment_new,
        gain_moment_new,
        in_moment_new,
        down_moment_new,
        qkv_new,
        out_new,
        router_new,
        gains_new,
        in_new,
        down_new,
    )


def solution(mesh):
    placed = (
        P("fsdp", "ctx", None),
        P("fsdp", "ctx", None),
        P(),
        P("fsdp", "ctx", None),
        P(None, ("ctx", "fsdp"), None),
        P(None, ("ctx", "fsdp"), None),
        P(("ctx", "fsdp"), None),
        P(None, ("ctx", "fsdp")),
        P("ctx", None, "fsdp", None),
        P("ctx", "fsdp", None),
        P(None, ("ctx", "fsdp"), None),
        P(None, ("ctx", "fsdp"), None),
        P(("ctx", "fsdp"), None),
        P(None, ("ctx", "fsdp")),
        P("ctx", None, "fsdp", None),
        P("ctx", "fsdp", None),
    )
    return jax.shard_map(
        on_device,
        mesh=mesh,
        in_specs=placed,
        out_specs=(
            P("fsdp", "ctx", None),
            P("fsdp", "ctx", None),
            P(None, ("ctx", "fsdp"), None),
            P(None, ("ctx", "fsdp"), None),
            P(("ctx", "fsdp"), None),
            P(None, ("ctx", "fsdp")),
            P("ctx", None, "fsdp", None),
            P("ctx", "fsdp", None),
            P(None, ("ctx", "fsdp"), None),
            P(None, ("ctx", "fsdp"), None),
            P(("ctx", "fsdp"), None),
            P(None, ("ctx", "fsdp")),
            P("ctx", None, "fsdp", None),
            P("ctx", "fsdp", None),
            P(None, ("ctx", "fsdp"), None),
            P(None, ("ctx", "fsdp"), None),
            P(("ctx", "fsdp"), None),
            P(None, ("ctx", "fsdp")),
            P("ctx", None, "fsdp", None),
            P("ctx", "fsdp", None),
        ),
        check_vma=False,
    )
```

```python
import functools
import math

import jax
import jax.numpy as jnp
from jax import lax
from jax.experimental import pallas as pl
from jax.experimental.pallas import tpu as pltpu
from jax.sharding import PartitionSpec as P

MODEL_WIDTH = 1024
QUERY_HEADS = 16
KEY_VALUE_HEADS = 8
HEAD_WIDTH = 64
E = 32
TOP = 8
MOST = 40
SCHULZ_STEPS = 2


EPSILON = 1e-06
ROTARY_BASE = 10000.0
MOMENTUM_DECAY = 0.95
AVERAGE_DECAY = 0.9
SCHULZ_LINEAR = 3.4445
SCHULZ_SQUARE = -4.775
SCHULZ_CUBIC = 2.0315
WEIGHT_DECAY = 0.1
RATE_INPUT = 0.016
RATE_OUTPUT = 0.25
RATE_EXPERT = 0.031
RATE_DOWN = 0.031
RATE_GAIN = 0.5
RATE_ROUTER = 0.008
MASKED = -1e30

MESH = pl.DeviceIdType.MESH
RING = {"x": 4, "y": 4, "z": 4, "zh": 2, "zl": 2, "c": 2}
EVERY = ("y", "zh", "c", "x", "zl")
PAIRS = ("y", "zh", "c", "x")
ALONG_CTX = ("y", "zh", "c")
ALONG_FSDP = ("x", "zl")


def place():
    ctx = lax.axis_index("ctx")
    fsdp = lax.axis_index("fsdp")
    at = {"y": ctx // 4, "zh": (ctx // 2) % 2, "c": ctx % 2, "x": fsdp // 2, "zl": fsdp % 2}
    at["z"] = at["zh"] * 2 + at["zl"]
    return at


def moved(at, dim, to):
    at = dict(at)
    at[dim] = to
    if dim == "z":
        at["zh"], at["zl"] = to // 2, to % 2
    return at


def device_at(at):
    return ((at["y"] * 2 + at["zh"]) * 2 + at["c"], at["x"] * 2 + at["zl"])


def greet(peers):
    barrier = pltpu.get_barrier_semaphore()
    for peer in peers:
        pl.semaphore_signal(barrier, inc=1, device_id=peer, device_id_type=MESH)
    pl.semaphore_wait(barrier, len(peers))


def network_dims(jobs):
    found = []
    for dims, pieces in jobs:
        for piece in pieces:
            for dim in piece[-1]:
                if dim not in found:
                    found.append(dim)
    return found


def advance(live):
    while live:
        live = [f for f in live if next(f, "end") != "end"]


def gather_copies(jobs):
    total = 0
    for dims, pieces in jobs:
        for piece in pieces:
            shared = 0 if piece[-2] is None else 1
            total += shared
            for dim in piece[-1]:
                if dim != piece[-2]:
                    total += 1 + shared if RING[dim] == 2 else 4 + 3 * shared
    return total


def gather_kernel(jobs, paired, *refs):
    n = len(jobs)
    sources, targets = list(refs[:n]), refs[n : 2 * n]
    send_sems, recv_sems, local_sems = refs[2 * n : 2 * n + 3]
    me = place()
    dims_used = network_dims(jobs) + (["zl"] if paired else [])
    peers = []
    for dim in dims_used:
        size = RING[dim]
        for step in (1,) if size == 2 else (1, 3):
            peers.append(device_at(moved(me, dim, (me[dim] + step) % size)))

    def keep(j):
        dims = jobs[j][0]
        copy = pltpu.make_async_copy(
            sources[j],
            targets[j].at[(slice(None),) + tuple(me[d] for d in dims)],
            local_sems.at[j],
        )
        copy.start()
        return copy

    own = [] if paired else [keep(j) for j in range(n)]
    greet(peers)
    if paired:
        pair_sends, pair_recvs = refs[2 * n + 3 : 2 * n + 5]
        landings, joined = refs[2 * n + 5 : 3 * n + 5], refs[3 * n + 5 :]
        pairs = []
        for j in range(n):
            copy = pltpu.make_async_remote_copy(
                src_ref=sources[j],
                dst_ref=landings[j],
                send_sem=pair_sends.at[j],
                recv_sem=pair_recvs.at[j],
                device_id=device_at(moved(me, "zl", 1 - me["zl"])),
                device_id_type=MESH,
            )
            copy.start()
            pairs.append(copy)
        second = me["zl"] == 1
        for j, copy in enumerate(pairs):
            copy.wait()
            mine, other = sources[j][...], landings[j][...]
            joined[j][...] = jnp.concatenate(
                [jnp.where(second, other, mine), jnp.where(second, mine, other)], 1
            ).astype(joined[j].dtype)
            sources[j] = joined[j]
            own.append(keep(j))
    for copy in own:
        copy.wait()
    copies, shared = [], []

    def flow(j, dims, lead, leads, first, rows, share_to, order):
        target = targets[j]
        order = tuple(d for d in order if d != share_to)
        columns = target.shape[-1]

        def view(sel, half):
            place_in = (pl.ds(lead, leads),) + tuple(sel[d] for d in dims)
            if half is None:
                return target.at[place_in + (pl.ds(first, rows),)]
            if rows >= 32:
                return target.at[place_in + (pl.ds(first + half * (rows // 2), rows // 2),)]
            return target.at[
                place_in + (pl.ds(first, rows), pl.ds(half * (columns // 2), columns // 2))
            ]

        def send(sel, dim, to, half=None):
            k = len(copies)
            part = view(sel, half)
            copy = pltpu.make_async_remote_copy(
                src_ref=part,
                dst_ref=part,
                send_sem=send_sems.at[k],
                recv_sem=recv_sems.at[k],
                device_id=device_at(moved(me, dim, to)),
                device_id_type=MESH,
            )
            copy.start()
            copies.append(copy)
            return copy

        def share(sel):
            if share_to is not None:
                shared.append(send(sel, share_to, 1 - me[share_to]))

        def whole(sel, dim):
            if dim == "z":
                return dict(sel, zh=pl.ds(0, 2), zl=pl.ds(0, 2))
            return dict(sel, **{dim: pl.ds(0, RING[dim])})

        sel = dict(me)
        for at, dim in enumerate(order):
            if RING[dim] == 2:
                copy = send(sel, dim, 1 - me[dim])
                if at == 0:
                    share(sel)
                yield
                copy.wait_recv()
                share(moved(sel, dim, 1 - me[dim]))
            else:
                right, left = (me[dim] + 1) % 4, (me[dim] + 3) % 4
                up = send(sel, dim, right)
                down = send(sel, dim, left)
                if at == 0:
                    share(sel)
                yield
                up.wait_recv()
                on_up = send(moved(sel, dim, left), dim, right, 0)
                share(moved(sel, dim, left))
                down.wait_recv()
                on_down = send(moved(sel, dim, right), dim, left, 1)
                share(moved(sel, dim, right))
                yield
                on_up.wait_recv()
                on_down.wait_recv()
                share(moved(sel, dim, (me[dim] + 2) % 4))
            sel = whole(sel, dim)

    advance([flow(j, dims, *piece) for j, (dims, pieces) in enumerate(jobs) for piece in pieces])
    for copy in shared:
        copy.wait_recv()
    for copy in copies:
        copy.wait_send()


def gather(jobs, blocks, collective_id, paired=False):
    n = gather_copies(jobs)
    shapes = []
    for j, ((dims, _), b) in enumerate(zip(jobs, blocks)):
        lead, rows, columns = b.shape
        shapes.append(
            jax.ShapeDtypeStruct(
                (lead,) + tuple(RING[d] for d in dims) + (rows * 2 if paired else rows, columns),
                jnp.bfloat16 if paired else b.dtype,
            )
        )
    scratch = [
        pltpu.SemaphoreType.DMA((n,)),
        pltpu.SemaphoreType.DMA((n,)),
        pltpu.SemaphoreType.DMA((len(jobs),)),
    ]
    specs = [pl.BlockSpec(memory_space=pl.ANY)] * len(jobs)
    if paired:
        specs = [pl.BlockSpec(memory_space=pltpu.VMEM)] * len(jobs)
        scratch += [pltpu.SemaphoreType.DMA((len(jobs),))] * 2
        scratch += [pltpu.VMEM(b.shape, jnp.float32) for b in blocks]
        scratch += [
            pltpu.VMEM((b.shape[0], b.shape[1] * 2, b.shape[2]), jnp.bfloat16) for b in blocks
        ]
    return pl.pallas_call(
        functools.partial(gather_kernel, jobs, paired),
        out_shape=shapes,
        in_specs=specs,
        out_specs=[pl.BlockSpec(memory_space=pl.ANY)] * len(jobs),
        scratch_shapes=scratch,
        compiler_params=pltpu.CompilerParams(collective_id=collective_id, has_side_effects=True),
        cost_estimate=pl.CostEstimate(flops=0, bytes_accessed=60_000_000, transcendentals=0),
    )(*blocks)


def scatter_buffers(jobs, shapes):
    buffers, sems = [], 0
    for (dims, pieces), shape in zip(jobs, shapes):
        for _, leads, order in pieces:
            left = dims
            for dim in order:
                left = tuple(d for d in left if d != dim)
                block = (leads,) + tuple(RING[d] for d in left) + shape[-2:]
                buffers.append(pltpu.VMEM((RING[dim] - 1,) + block, jnp.bfloat16))
                if left:
                    buffers.append(pltpu.VMEM(block, jnp.bfloat16))
                sems += RING[dim] - 1
    return buffers, sems


def scatter_kernel(jobs, paired, *refs):
    n = len(jobs)
    sources, targets = refs[:n], list(refs[n : 2 * n])
    buffers = list(refs[2 * n :])
    if paired:
        targets, landings = buffers[:n], buffers[n : 2 * n]
        pair_sends, pair_recvs = buffers[2 * n : 2 * n + 2]
        buffers = buffers[2 * n + 2 :]
    send_sems, recv_sems = buffers[-2:]
    buffers = buffers[:-2]
    me = place()
    peers = []
    for dim in network_dims(jobs) + (["zl"] if paired else []):
        for step in range(1, RING[dim]):
            peers.append(device_at(moved(me, dim, (me[dim] + step) % RING[dim])))
    greet(peers)
    copies = []

    def flow(j, dims, lead, leads, order, held):
        current, left, base = sources[j], dims, lead
        for (landing, total), dim in zip(held, order):
            size = RING[dim]
            rest = tuple(d for d in left if d != dim)
            mine = []
            for step in range(1, size):
                to = (me[dim] + step) % size
                k = len(copies)
                index = tuple(to if d == dim else pl.ds(0, RING[d]) for d in left)
                copy = pltpu.make_async_remote_copy(
                    src_ref=current.at[(pl.ds(base, leads),) + index],
                    dst_ref=landing.at[step - 1],
                    send_sem=send_sems.at[k],
                    recv_sem=recv_sems.at[k],
                    device_id=device_at(moved(me, dim, to)),
                    device_id_type=MESH,
                )
                copy.start()
                copies.append(copy)
                mine.append(copy)
            yield
            for copy in mine:
                copy.wait_recv()
            to_base = 0 if rest else lead
            looped = rest[:1]
            trips = leads * math.prod(RING[d] for d in looped)

            def add(i, carry, current=current, landing=landing, total=total, left=left, base=base):
                at = i // RING[looped[0]] if looped else i
                inner = {looped[0]: i % RING[looped[0]]} if looped else {}
                inner[dim] = me[dim]
                index = tuple(inner.get(d, pl.ds(0, RING[d])) for d in left)
                value = current[(base + at,) + index].astype(jnp.float32)
                short = tuple(inner.get(d, pl.ds(0, RING[d])) for d in rest)
                for step in range(size - 1):
                    value += landing[(step, at) + short].astype(jnp.float32)
                total[(to_base + at,) + short] = value.astype(total.dtype)
                return carry

            lax.fori_loop(0, trips, add, 0)
            current, left, base = total, rest, 0

    live = []
    for j, (dims, pieces) in enumerate(jobs):
        for lead, leads, order in pieces:
            held, left = [], dims
            for dim in order:
                left = tuple(d for d in left if d != dim)
                landing = buffers.pop(0)
                held.append((landing, buffers.pop(0) if left else targets[j]))
            live.append(flow(j, dims, lead, leads, order, held))
    advance(live)
    for copy in copies:
        copy.wait_send()
    if paired:
        half = targets[0].shape[1] // 2
        theirs = pl.ds(pl.multiple_of((1 - me["zl"]) * half, half), half)
        ours = pl.ds(pl.multiple_of(me["zl"] * half, half), half)
        pairs = []
        for j in range(n):
            copy = pltpu.make_async_remote_copy(
                src_ref=targets[j].at[:, theirs],
                dst_ref=landings[j],
                send_sem=pair_sends.at[j],
                recv_sem=pair_recvs.at[j],
                device_id=device_at(moved(me, "zl", 1 - me["zl"])),
                device_id_type=MESH,
            )
            copy.start()
            pairs.append(copy)
        for j, copy in enumerate(pairs):
            copy.wait()
            refs[n + j][...] = targets[j][:, ours, :] + landings[j][...]


def scatter(jobs, blocks, collective_id, paired=False):
    buffers, n = scatter_buffers(jobs, [b.shape for b in blocks])
    scratch = buffers + [pltpu.SemaphoreType.DMA((n,)), pltpu.SemaphoreType.DMA((n,))]
    shapes = [(b.shape[0],) + b.shape[-2:] for b in blocks]
    if paired:
        whole, shapes = shapes, [(lead, rows // 2, columns) for lead, rows, columns in shapes]
        scratch = (
            [pltpu.VMEM(w, jnp.float32) for w in whole]
            + [pltpu.VMEM(h, jnp.float32) for h in shapes]
            + [pltpu.SemaphoreType.DMA((len(jobs),))] * 2
            + scratch
        )
    return pl.pallas_call(
        functools.partial(scatter_kernel, jobs, paired),
        out_shape=[jax.ShapeDtypeStruct(s, jnp.float32) for s in shapes],
        in_specs=[pl.BlockSpec(memory_space=pltpu.VMEM)] * len(jobs),
        out_specs=[pl.BlockSpec(memory_space=pltpu.VMEM)] * len(jobs),
        scratch_shapes=scratch,
        compiler_params=pltpu.CompilerParams(
            collective_id=collective_id, has_side_effects=True, vmem_limit_bytes=56 * 2**20
        ),
        cost_estimate=pl.CostEstimate(flops=0, bytes_accessed=60_000_000, transcendentals=0),
    )(*blocks)
CHUNK = 256


def transposed(left, right):
    return lax.dot_general(left, right, (((1,), (1,)), ((), ())), preferred_element_type=jnp.float32)


def on_rows(left, right):
    return lax.dot_general(left, right, (((0,), (0,)), ((), ())), preferred_element_type=jnp.float32)


def attend_kernel(query_ref, both_ref, key_at_ref, query_at_ref, mixed_ref, log_ref, score_ref):
    query = query_ref[0]
    query_at = query_at_ref[...]
    keys = both_ref.shape[1]
    peak = jnp.full((1, query.shape[0]), MASKED, jnp.float32)
    for start in range(0, keys, CHUNK):
        span = pl.ds(start, CHUNK)
        scores = transposed(both_ref[0, span], query)
        scores = jnp.where(key_at_ref[span] <= query_at, scores, MASKED)
        score_ref[span] = scores
        peak = jnp.maximum(peak, jnp.max(scores, 0, keepdims=True))
    total = jnp.zeros_like(peak)
    mixed = jnp.zeros((both_ref.shape[2], query.shape[0]), jnp.float32)
    for start in range(0, keys, CHUNK):
        span = pl.ds(start, CHUNK)
        weights = jnp.exp(score_ref[span] - peak)
        total += jnp.sum(weights, 0, keepdims=True)
        mixed += on_rows(both_ref[0, span], weights.astype(jnp.bfloat16))
    mixed_ref[0] = (mixed[HEAD_WIDTH:] / total).astype(mixed_ref.dtype)
    log_ref[0] = peak + jnp.log(total)


def attend_back_kernel(
    query_ref,
    both_ref,
    key_at_ref,
    query_at_ref,
    log_ref,
    upstream_ref,
    query_grad_ref,
    both_grad_ref,
    chance_ref,
    change_ref,
):
    query, upstream = query_ref[0], upstream_ref[0]
    query_at, log_total = query_at_ref[...], log_ref[0]
    keys = both_ref.shape[1]
    inner = jnp.zeros((1, query.shape[0]), jnp.float32)
    for start in range(0, keys, CHUNK):
        span = pl.ds(start, CHUNK)
        both = both_ref[0, span]
        scores = jnp.where(key_at_ref[span] <= query_at, transposed(both, query), MASKED)
        chance = jnp.exp(scores - log_total)
        change = transposed(both, upstream)
        chance_ref[span] = chance
        change_ref[span] = change
        inner += jnp.sum(chance * change, 0, keepdims=True)
    query_grad = jnp.zeros((both_ref.shape[2], query.shape[0]), jnp.float32)
    for start in range(0, keys, CHUNK):
        span = pl.ds(start, CHUNK)
        chance = chance_ref[span]
        grad_scores = (chance * (change_ref[span] - inner)).astype(jnp.bfloat16)
        both_grad_ref[0, span] = (
            jnp.dot(grad_scores, query, preferred_element_type=jnp.float32)
            + jnp.dot(
                chance.astype(jnp.bfloat16), upstream, preferred_element_type=jnp.float32
            )
        ).astype(both_grad_ref.dtype)
        query_grad += on_rows(both_ref[0, span], grad_scores)
    query_grad_ref[0] = query_grad[:HEAD_WIDTH]


def by_head(*block):
    return pl.BlockSpec((1,) + block, lambda g: (g, 0, 0))


def for_all(*block):
    return pl.BlockSpec(block, lambda g: (0, 0))


def attend(query, both, key_at, query_at):
    heads, queries, columns = query.shape
    keys = both.shape[1]
    return pl.pallas_call(
        attend_kernel,
        grid=(heads,),
        out_shape=[
            jax.ShapeDtypeStruct((heads, HEAD_WIDTH, queries), jnp.bfloat16),
            jax.ShapeDtypeStruct((heads, 1, queries), jnp.float32),
        ],
        in_specs=[
            by_head(queries, columns),
            by_head(keys, columns),
            for_all(keys, 1),
            for_all(1, queries),
        ],
        out_specs=[by_head(HEAD_WIDTH, queries), by_head(1, queries)],
        scratch_shapes=[pltpu.VMEM((keys, queries), jnp.float32)],
        compiler_params=pltpu.CompilerParams(vmem_limit_bytes=40 * 2**20),
        cost_estimate=pl.CostEstimate(
            flops=4 * heads * queries * keys * columns,
            bytes_accessed=6_000_000,
            transcendentals=heads * queries * keys,
        ),
    )(query, both, key_at, query_at)


def attend_back(query, both, key_at, query_at, log_total, upstream):
    heads, queries, columns = query.shape
    keys = both.shape[1]
    return pl.pallas_call(
        attend_back_kernel,
        grid=(heads,),
        out_shape=[
            jax.ShapeDtypeStruct((heads, HEAD_WIDTH, queries), jnp.float32),
            jax.ShapeDtypeStruct((heads, keys, columns), jnp.bfloat16),
        ],
        in_specs=[
            by_head(queries, columns),
            by_head(keys, columns),
            for_all(keys, 1),
            for_all(1, queries),
            by_head(1, queries),
            by_head(queries, columns),
        ],
        out_specs=[by_head(HEAD_WIDTH, queries), by_head(keys, columns)],
        scratch_shapes=[pltpu.VMEM((keys, queries), jnp.float32)] * 2,
        compiler_params=pltpu.CompilerParams(vmem_limit_bytes=40 * 2**20),
        cost_estimate=pl.CostEstimate(
            flops=10 * heads * queries * keys * columns,
            bytes_accessed=12_000_000,
            transcendentals=heads * queries * keys,
        ),
    )(query, both, key_at, query_at, log_total, upstream)


def apply_rotation(tensor, cosine_values, sine_lookup):
    half_size = tensor.shape[-1] // 2
    leading = tensor[..., :half_size]
    trailing = tensor[..., half_size:]
    table_shape = (tensor.shape[0],) + (1,) * (tensor.ndim - 2) + (half_size,)
    cosine_values = cosine_values.reshape(table_shape)
    sine_lookup = sine_lookup.reshape(table_shape)
    return jnp.concatenate(
        [
            leading * cosine_values - trailing * sine_lookup,
            trailing * cosine_values + leading * sine_lookup,
        ],
        -1,
    )


def low(value):
    return value.astype(jnp.bfloat16)


def high(value):
    return value.astype(jnp.float32)


def product(spec, left, right):
    return jnp.einsum(spec, low(left), low(right), preferred_element_type=jnp.float32)


def orthogonal(matrix, rows):
    gram = product("dw,dv->wv", matrix, matrix)
    norm = jnp.sqrt(jnp.sum(jnp.square(high(matrix)))) + 1e-07
    gram = gram / (norm * norm)
    scaled = high(rows) / norm
    for sweep_index in range(SCHULZ_STEPS):
        polynomial = SCHULZ_SQUARE * gram + SCHULZ_CUBIC * product("wv,vu->wu", gram, gram)
        scaled = SCHULZ_LINEAR * scaled + product("dw,wv->dv", scaled, polynomial)
        if sweep_index < SCHULZ_STEPS - 1:
            gram = SCHULZ_LINEAR * gram + product("wv,vu->wu", gram, polynomial)
            gram = SCHULZ_LINEAR * gram + product("wv,vu->wu", polynomial, gram)
    return scaled * math.sqrt(max(matrix.shape))


def norm_backward(values_in, inverse, gain_row, grad_normed):
    weighted = gain_row * grad_normed
    grad_values = inverse * weighted - values_in * inverse**3 * jnp.mean(
        weighted * values_in, -1, keepdims=True
    )
    grad_gain = jnp.sum(grad_normed * values_in * inverse, 0)
    return (grad_values, grad_gain)


def two_halves(value):
    upper = low(value)
    return upper, low(value - high(upper))


def slots_of(chosen):
    rows = chosen.shape[1]
    before = jnp.tril(jnp.ones((rows, rows), jnp.bfloat16), -1)
    rank = jnp.einsum("st,bte->bes", before, low(chosen), preferred_element_type=jnp.float32)
    taken = jnp.swapaxes(chosen, 1, 2)
    slot = jnp.arange(MOST, dtype=jnp.int32)[None, None, :, None]
    filled = (rank.astype(jnp.int32)[:, :, None, :] == slot) & (taken[:, :, None, :] > 0.5)
    return filled


ONE_WAY, OTHER_WAY = ("zh", "x", "y", "c"), ("zh", "y", "x", "c")
ATTENTION_WEIGHTS = (
    (PAIRS, ((0, 2, 0, 16, "c", ONE_WAY), (2, 2, 0, 16, "c", OTHER_WAY))),
    (PAIRS, ((0, 1, 0, 16, "c", ONE_WAY), (1, 1, 0, 16, "c", OTHER_WAY))),
    (PAIRS, ((0, 1, 0, 16, "c", ONE_WAY),)),
)


def over_fsdp(leads):
    return tuple(
        (i, 1, 0, 128) + ((None, ("zl", "x")) if i % 2 == 0 else ("zl", ("x", "zl")))
        for i in range(leads)
    )


KEYS_VALUES_EXPERTS = (
    (ALONG_CTX, tuple((i, 4, 0, 128, "c", ("zh", "y", "c")) for i in (0, 4))),
    (ALONG_FSDP, over_fsdp(4)),
    (ALONG_FSDP, over_fsdp(2)),
)
TOKEN_ROWS = ((ALONG_CTX, tuple((0, 1, i, 64, "c", ("zh", "y", "c")) for i in (0, 64))),)
ATTENTION_MOMENTA = ((ALONG_FSDP, ((0, 1, 0, 128, None, ("zl", "x")), (0, 1, 128, 16, None, ("zl", "x")))),)
SUM_ONE_WAY, SUM_OTHER_WAY = ("c", "x", "y", "zh"), ("c", "y", "x", "zh")
KEY_VALUE_SUMS = (
    (ALONG_CTX, ((0, 4, ("c", "y", "zh")), (4, 4, ("c", "y", "zh")))),
    (ALONG_FSDP, tuple((i, 1, ("x", "zl") if i % 2 == 0 else ("zl", "x")) for i in range(4))),
    (ALONG_FSDP, tuple((i, 1, ("x", "zl") if i % 2 == 0 else ("zl", "x")) for i in range(2))),
)
ATTENTION_SUMS = tuple(
    (PAIRS, ((0, 1, SUM_ONE_WAY if i % 2 == 0 else SUM_OTHER_WAY),)) for i in range(7)
)


def on_device(
    hidden_in,
    cotangent,
    block_deal,
    routes,
    query_key_value_weight,
    output_weight_matrix,
    router_weights,
    norm_gains,
    expert_in,
    expert_out,
    query_key_value_momentum,
    output_momentum,
    router_moment,
    gain_moment,
    in_moment,
    down_moment,
):
    ctx_count = lax.axis_size("ctx")
    fsdp_count = lax.axis_size("fsdp")
    device_count = ctx_count * fsdp_count
    ctx_index = lax.axis_index("ctx")
    rows = hidden_in.shape[1]
    sequence_length = rows * ctx_count
    half_rows = rows // 2
    shard = query_key_value_weight.shape[1]
    width = query_key_value_weight.shape[2]
    group_width = QUERY_HEADS // KEY_VALUE_HEADS
    score_scale = 1.0 / math.sqrt(HEAD_WIDTH)

    steps = jnp.arange(half_rows, dtype=jnp.int32)[None, :]
    token_positions = (block_deal[:, None] * half_rows + steps).reshape(sequence_length)
    local_deal = lax.dynamic_slice_in_dim(block_deal, ctx_index * 2, 2)
    local_pos = (local_deal[:, None] * half_rows + steps).reshape(rows)
    half_size = HEAD_WIDTH // 2
    powers = jnp.arange(half_size).astype(jnp.float32) * (2.0 / HEAD_WIDTH)
    frequency = jnp.exp(-math.log(ROTARY_BASE) * powers)
    angles = local_pos.astype(jnp.float32)[:, None] * frequency[None, :]
    cosine_values, sine_lookup = jnp.cos(angles), jnp.sin(angles)
    key_at = token_positions[:, None]
    query_at = jnp.tile(local_pos, group_width)[None, :]

    spare = jnp.concatenate(
        [
            jnp.pad(router_weights.reshape(1, -1), ((0, 0), (0, width - shard * E))),
            jnp.pad(norm_gains.reshape(1, -1), ((0, shard - 2), (0, width - 2 * shard))),
        ],
        0,
    )
    qkv_full, out_full, spare_full = gather(
        ATTENTION_WEIGHTS,
        [high(query_key_value_weight), high(output_weight_matrix), high(spare)[None]],
        1,
        paired=True,
    )
    qkv_full = qkv_full.reshape(4, MODEL_WIDTH, width)
    out_full = out_full.reshape(2, MODEL_WIDTH, width)
    spare_full = spare_full.reshape(device_count, shard, width)
    router_full = spare_full[:, 0, : shard * E].reshape(MODEL_WIDTH, E)
    gains_full = (
        spare_full[:, 1, : 2 * shard]
        .reshape(device_count, 2, shard)
        .transpose(1, 0, 2)
        .reshape(2, MODEL_WIDTH)
    )

    part = expert_in.shape[2]
    experts_here = expert_in.shape[0]
    cotangent_all = lax.all_gather(cotangent[0], "ctx", axis=0)

    tokens = high(hidden_in[0])
    inverse_first = lax.rsqrt(jnp.mean(tokens * tokens, -1, keepdims=True) + EPSILON)
    gain_first = high(gains_full[0])
    normed = low(tokens * inverse_first * gain_first)
    split_heads = [
        product("td,dw->tw", normed, qkv_full[j]).reshape(rows, KEY_VALUE_HEADS, HEAD_WIDTH)
        for j in range(4)
    ]
    keys_local = low(apply_rotation(split_heads[2], cosine_values, sine_lookup))
    values_local = low(split_heads[3])
    keys_values, gateup_full, down_full = gather(
        KEYS_VALUES_EXPERTS,
        [
            jnp.concatenate([keys_local, values_local], -1).transpose(1, 0, 2),
            expert_in.reshape(2 * experts_here, part, width),
            expert_out,
        ],
        2,
    )
    gateup_full = gateup_full.reshape(experts_here, 2, MODEL_WIDTH, width)
    down_full = down_full.reshape(experts_here, MODEL_WIDTH, width)
    query_matrix = low(
        apply_rotation(jnp.stack(split_heads[:2], 1), cosine_values, sine_lookup)
    )
    keys_values = keys_values.reshape(KEY_VALUE_HEADS, sequence_length, 2 * HEAD_WIDTH)

    def heads_first(values, before, after):
        values = values.reshape(rows, KEY_VALUE_HEADS, group_width, HEAD_WIDTH)
        values = values.transpose(1, 2, 0, 3).reshape(KEY_VALUE_HEADS, group_width * rows, HEAD_WIDTH)
        return jnp.pad(values, ((0, 0), (0, 0), (before, after)))

    def rows_first(values):
        values = values.reshape(KEY_VALUE_HEADS, HEAD_WIDTH, group_width, rows)
        return values.transpose(3, 0, 2, 1).reshape(rows, 2, width)

    queries = heads_first(query_matrix * score_scale, 0, HEAD_WIDTH)
    mixture, log_total = attend(queries, keys_values, key_at, query_at)
    mixture_rows = rows_first(mixture)
    residual = tokens + sum(
        product("tw,dw->td", mixture_rows[:, j], out_full[j]) for j in range(2)
    )
    inverse_second = lax.rsqrt(jnp.mean(residual * residual, -1, keepdims=True) + EPSILON)
    gain_second = high(gains_full[1])
    normed_second = low(residual * inverse_second * gain_second)
    logits = product("td,de->te", normed_second, router_full)
    routed = routes[0]
    chosen = jnp.sum(
        high(routed[:, :, None] == jnp.arange(E, dtype=jnp.int32)[None, None, :]), 1
    )
    peak = jnp.max(jnp.where(chosen > 0.5, logits, MASKED), -1, keepdims=True)
    weighed = jnp.where(chosen > 0.5, jnp.exp(jnp.minimum(logits - peak, 0.0)), 0.0)
    gates = weighed / jnp.sum(weighed, -1, keepdims=True)
    upstream = high(cotangent[0])

    gate_upper, gate_lower = two_halves(gates)
    (sent,) = gather(
        TOKEN_ROWS,
        [
            jnp.concatenate(
                [normed_second, gate_upper, gate_lower, low(chosen), jnp.zeros_like(gate_upper)], 1
            )[None]
        ],
        3,
    )
    sent = sent.reshape(ctx_count, rows, MODEL_WIDTH + 4 * E)

    def mine(start):
        return lax.dynamic_slice_in_dim(
            sent, MODEL_WIDTH + start + ctx_index * experts_here, experts_here, 2
        )

    gates_mine = high(mine(0)) + high(mine(E))
    filled = slots_of(high(mine(2 * E)))
    picks = low(filled)
    capacity = ctx_count * MOST
    row_gates = jnp.sum(
        jnp.where(filled, jnp.swapaxes(gates_mine, 1, 2)[:, :, None, :], 0.0), -1
    ).transpose(1, 0, 2).reshape(experts_here, capacity, 1)

    def select(values):
        found = low(product("bert,btd->ebrd", picks, values))
        return found.reshape(experts_here, capacity, MODEL_WIDTH)

    expert_rows = select(sent[:, :, :MODEL_WIDTH])
    upstream_rows = high(select(cotangent_all))
    gate_up = product("erd,ejdf->ejrf", expert_rows, gateup_full)
    upper_pre, lower_pre = gate_up[:, 0], gate_up[:, 1]
    sigmoid_up = jax.nn.sigmoid(upper_pre)
    hidden = low(upper_pre * sigmoid_up * lower_pre)
    outputs = high(low(product("erf,edf->erd", hidden, down_full)))
    row_grads = low(row_gates * upstream_rows)
    row_dgate = jnp.sum(upstream_rows * outputs, -1)
    grad_hidden = product("erd,edf->erf", row_grads, down_full)
    grad_upper = grad_hidden * lower_pre * sigmoid_up * (1.0 + upper_pre * (1.0 - sigmoid_up))
    grad_lower = grad_hidden * (upper_pre * sigmoid_up)
    grad_both = low(jnp.stack([grad_upper, grad_lower], 1))
    back_rows = low(product("ejrf,ejdf->erd", grad_both, gateup_full))

    def by_block(values):
        values = values.reshape(experts_here, ctx_count, MOST, values.shape[-1])
        return values.transpose(1, 0, 2, 3).reshape(ctx_count, experts_here * MOST, -1)

    dgate_upper, dgate_lower = two_halves(by_block(row_dgate[:, :, None])[:, :, 0])
    dgate_rows = jnp.stack([dgate_upper, dgate_lower], 1)
    dgate_rows = jnp.pad(
        dgate_rows, ((0, 0), (0, 6), (0, MODEL_WIDTH - experts_here * MOST))
    )
    back_sent = jnp.concatenate([by_block(back_rows), dgate_rows], 1)
    back_returned = lax.all_to_all(back_sent, "ctx", split_axis=0, concat_axis=0, tiled=True)
    blend_sent = by_block(low(row_gates * outputs))
    blend_sent, back_returned = lax.optimization_barrier((blend_sent, back_returned))
    blend_returned = lax.all_to_all(blend_sent, "ctx", split_axis=0, concat_axis=0, tiled=True)

    grad_gateup = low(product("erd,ejrf->ejdf", expert_rows, grad_both))
    grad_down = low(product("erd,erf->edf", row_grads, hidden))

    own_filled = slots_of(chosen[None])[0]
    own_picks = low(own_filled).reshape(E * MOST, rows)
    back_values = back_returned[:, : experts_here * MOST].reshape(E * MOST, MODEL_WIDTH)
    back_sum = product("st,sd->td", own_picks, back_values)
    own_dgate = high(back_returned[:, experts_here * MOST, : experts_here * MOST]) + high(
        back_returned[:, experts_here * MOST + 1, : experts_here * MOST]
    )
    grad_gates = jnp.sum(
        jnp.where(own_filled, own_dgate.reshape(E, MOST, 1), 0.0), 1
    ).T
    grad_logits = low(gates * (grad_gates - jnp.sum(gates * grad_gates, -1, keepdims=True)))
    grad_router_part = product("td,te->de", normed_second, grad_logits)
    grad_normed_second = back_sum + product("te,de->td", grad_logits, router_full)
    grad_residual_norm, grad_gain_second = norm_backward(
        residual, inverse_second, gain_second, grad_normed_second
    )
    grad_residual = upstream + grad_residual_norm
    grad_attention = low(grad_residual)
    grad_out_parts = [product("td,tw->dw", grad_attention, mixture_rows[:, j]) for j in range(2)]
    mixture_gradient = low(
        jnp.stack([product("td,dw->tw", grad_attention, out_full[j]) for j in range(2)], 1)
    )
    query_gradient, grad_keys_values = attend_back(
        queries,
        keys_values,
        key_at,
        query_at,
        log_total,
        heads_first(mixture_gradient, HEAD_WIDTH, 0),
    )
    query_gradient = rows_first(query_gradient * score_scale)
    grad_keys_values, blend_returned = lax.optimization_barrier((grad_keys_values, blend_returned))
    local_gradient, in_grad, down_grad = scatter(
        KEY_VALUE_SUMS,
        [
            grad_keys_values.reshape(KEY_VALUE_HEADS, 4, 2, 2, rows, 2 * HEAD_WIDTH),
            grad_gateup.reshape(2 * experts_here, 4, 2, part, width),
            grad_down.reshape(experts_here, 4, 2, part, width),
        ],
        4,
    )
    local_gradient = local_gradient.transpose(1, 0, 2)
    in_grad = in_grad.reshape(experts_here, 2, part, width)
    in_moment_new = MOMENTUM_DECAY * in_moment + in_grad
    down_moment_new = MOMENTUM_DECAY * down_moment + down_grad
    expert_count = experts_here * 3
    expert_stack = low(jnp.concatenate([in_moment_new, down_moment_new[:, None]], 1)).reshape(
        expert_count, part, width
    )
    expert_stack = jnp.pad(expert_stack, ((0, fsdp_count - expert_count), (0, 0), (0, 0)))
    expert_part = lax.all_to_all(expert_stack, "fsdp", split_axis=0, concat_axis=0, tiled=True)
    query_row_gradient = apply_rotation(
        query_gradient.reshape(rows, 2, KEY_VALUE_HEADS, HEAD_WIDTH), cosine_values, -sine_lookup
    )
    key_row_gradient = apply_rotation(
        local_gradient[..., :HEAD_WIDTH],
        cosine_values,
        -sine_lookup,
    )
    grad_project = low(
        jnp.concatenate(
            [
                query_row_gradient.reshape(rows, 2, width),
                key_row_gradient.reshape(rows, 1, width),
                local_gradient[..., HEAD_WIDTH:].reshape(rows, 1, width),
            ],
            1,
        )
    )
    grad_qkv_parts = [product("td,tw->dw", normed, grad_project[:, j]) for j in range(4)]
    grad_normed_first = sum(
        product("tw,dw->td", grad_project[:, j], qkv_full[j]) for j in range(4)
    )
    grad_tokens_norm, grad_gain_first = norm_backward(
        tokens, inverse_first, gain_first, grad_normed_first
    )
    input_grad = (grad_residual + grad_tokens_norm)[None]

    gains_part = jnp.stack([grad_gain_first, grad_gain_second], 0)
    gains_part = gains_part.reshape(2, device_count, shard).transpose(1, 0, 2)
    spare_part = jnp.concatenate(
        [
            jnp.pad(
                low(grad_router_part).reshape(device_count, 1, shard * E),
                ((0, 0), (0, 0), (0, width - shard * E)),
            ),
            jnp.pad(
                low(gains_part).reshape(device_count, 1, 2 * shard),
                ((0, 0), (0, shard - 2), (0, width - 2 * shard)),
            ),
        ],
        1,
    )
    parts = [
        low(part).reshape(1, 4, 2, 2, 4, 2 * shard, width)
        for part in grad_qkv_parts + grad_out_parts + [spare_part]
    ]
    parts[0], expert_part = lax.optimization_barrier((parts[0], expert_part))
    summed = scatter(ATTENTION_SUMS, parts, 5, paired=True)
    qkv_grad, out_grad = jnp.concatenate(summed[:4], 0), jnp.concatenate(summed[4:6], 0)
    router_grad = summed[6][0, 0, : shard * E].reshape(shard, E)
    gain_grad = summed[6][0, 1, : 2 * shard].reshape(2, shard)
    qkv_moment_new = MOMENTUM_DECAY * query_key_value_momentum + qkv_grad
    out_moment_new = MOMENTUM_DECAY * output_momentum + out_grad
    gain_moment_new = AVERAGE_DECAY * gain_moment + (1.0 - AVERAGE_DECAY) * gain_grad
    router_moment_new = AVERAGE_DECAY * router_moment + (1.0 - AVERAGE_DECAY) * router_grad
    squares = jnp.concatenate(
        [
            jnp.sum(gain_moment_new * gain_moment_new, 1),
            jnp.sum(router_moment_new * router_moment_new)[None],
        ]
    )

    def squares_rows(count):
        upper = low(squares)
        row = jnp.concatenate([upper, low(squares - high(upper))])
        return jnp.pad(row[None], ((0, count - 1), (0, width - 6)))

    def squares_total(row):
        row = jnp.sum(high(row), 0)
        return row[:3] + row[3:6]

    attn_stack = low(jnp.concatenate([qkv_moment_new, out_moment_new], 0))
    attn_stack = jnp.pad(attn_stack, ((0, ctx_count - 6), (0, 0), (0, 0)))
    attn_stack = jnp.concatenate(
        [attn_stack, jnp.broadcast_to(squares_rows(shard)[None], attn_stack.shape)], 1
    )
    attn_rows = lax.all_to_all(attn_stack, "ctx", split_axis=0, concat_axis=0, tiled=True)
    squares = squares_total(attn_rows[:, shard, :6])
    attn_rows = attn_rows[:, :shard].reshape(ctx_count * shard, width)
    expert_part = expert_part.reshape(MODEL_WIDTH, width)
    expert_solved = low(orthogonal(expert_part, expert_part))
    attn_rows, expert_solved = lax.optimization_barrier((attn_rows, expert_solved))
    expert_ortho = lax.all_to_all(
        expert_solved.reshape(fsdp_count, part, width),
        "fsdp",
        split_axis=0,
        concat_axis=0,
        tiled=True,
    )
    (attn_full,) = gather(
        ATTENTION_MOMENTA, [jnp.concatenate([attn_rows, squares_rows(2 * shard)], 0)[None]], 6
    )
    attn_full, expert_ortho = lax.optimization_barrier((attn_full, expert_ortho))
    attn_full = attn_full.reshape(fsdp_count, (ctx_count + 2) * shard, width)
    squares = squares_total(attn_full[:, ctx_count * shard, :6])
    attn_full = attn_full[:, : ctx_count * shard].reshape(MODEL_WIDTH, width)
    attn_solved = low(orthogonal(attn_full, attn_rows))
    attn_ortho = lax.all_to_all(
        attn_solved.reshape(ctx_count, shard, width),
        "ctx",
        split_axis=0,
        concat_axis=0,
        tiled=True,
    )
    attn_ortho = high(attn_ortho[:6])
    expert_ortho = high(expert_ortho[:expert_count]).reshape(experts_here, 3, part, width)
    in_new = (
        high(expert_in) * (1.0 - RATE_EXPERT * WEIGHT_DECAY) - RATE_EXPERT * expert_ortho[:, :2]
    )
    down_new = (
        high(expert_out) * (1.0 - RATE_DOWN * WEIGHT_DECAY) - RATE_DOWN * expert_ortho[:, 2]
    )
    qkv_new = (
        high(query_key_value_weight) * (1.0 - RATE_INPUT * WEIGHT_DECAY)
        - RATE_INPUT * attn_ortho[:4]
    )
    out_new = (
        high(output_weight_matrix) * (1.0 - RATE_OUTPUT * WEIGHT_DECAY)
        - RATE_OUTPUT * attn_ortho[4:6]
    )

    gains_new = (
        high(norm_gains)
        - RATE_GAIN * gain_moment_new * lax.rsqrt(squares[:2] / MODEL_WIDTH + EPSILON)[:, None]
    )
    router_new = high(router_weights) - RATE_ROUTER * router_moment_new * lax.rsqrt(
        squares[2] / (MODEL_WIDTH * E) + EPSILON
    )
    hidden_out = low(
        residual + product("st,sd->td", own_picks, blend_returned.reshape(E * MOST, MODEL_WIDTH))
    )[None]
    return (
        hidden_out,
        input_grad,
        qkv_grad,
        out_grad,
        router_grad,
        gain_grad,
        in_grad,
        down_grad,
        qkv_moment_new,
        out_moment_new,
        router_moment_new,
        gain_moment_new,
        in_moment_new,
        down_moment_new,
        qkv_new,
        out_new,
        router_new,
        gains_new,
        in_new,
        down_new,
    )


def solution(mesh):
    placed = (
        P("fsdp", "ctx", None),
        P("fsdp", "ctx", None),
        P(),
        P("fsdp", "ctx", None),
        P(None, ("ctx", "fsdp"), None),
        P(None, ("ctx", "fsdp"), None),
        P(("ctx", "fsdp"), None),
        P(None, ("ctx", "fsdp")),
        P("ctx", None, "fsdp", None),
        P("ctx", "fsdp", None),
        P(None, ("ctx", "fsdp"), None),
        P(None, ("ctx", "fsdp"), None),
        P(("ctx", "fsdp"), None),
        P(None, ("ctx", "fsdp")),
        P("ctx", None, "fsdp", None),
        P("ctx", "fsdp", None),
    )
    return jax.shard_map(
        on_device,
        mesh=mesh,
        in_specs=placed,
        out_specs=(
            P("fsdp", "ctx", None),
            P("fsdp", "ctx", None),
            P(None, ("ctx", "fsdp"), None),
            P(None, ("ctx", "fsdp"), None),
            P(("ctx", "fsdp"), None),
            P(None, ("ctx", "fsdp")),
            P("ctx", None, "fsdp", None),
            P("ctx", "fsdp", None),
            P(None, ("ctx", "fsdp"), None),
            P(None, ("ctx", "fsdp"), None),
            P(("ctx", "fsdp"), None),
            P(None, ("ctx", "fsdp")),
            P("ctx", None, "fsdp", None),
            P("ctx", "fsdp", None),
            P(None, ("ctx", "fsdp"), None),
            P(None, ("ctx", "fsdp"), None),
            P(("ctx", "fsdp"), None),
            P(None, ("ctx", "fsdp")),
            P("ctx", None, "fsdp", None),
            P("ctx", "fsdp", None),
        ),
        check_vma=False,
    )
```

```python
import functools
import math

import jax
import jax.numpy as jnp
from jax import lax
from jax.experimental import pallas as pl
from jax.experimental.pallas import tpu as pltpu
from jax.sharding import PartitionSpec as P

MODEL_WIDTH = 1024
QUERY_HEADS = 16
KEY_VALUE_HEADS = 8
HEAD_WIDTH = 64
E = 32
TOP = 8
MOST = 40
SCHULZ_STEPS = 2


EPSILON = 1e-06
ROTARY_BASE = 10000.0
MOMENTUM_DECAY = 0.95
AVERAGE_DECAY = 0.9
SCHULZ_LINEAR = 3.4445
SCHULZ_SQUARE = -4.775
SCHULZ_CUBIC = 2.0315
WEIGHT_DECAY = 0.1
RATE_INPUT = 0.016
RATE_OUTPUT = 0.25
RATE_EXPERT = 0.031
RATE_DOWN = 0.031
RATE_GAIN = 0.5
RATE_ROUTER = 0.008
MASKED = -1e30

MESH = pl.DeviceIdType.MESH
RING = {"x": 4, "y": 4, "z": 4, "zh": 2, "zl": 2, "c": 2}
EVERY = ("y", "zh", "c", "x", "zl")
PAIRS = ("y", "zh", "c", "x")
ALONG_CTX = ("y", "zh", "c")
ALONG_FSDP = ("x", "zl")


def place():
    ctx = lax.axis_index("ctx")
    fsdp = lax.axis_index("fsdp")
    at = {"y": ctx // 4, "zh": (ctx // 2) % 2, "c": ctx % 2, "x": fsdp // 2, "zl": fsdp % 2}
    at["z"] = at["zh"] * 2 + at["zl"]
    return at


def moved(at, dim, to):
    at = dict(at)
    at[dim] = to
    if dim == "z":
        at["zh"], at["zl"] = to // 2, to % 2
    return at


def device_at(at):
    return ((at["y"] * 2 + at["zh"]) * 2 + at["c"], at["x"] * 2 + at["zl"])


def greet(peers):
    barrier = pltpu.get_barrier_semaphore()
    for peer in peers:
        pl.semaphore_signal(barrier, inc=1, device_id=peer, device_id_type=MESH)
    pl.semaphore_wait(barrier, len(peers))


def network_dims(jobs):
    found = []
    for dims, pieces in jobs:
        for piece in pieces:
            for dim in piece[-1]:
                if dim not in found:
                    found.append(dim)
    return found


def advance(live):
    while live:
        live = [f for f in live if next(f, "end") != "end"]


def gather_copies(jobs):
    total = 0
    for dims, pieces in jobs:
        for piece in pieces:
            shared = 0 if piece[-2] is None else 1
            total += shared
            for dim in piece[-1]:
                if dim != piece[-2]:
                    total += 1 + shared if RING[dim] == 2 else 4 + 3 * shared
    return total


def gather_kernel(jobs, paired, *refs):
    n = len(jobs)
    sources, targets = list(refs[:n]), refs[n : 2 * n]
    send_sems, recv_sems, local_sems = refs[2 * n : 2 * n + 3]
    me = place()
    dims_used = network_dims(jobs) + (["zl"] if paired else [])
    peers = []
    for dim in dims_used:
        size = RING[dim]
        for step in (1,) if size == 2 else (1, 3):
            peers.append(device_at(moved(me, dim, (me[dim] + step) % size)))

    def keep(j):
        dims = jobs[j][0]
        copy = pltpu.make_async_copy(
            sources[j],
            targets[j].at[(slice(None),) + tuple(me[d] for d in dims)],
            local_sems.at[j],
        )
        copy.start()
        return copy

    own = [] if paired else [keep(j) for j in range(n)]
    greet(peers)
    if paired:
        pair_sends, pair_recvs = refs[2 * n + 3 : 2 * n + 5]
        landings, joined = refs[2 * n + 5 : 3 * n + 5], refs[3 * n + 5 :]
        pairs = []
        for j in range(n):
            copy = pltpu.make_async_remote_copy(
                src_ref=sources[j],
                dst_ref=landings[j],
                send_sem=pair_sends.at[j],
                recv_sem=pair_recvs.at[j],
                device_id=device_at(moved(me, "zl", 1 - me["zl"])),
                device_id_type=MESH,
            )
            copy.start()
            pairs.append(copy)
        second = me["zl"] == 1
        for j, copy in enumerate(pairs):
            copy.wait()
            mine, other = sources[j][...], landings[j][...]
            joined[j][...] = jnp.concatenate(
                [jnp.where(second, other, mine), jnp.where(second, mine, other)], 1
            ).astype(joined[j].dtype)
            sources[j] = joined[j]
            own.append(keep(j))
    for copy in own:
        copy.wait()
    copies, shared = [], []

    def flow(j, dims, lead, leads, first, rows, share_to, order):
        target = targets[j]
        order = tuple(d for d in order if d != share_to)
        columns = target.shape[-1]

        def view(sel, half):
            place_in = (pl.ds(lead, leads),) + tuple(sel[d] for d in dims)
            if half is None:
                return target.at[place_in + (pl.ds(first, rows),)]
            if rows >= 32:
                return target.at[place_in + (pl.ds(first + half * (rows // 2), rows // 2),)]
            return target.at[
                place_in + (pl.ds(first, rows), pl.ds(half * (columns // 2), columns // 2))
            ]

        def send(sel, dim, to, half=None):
            k = len(copies)
            part = view(sel, half)
            copy = pltpu.make_async_remote_copy(
                src_ref=part,
                dst_ref=part,
                send_sem=send_sems.at[k],
                recv_sem=recv_sems.at[k],
                device_id=device_at(moved(me, dim, to)),
                device_id_type=MESH,
            )
            copy.start()
            copies.append(copy)
            return copy

        def share(sel):
            if share_to is not None:
                shared.append(send(sel, share_to, 1 - me[share_to]))

        def whole(sel, dim):
            if dim == "z":
                return dict(sel, zh=pl.ds(0, 2), zl=pl.ds(0, 2))
            return dict(sel, **{dim: pl.ds(0, RING[dim])})

        sel = dict(me)
        for at, dim in enumerate(order):
            if RING[dim] == 2:
                copy = send(sel, dim, 1 - me[dim])
                if at == 0:
                    share(sel)
                yield
                copy.wait_recv()
                share(moved(sel, dim, 1 - me[dim]))
            else:
                right, left = (me[dim] + 1) % 4, (me[dim] + 3) % 4
                up = send(sel, dim, right)
                down = send(sel, dim, left)
                if at == 0:
                    share(sel)
                yield
                up.wait_recv()
                on_up = send(moved(sel, dim, left), dim, right, 0)
                share(moved(sel, dim, left))
                down.wait_recv()
                on_down = send(moved(sel, dim, right), dim, left, 1)
                share(moved(sel, dim, right))
                yield
                on_up.wait_recv()
                on_down.wait_recv()
                share(moved(sel, dim, (me[dim] + 2) % 4))
            sel = whole(sel, dim)

    advance([flow(j, dims, *piece) for j, (dims, pieces) in enumerate(jobs) for piece in pieces])
    for copy in shared:
        copy.wait_recv()
    for copy in copies:
        copy.wait_send()


def gather(jobs, blocks, collective_id, paired=False):
    n = gather_copies(jobs)
    shapes = []
    for j, ((dims, _), b) in enumerate(zip(jobs, blocks)):
        lead, rows, columns = b.shape
        shapes.append(
            jax.ShapeDtypeStruct(
                (lead,) + tuple(RING[d] for d in dims) + (rows * 2 if paired else rows, columns),
                jnp.bfloat16 if paired else b.dtype,
            )
        )
    scratch = [
        pltpu.SemaphoreType.DMA((n,)),
        pltpu.SemaphoreType.DMA((n,)),
        pltpu.SemaphoreType.DMA((len(jobs),)),
    ]
    if paired:
        scratch += [pltpu.SemaphoreType.DMA((len(jobs),))] * 2
        scratch += [pltpu.VMEM(b.shape, jnp.float32) for b in blocks]
        scratch += [
            pltpu.VMEM((b.shape[0], b.shape[1] * 2, b.shape[2]), jnp.bfloat16) for b in blocks
        ]
    return pl.pallas_call(
        functools.partial(gather_kernel, jobs, paired),
        out_shape=shapes,
        in_specs=[pl.BlockSpec(memory_space=pltpu.VMEM)] * len(jobs),
        out_specs=[pl.BlockSpec(memory_space=pl.ANY)] * len(jobs),
        scratch_shapes=scratch,
        compiler_params=pltpu.CompilerParams(collective_id=collective_id, has_side_effects=True),
        cost_estimate=pl.CostEstimate(flops=0, bytes_accessed=60_000_000, transcendentals=0),
    )(*blocks)


def scatter_buffers(jobs, shapes):
    buffers, sems = [], 0
    for (dims, pieces), shape in zip(jobs, shapes):
        for _, leads, order in pieces:
            left = dims
            for dim in order:
                left = tuple(d for d in left if d != dim)
                block = (leads,) + tuple(RING[d] for d in left) + shape[-2:]
                buffers.append(pltpu.VMEM((RING[dim] - 1,) + block, jnp.bfloat16))
                if left:
                    buffers.append(pltpu.VMEM(block, jnp.bfloat16))
                sems += RING[dim] - 1
    return buffers, sems


def scatter_kernel(jobs, *refs):
    n = len(jobs)
    sources, targets = refs[:n], list(refs[n : 2 * n])
    buffers = list(refs[2 * n :])
    paired = [j for j in range(n) if jobs[j][0] == PAIRS]
    if paired:
        landings = {}
        for j in paired:
            targets[j], landings[j] = buffers.pop(0), buffers.pop(0)
        pair_sends, pair_recvs = buffers.pop(0), buffers.pop(0)
    send_sems, recv_sems = buffers[-2:]
    buffers = buffers[:-2]
    me = place()
    peers = []
    for dim in network_dims(jobs) + (["zl"] if paired and "zl" not in network_dims(jobs) else []):
        for step in range(1, RING[dim]):
            peers.append(device_at(moved(me, dim, (me[dim] + step) % RING[dim])))
    greet(peers)
    copies = []

    def flow(j, dims, lead, leads, order, held):
        current, left, base = sources[j], dims, lead
        for (landing, total), dim in zip(held, order):
            size = RING[dim]
            rest = tuple(d for d in left if d != dim)
            mine = []
            for step in range(1, size):
                to = (me[dim] + step) % size
                k = len(copies)
                index = tuple(to if d == dim else pl.ds(0, RING[d]) for d in left)
                copy = pltpu.make_async_remote_copy(
                    src_ref=current.at[(pl.ds(base, leads),) + index],
                    dst_ref=landing.at[step - 1],
                    send_sem=send_sems.at[k],
                    recv_sem=recv_sems.at[k],
                    device_id=device_at(moved(me, dim, to)),
                    device_id_type=MESH,
                )
                copy.start()
                copies.append(copy)
                mine.append(copy)
            yield
            for copy in mine:
                copy.wait_recv()
            to_base = 0 if rest else lead
            looped = rest[:1]
            trips = leads * math.prod(RING[d] for d in looped)

            def add(i, carry, current=current, landing=landing, total=total, left=left, base=base):
                at = i // RING[looped[0]] if looped else i
                inner = {looped[0]: i % RING[looped[0]]} if looped else {}
                inner[dim] = me[dim]
                index = tuple(inner.get(d, pl.ds(0, RING[d])) for d in left)
                value = current[(base + at,) + index].astype(jnp.float32)
                short = tuple(inner.get(d, pl.ds(0, RING[d])) for d in rest)
                for step in range(size - 1):
                    value += landing[(step, at) + short].astype(jnp.float32)
                total[(to_base + at,) + short] = value.astype(total.dtype)
                return carry

            lax.fori_loop(0, trips, add, 0)
            current, left, base = total, rest, 0

    live = []
    for j, (dims, pieces) in enumerate(jobs):
        for lead, leads, order in pieces:
            held, left = [], dims
            for dim in order:
                left = tuple(d for d in left if d != dim)
                landing = buffers.pop(0)
                held.append((landing, buffers.pop(0) if left else targets[j]))
            live.append(flow(j, dims, lead, leads, order, held))
    advance(live)
    for copy in copies:
        copy.wait_send()
    if paired:
        half = targets[paired[0]].shape[1] // 2
        theirs = pl.ds(pl.multiple_of((1 - me["zl"]) * half, half), half)
        ours = pl.ds(pl.multiple_of(me["zl"] * half, half), half)
        pairs = []
        for j in paired:
            copy = pltpu.make_async_remote_copy(
                src_ref=targets[j].at[:, theirs],
                dst_ref=landings[j],
                send_sem=pair_sends.at[j],
                recv_sem=pair_recvs.at[j],
                device_id=device_at(moved(me, "zl", 1 - me["zl"])),
                device_id_type=MESH,
            )
            copy.start()
            pairs.append(copy)
        for j, copy in zip(paired, pairs):
            copy.wait()
            refs[n + j][...] = targets[j][:, ours, :] + landings[j][...]


def scatter(jobs, blocks, collective_id):
    buffers, n = scatter_buffers(jobs, [b.shape for b in blocks])
    scratch = buffers + [pltpu.SemaphoreType.DMA((n,)), pltpu.SemaphoreType.DMA((n,))]
    shapes = [(b.shape[0],) + b.shape[-2:] for b in blocks]
    pairs = []
    for j, (dims, _) in enumerate(jobs):
        if dims == PAIRS:
            lead, rows, columns = shapes[j]
            shapes[j] = (lead, rows // 2, columns)
            pairs += [pltpu.VMEM((lead, rows, columns), jnp.float32), pltpu.VMEM(shapes[j], jnp.float32)]
    if pairs:
        scratch = pairs + [pltpu.SemaphoreType.DMA((len(jobs),))] * 2 + scratch
    return pl.pallas_call(
        functools.partial(scatter_kernel, jobs),
        out_shape=[jax.ShapeDtypeStruct(s, jnp.float32) for s in shapes],
        in_specs=[pl.BlockSpec(memory_space=pltpu.VMEM)] * len(jobs),
        out_specs=[pl.BlockSpec(memory_space=pltpu.VMEM)] * len(jobs),
        scratch_shapes=scratch,
        compiler_params=pltpu.CompilerParams(
            collective_id=collective_id, has_side_effects=True, vmem_limit_bytes=56 * 2**20
        ),
        cost_estimate=pl.CostEstimate(flops=0, bytes_accessed=60_000_000, transcendentals=0),
    )(*blocks)
CHUNK = 256


def transposed(left, right):
    return lax.dot_general(left, right, (((1,), (1,)), ((), ())), preferred_element_type=jnp.float32)


def on_rows(left, right):
    return lax.dot_general(left, right, (((0,), (0,)), ((), ())), preferred_element_type=jnp.float32)


def attend_kernel(query_ref, both_ref, key_at_ref, query_at_ref, mixed_ref, log_ref, score_ref):
    query = query_ref[0]
    query_at = query_at_ref[...]
    keys = both_ref.shape[1]
    peak = jnp.full((1, query.shape[0]), MASKED, jnp.float32)
    for start in range(0, keys, CHUNK):
        span = pl.ds(start, CHUNK)
        scores = transposed(both_ref[0, span], query)
        scores = jnp.where(key_at_ref[span] <= query_at, scores, MASKED)
        score_ref[span] = scores
        peak = jnp.maximum(peak, jnp.max(scores, 0, keepdims=True))
    total = jnp.zeros_like(peak)
    mixed = jnp.zeros((both_ref.shape[2], query.shape[0]), jnp.float32)
    for start in range(0, keys, CHUNK):
        span = pl.ds(start, CHUNK)
        weights = jnp.exp(score_ref[span] - peak)
        total += jnp.sum(weights, 0, keepdims=True)
        mixed += on_rows(both_ref[0, span], weights.astype(jnp.bfloat16))
    mixed_ref[0] = (mixed[HEAD_WIDTH:] / total).astype(mixed_ref.dtype)
    log_ref[0] = peak + jnp.log(total)


def attend_back_kernel(
    query_ref,
    both_ref,
    key_at_ref,
    query_at_ref,
    log_ref,
    upstream_ref,
    query_grad_ref,
    both_grad_ref,
    chance_ref,
    change_ref,
):
    query, upstream = query_ref[0], upstream_ref[0]
    query_at, log_total = query_at_ref[...], log_ref[0]
    keys = both_ref.shape[1]
    inner = jnp.zeros((1, query.shape[0]), jnp.float32)
    for start in range(0, keys, CHUNK):
        span = pl.ds(start, CHUNK)
        both = both_ref[0, span]
        scores = jnp.where(key_at_ref[span] <= query_at, transposed(both, query), MASKED)
        chance = jnp.exp(scores - log_total)
        change = transposed(both, upstream)
        chance_ref[span] = chance
        change_ref[span] = change
        inner += jnp.sum(chance * change, 0, keepdims=True)
    query_grad = jnp.zeros((both_ref.shape[2], query.shape[0]), jnp.float32)
    for start in range(0, keys, CHUNK):
        span = pl.ds(start, CHUNK)
        chance = chance_ref[span]
        grad_scores = (chance * (change_ref[span] - inner)).astype(jnp.bfloat16)
        both_grad_ref[0, span] = (
            jnp.dot(grad_scores, query, preferred_element_type=jnp.float32)
            + jnp.dot(
                chance.astype(jnp.bfloat16), upstream, preferred_element_type=jnp.float32
            )
        ).astype(both_grad_ref.dtype)
        query_grad += on_rows(both_ref[0, span], grad_scores)
    query_grad_ref[0] = query_grad[:HEAD_WIDTH]


def by_head(*block):
    return pl.BlockSpec((1,) + block, lambda g: (g, 0, 0))


def for_all(*block):
    return pl.BlockSpec(block, lambda g: (0, 0))


def attend(query, both, key_at, query_at):
    heads, queries, columns = query.shape
    keys = both.shape[1]
    return pl.pallas_call(
        attend_kernel,
        grid=(heads,),
        out_shape=[
            jax.ShapeDtypeStruct((heads, HEAD_WIDTH, queries), jnp.bfloat16),
            jax.ShapeDtypeStruct((heads, 1, queries), jnp.float32),
        ],
        in_specs=[
            by_head(queries, columns),
            by_head(keys, columns),
            for_all(keys, 1),
            for_all(1, queries),
        ],
        out_specs=[by_head(HEAD_WIDTH, queries), by_head(1, queries)],
        scratch_shapes=[pltpu.VMEM((keys, queries), jnp.float32)],
        compiler_params=pltpu.CompilerParams(vmem_limit_bytes=40 * 2**20),
        cost_estimate=pl.CostEstimate(
            flops=4 * heads * queries * keys * columns,
            bytes_accessed=6_000_000,
            transcendentals=heads * queries * keys,
        ),
    )(query, both, key_at, query_at)


def attend_back(query, both, key_at, query_at, log_total, upstream):
    heads, queries, columns = query.shape
    keys = both.shape[1]
    return pl.pallas_call(
        attend_back_kernel,
        grid=(heads,),
        out_shape=[
            jax.ShapeDtypeStruct((heads, HEAD_WIDTH, queries), jnp.float32),
            jax.ShapeDtypeStruct((heads, keys, columns), jnp.bfloat16),
        ],
        in_specs=[
            by_head(queries, columns),
            by_head(keys, columns),
            for_all(keys, 1),
            for_all(1, queries),
            by_head(1, queries),
            by_head(queries, columns),
        ],
        out_specs=[by_head(HEAD_WIDTH, queries), by_head(keys, columns)],
        scratch_shapes=[pltpu.VMEM((keys, queries), jnp.float32)] * 2,
        compiler_params=pltpu.CompilerParams(vmem_limit_bytes=40 * 2**20),
        cost_estimate=pl.CostEstimate(
            flops=10 * heads * queries * keys * columns,
            bytes_accessed=12_000_000,
            transcendentals=heads * queries * keys,
        ),
    )(query, both, key_at, query_at, log_total, upstream)


def expert_kernel(
    sent_ref,
    upstream_ref,
    picks_ref,
    gates_ref,
    inward_ref,
    outward_ref,
    rows_ref,
    grads_ref,
    hidden_ref,
    both_ref,
    back_ref,
    blend_ref,
    dgate_ref,
    found_ref,
):
    blocks, most = picks_ref.shape[1:3]

    def find(source):
        for b in range(blocks):
            found_ref[pl.ds(b * most, most)] = jnp.dot(
                picks_ref[0, b], source[b, :, :MODEL_WIDTH], preferred_element_type=jnp.float32
            )

    find(sent_ref)
    rows = found_ref[...].astype(jnp.bfloat16)
    rows_ref[0] = rows
    find(upstream_ref)
    gates = gates_ref[0]
    row_grads = (found_ref[...] * gates).astype(jnp.bfloat16)
    grads_ref[0] = row_grads
    upper = jnp.dot(rows, inward_ref[0, 0], preferred_element_type=jnp.float32)
    lower = jnp.dot(rows, inward_ref[0, 1], preferred_element_type=jnp.float32)
    sigmoid = jax.nn.sigmoid(upper)
    hidden = (upper * sigmoid * lower).astype(jnp.bfloat16)
    hidden_ref[0] = hidden
    grad_hidden = jnp.dot(row_grads, outward_ref[0], preferred_element_type=jnp.float32)
    grad_upper = (grad_hidden * lower * sigmoid * (1.0 + upper * (1.0 - sigmoid))).astype(
        jnp.bfloat16
    )
    grad_lower = (grad_hidden * (upper * sigmoid)).astype(jnp.bfloat16)
    both_ref[0, 0] = grad_upper
    both_ref[0, 1] = grad_lower
    outputs = transposed(hidden, outward_ref[0]).astype(jnp.bfloat16).astype(jnp.float32)
    dgate_ref[0] = jnp.sum(found_ref[...] * outputs, -1, keepdims=True)
    blend = outputs * gates
    for b in range(blocks):
        blend_ref[b, 0] = blend[b * most : (b + 1) * most].astype(jnp.bfloat16)
    back = transposed(grad_upper, inward_ref[0, 0]) + transposed(grad_lower, inward_ref[0, 1])
    for b in range(blocks):
        back_ref[b, 0] = back[b * most : (b + 1) * most].astype(jnp.bfloat16)


def expert_pass(sent, upstream, picks, gates, inward, outward):
    experts, blocks, most, rows = picks.shape
    capacity = blocks * most
    hidden = inward.shape[-1]

    def one(*block):
        return pl.BlockSpec((1,) + block, lambda e: (e,) + (0,) * len(block))

    def fixed(shape):
        return pl.BlockSpec(shape, lambda e: (0,) * len(shape), pipeline_mode=pl.Buffered(1))

    by_block = pl.BlockSpec((blocks, 1, most, MODEL_WIDTH), lambda e: (0, e, 0, 0))
    low_shape = functools.partial(jax.ShapeDtypeStruct, dtype=jnp.bfloat16)
    return pl.pallas_call(
        expert_kernel,
        grid=(experts,),
        out_shape=[
            low_shape((experts, capacity, MODEL_WIDTH)),
            low_shape((experts, capacity, MODEL_WIDTH)),
            low_shape((experts, capacity, hidden)),
            low_shape((experts, 2, capacity, hidden)),
            low_shape((blocks, experts, most, MODEL_WIDTH)),
            low_shape((blocks, experts, most, MODEL_WIDTH)),
            jax.ShapeDtypeStruct((experts, capacity, 1), jnp.float32),
        ],
        in_specs=[
            fixed(sent.shape),
            fixed(upstream.shape),
            one(blocks, most, rows),
            one(capacity, 1),
            one(2, MODEL_WIDTH, hidden),
            one(MODEL_WIDTH, hidden),
        ],
        out_specs=[
            one(capacity, MODEL_WIDTH),
            one(capacity, MODEL_WIDTH),
            one(capacity, hidden),
            one(2, capacity, hidden),
            by_block,
            by_block,
            one(capacity, 1),
        ],
        scratch_shapes=[pltpu.VMEM((capacity, MODEL_WIDTH), jnp.float32)],
        compiler_params=pltpu.CompilerParams(vmem_limit_bytes=56 * 2**20),
        cost_estimate=pl.CostEstimate(
            flops=16 * experts * capacity * MODEL_WIDTH * hidden,
            bytes_accessed=40_000_000,
            transcendentals=experts * capacity * hidden,
        ),
    )(sent, upstream, picks, gates, inward, outward)


def apply_rotation(tensor, cosine_values, sine_lookup):
    half_size = tensor.shape[-1] // 2
    leading = tensor[..., :half_size]
    trailing = tensor[..., half_size:]
    table_shape = (tensor.shape[0],) + (1,) * (tensor.ndim - 2) + (half_size,)
    cosine_values = cosine_values.reshape(table_shape)
    sine_lookup = sine_lookup.reshape(table_shape)
    return jnp.concatenate(
        [
            leading * cosine_values - trailing * sine_lookup,
            trailing * cosine_values + leading * sine_lookup,
        ],
        -1,
    )


def low(value):
    return value.astype(jnp.bfloat16)


def high(value):
    return value.astype(jnp.float32)


def product(spec, left, right):
    return jnp.einsum(spec, low(left), low(right), preferred_element_type=jnp.float32)


def orthogonal_kernel(matrix_ref, rows_ref, solved_ref):
    matrix = matrix_ref[...]
    norm = jnp.sqrt(jnp.sum(jnp.square(high(matrix)), keepdims=True)) + 1e-07
    scaled = high(rows_ref[...]) / norm
    gram = on_rows(matrix, matrix) / (norm * norm)

    def times(left, right):
        return jnp.dot(low(left), low(right), preferred_element_type=jnp.float32)

    for sweep_index in range(SCHULZ_STEPS):
        polynomial = SCHULZ_SQUARE * gram + SCHULZ_CUBIC * times(gram, gram)
        scaled = SCHULZ_LINEAR * scaled + times(scaled, polynomial)
        if sweep_index < SCHULZ_STEPS - 1:
            gram = SCHULZ_LINEAR * gram + times(gram, polynomial)
            gram = SCHULZ_LINEAR * gram + times(polynomial, gram)
    solved_ref[...] = (scaled * math.sqrt(MODEL_WIDTH)).astype(solved_ref.dtype)


def orthogonal(matrix, rows):
    return pl.pallas_call(
        orthogonal_kernel,
        out_shape=jax.ShapeDtypeStruct(rows.shape, jnp.bfloat16),
        compiler_params=pltpu.CompilerParams(vmem_limit_bytes=40 * 2**20),
        cost_estimate=pl.CostEstimate(
            flops=3_000_000_000, bytes_accessed=3_000_000, transcendentals=0
        ),
    )(matrix, rows)


def norm_backward(values_in, inverse, gain_row, grad_normed):
    weighted = gain_row * grad_normed
    grad_values = inverse * weighted - values_in * inverse**3 * jnp.mean(
        weighted * values_in, -1, keepdims=True
    )
    grad_gain = jnp.sum(grad_normed * values_in * inverse, 0)
    return (grad_values, grad_gain)


def two_halves(value):
    upper = low(value)
    return upper, low(value - high(upper))


def slots_of(chosen):
    rows = chosen.shape[1]
    before = jnp.tril(jnp.ones((rows, rows), jnp.bfloat16), -1)
    rank = jnp.einsum("st,bte->bes", before, low(chosen), preferred_element_type=jnp.float32)
    taken = jnp.swapaxes(chosen, 1, 2)
    slot = jnp.arange(MOST, dtype=jnp.int32)[None, None, :, None]
    filled = (rank.astype(jnp.int32)[:, :, None, :] == slot) & (taken[:, :, None, :] > 0.5)
    return filled


ONE_WAY, OTHER_WAY = ("zh", "x", "y", "c"), ("zh", "y", "x", "c")
ATTENTION_WEIGHTS = tuple(
    (PAIRS, ((0, 1, 0, 16, "c", ONE_WAY if i % 2 == 0 else OTHER_WAY),)) for i in range(7)
)


def over_fsdp(leads):
    return tuple(
        (i, 1, 0, 128) + ((None, ("zl", "x")) if i % 3 < 2 else ("zl", ("x", "zl")))
        for i in range(leads)
    )


KEYS_VALUES_EXPERTS = (
    (ALONG_CTX, tuple((i, 4, 0, 128, "c", ("zh", "y", "c")) for i in (0, 4))),
    (ALONG_FSDP, over_fsdp(4)),
)
TOKEN_ROWS = ((ALONG_CTX, tuple((0, 1, i, 64, "c", ("zh", "y", "c")) for i in (0, 64))),)
ATTENTION_MOMENTA = (
    (
        ALONG_FSDP,
        (
            (0, 1, 0, 64, None, ("zl", "x")),
            (0, 1, 64, 64, "zl", ("x", "zl")),
            (0, 1, 128, 16, None, ("zl", "x")),
        ),
    ),
)
SUM_ONE_WAY, SUM_OTHER_WAY = ("c", "x", "y", "zh"), ("c", "y", "x", "zh")
KEY_VALUE_SUMS = (
    (ALONG_CTX, ((0, 4, ("c", "y", "zh")), (4, 4, ("c", "y", "zh")))),
    (ALONG_FSDP, tuple((i, 1, ("x", "zl") if i % 2 == 0 else ("zl", "x")) for i in range(4))),
    (PAIRS, ((0, 1, SUM_OTHER_WAY),)),
    (PAIRS, ((0, 1, SUM_OTHER_WAY),)),
)
ATTENTION_SUMS = tuple(
    (PAIRS, ((0, 1, SUM_ONE_WAY if i % 2 == 0 else SUM_OTHER_WAY),)) for i in range(5)
)


def on_device(
    hidden_in,
    cotangent,
    block_deal,
    routes,
    query_key_value_weight,
    output_weight_matrix,
    router_weights,
    norm_gains,
    expert_in,
    expert_out,
    query_key_value_momentum,
    output_momentum,
    router_moment,
    gain_moment,
    in_moment,
    down_moment,
):
    ctx_count = lax.axis_size("ctx")
    fsdp_count = lax.axis_size("fsdp")
    device_count = ctx_count * fsdp_count
    ctx_index = lax.axis_index("ctx")
    rows = hidden_in.shape[1]
    sequence_length = rows * ctx_count
    half_rows = rows // 2
    shard = query_key_value_weight.shape[1]
    width = query_key_value_weight.shape[2]
    group_width = QUERY_HEADS // KEY_VALUE_HEADS
    score_scale = 1.0 / math.sqrt(HEAD_WIDTH)

    steps = jnp.arange(half_rows, dtype=jnp.int32)[None, :]
    token_positions = (block_deal[:, None] * half_rows + steps).reshape(sequence_length)
    local_deal = lax.dynamic_slice_in_dim(block_deal, ctx_index * 2, 2)
    local_pos = (local_deal[:, None] * half_rows + steps).reshape(rows)
    half_size = HEAD_WIDTH // 2
    powers = jnp.arange(half_size).astype(jnp.float32) * (2.0 / HEAD_WIDTH)
    frequency = jnp.exp(-math.log(ROTARY_BASE) * powers)
    angles = local_pos.astype(jnp.float32)[:, None] * frequency[None, :]
    cosine_values, sine_lookup = jnp.cos(angles), jnp.sin(angles)
    key_at = token_positions[:, None]
    query_at = jnp.tile(local_pos, group_width)[None, :]

    spare = jnp.concatenate(
        [
            jnp.pad(router_weights.reshape(1, -1), ((0, 0), (0, width - shard * E))),
            jnp.pad(norm_gains.reshape(1, -1), ((0, shard - 2), (0, width - 2 * shard))),
        ],
        0,
    )
    *weights, spare_full = gather(
        ATTENTION_WEIGHTS,
        [
            high(block)[None]
            for block in [query_key_value_weight[j] for j in range(4)]
            + [output_weight_matrix[j] for j in range(2)]
            + [spare]
        ],
        1,
        paired=True,
    )
    weights = [w.reshape(MODEL_WIDTH, width) for w in weights]
    qkv_full, out_full = weights[:4], weights[4:]
    spare_full = spare_full.reshape(device_count, shard, width)
    router_full = spare_full[:, 0, : shard * E].reshape(MODEL_WIDTH, E)
    gains_full = (
        spare_full[:, 1, : 2 * shard]
        .reshape(device_count, 2, shard)
        .transpose(1, 0, 2)
        .reshape(2, MODEL_WIDTH)
    )

    part = expert_in.shape[2]
    experts_here = expert_in.shape[0]
    cotangent_all = lax.all_gather(cotangent[0], "ctx", axis=0)
    down_full = lax.all_gather(expert_out, "fsdp", axis=1, tiled=True)

    tokens = high(hidden_in[0])
    inverse_first = lax.rsqrt(jnp.mean(tokens * tokens, -1, keepdims=True) + EPSILON)
    gain_first = high(gains_full[0])
    normed = low(tokens * inverse_first * gain_first)
    split_heads = [
        product("td,dw->tw", normed, qkv_full[j]).reshape(rows, KEY_VALUE_HEADS, HEAD_WIDTH)
        for j in range(4)
    ]
    keys_local = low(apply_rotation(split_heads[2], cosine_values, sine_lookup))
    values_local = low(split_heads[3])
    keys_values, gateup_full = gather(
        KEYS_VALUES_EXPERTS,
        [
            jnp.concatenate([keys_local, values_local], -1).transpose(1, 0, 2),
            expert_in.reshape(2 * experts_here, part, width),
        ],
        2,
    )
    gateup_full = gateup_full.reshape(experts_here, 2, MODEL_WIDTH, width)
    query_matrix = low(
        apply_rotation(jnp.stack(split_heads[:2], 1), cosine_values, sine_lookup)
    )
    keys_values = keys_values.reshape(KEY_VALUE_HEADS, sequence_length, 2 * HEAD_WIDTH)

    def heads_first(values, before, after):
        values = values.reshape(rows, KEY_VALUE_HEADS, group_width, HEAD_WIDTH)
        values = values.transpose(1, 2, 0, 3).reshape(KEY_VALUE_HEADS, group_width * rows, HEAD_WIDTH)
        return jnp.pad(values, ((0, 0), (0, 0), (before, after)))

    def rows_first(values):
        values = values.reshape(KEY_VALUE_HEADS, HEAD_WIDTH, group_width, rows)
        return values.transpose(3, 0, 2, 1).reshape(rows, 2, width)

    queries = heads_first(query_matrix * score_scale, 0, HEAD_WIDTH)
    mixture, log_total = attend(queries, keys_values, key_at, query_at)
    mixture_rows = rows_first(mixture)
    residual = tokens + sum(
        product("tw,dw->td", mixture_rows[:, j], out_full[j]) for j in range(2)
    )
    inverse_second = lax.rsqrt(jnp.mean(residual * residual, -1, keepdims=True) + EPSILON)
    gain_second = high(gains_full[1])
    normed_second = low(residual * inverse_second * gain_second)
    logits = product("td,de->te", normed_second, router_full)
    routed = routes[0]
    chosen = jnp.sum(
        high(routed[:, :, None] == jnp.arange(E, dtype=jnp.int32)[None, None, :]), 1
    )
    peak = jnp.max(jnp.where(chosen > 0.5, logits, MASKED), -1, keepdims=True)
    weighed = jnp.where(chosen > 0.5, jnp.exp(jnp.minimum(logits - peak, 0.0)), 0.0)
    gates = weighed / jnp.sum(weighed, -1, keepdims=True)
    upstream = high(cotangent[0])

    gate_upper, gate_lower = two_halves(gates)
    (sent,) = gather(
        TOKEN_ROWS,
        [
            jnp.concatenate(
                [normed_second, gate_upper, gate_lower, low(chosen), jnp.zeros_like(gate_upper)], 1
            )[None]
        ],
        3,
    )
    sent = sent.reshape(ctx_count, rows, MODEL_WIDTH + 4 * E)

    def mine(start):
        return lax.dynamic_slice_in_dim(
            sent, MODEL_WIDTH + start + ctx_index * experts_here, experts_here, 2
        )

    gates_mine = high(mine(0)) + high(mine(E))
    filled = slots_of(high(mine(2 * E)))
    picks = low(filled)
    capacity = ctx_count * MOST
    row_gates = jnp.sum(
        jnp.where(filled, jnp.swapaxes(gates_mine, 1, 2)[:, :, None, :], 0.0), -1
    ).transpose(1, 0, 2).reshape(experts_here, capacity, 1)

    expert_rows, row_grads, hidden, grad_both, back_rows, blend_sent, row_dgate = expert_pass(
        sent, cotangent_all, picks.transpose(1, 0, 2, 3), row_gates, gateup_full, down_full
    )
    row_dgate = row_dgate.reshape(experts_here, ctx_count, MOST).transpose(1, 0, 2)
    dgate_upper, dgate_lower = two_halves(row_dgate.reshape(ctx_count, experts_here * MOST))
    dgate_rows = jnp.stack([dgate_upper, dgate_lower], 1)
    dgate_rows = jnp.pad(
        dgate_rows, ((0, 0), (0, 6), (0, MODEL_WIDTH - experts_here * MOST))
    )
    back_rows = back_rows.reshape(ctx_count, experts_here * MOST, MODEL_WIDTH)
    back_sent = jnp.concatenate([back_rows, dgate_rows], 1)
    back_returned = lax.all_to_all(back_sent, "ctx", split_axis=0, concat_axis=0, tiled=True)
    blend_sent = blend_sent.reshape(ctx_count, experts_here * MOST, MODEL_WIDTH)
    blend_sent, back_returned = lax.optimization_barrier((blend_sent, back_returned))
    blend_returned = lax.all_to_all(blend_sent, "ctx", split_axis=0, concat_axis=0, tiled=True)

    grad_gateup = low(product("erd,ejrf->ejdf", expert_rows, grad_both))
    grad_down = low(product("erd,erf->def", row_grads, hidden))
    grad_down = lax.psum_scatter(grad_down, "fsdp", scatter_dimension=0, tiled=True)

    own_filled = slots_of(chosen[None])[0]
    own_picks = low(own_filled).reshape(E * MOST, rows)
    back_values = back_returned[:, : experts_here * MOST].reshape(E * MOST, MODEL_WIDTH)
    back_sum = product("st,sd->td", own_picks, back_values)
    own_dgate = high(back_returned[:, experts_here * MOST, : experts_here * MOST]) + high(
        back_returned[:, experts_here * MOST + 1, : experts_here * MOST]
    )
    grad_gates = jnp.sum(
        jnp.where(own_filled, own_dgate.reshape(E, MOST, 1), 0.0), 1
    ).T
    grad_logits = low(gates * (grad_gates - jnp.sum(gates * grad_gates, -1, keepdims=True)))
    grad_router_part = product("td,te->de", normed_second, grad_logits)
    grad_normed_second = back_sum + product("te,de->td", grad_logits, router_full)
    grad_residual_norm, grad_gain_second = norm_backward(
        residual, inverse_second, gain_second, grad_normed_second
    )
    grad_residual = upstream + grad_residual_norm
    grad_attention = low(grad_residual)
    grad_out_parts = [product("td,tw->dw", grad_attention, mixture_rows[:, j]) for j in range(2)]
    mixture_gradient = low(
        jnp.stack([product("td,dw->tw", grad_attention, out_full[j]) for j in range(2)], 1)
    )
    query_gradient, grad_keys_values = attend_back(
        queries,
        keys_values,
        key_at,
        query_at,
        log_total,
        heads_first(mixture_gradient, HEAD_WIDTH, 0),
    )
    query_gradient = rows_first(query_gradient * score_scale)
    grad_keys_values, blend_returned = lax.optimization_barrier((grad_keys_values, blend_returned))

    def as_pairs(part):
        return low(part).reshape(1, 4, 2, 2, 4, 2 * shard, width)

    local_gradient, in_grad, *out_grad = scatter(
        KEY_VALUE_SUMS,
        [
            grad_keys_values.reshape(KEY_VALUE_HEADS, 4, 2, 2, rows, 2 * HEAD_WIDTH),
            grad_gateup.reshape(2 * experts_here, 4, 2, part, width),
        ]
        + [as_pairs(part) for part in grad_out_parts],
        4,
    )
    local_gradient = local_gradient.transpose(1, 0, 2)
    in_grad = in_grad.reshape(experts_here, 2, part, width)
    down_grad = high(grad_down).transpose(1, 0, 2)
    in_moment_new = MOMENTUM_DECAY * in_moment + in_grad
    down_moment_new = MOMENTUM_DECAY * down_moment + down_grad
    expert_count = experts_here * 3
    expert_stack = low(jnp.concatenate([in_moment_new, down_moment_new[:, None]], 1)).reshape(
        expert_count, part, width
    )
    expert_stack = jnp.pad(expert_stack, ((0, fsdp_count - expert_count), (0, 0), (0, 0)))
    expert_part = lax.all_to_all(expert_stack, "fsdp", split_axis=0, concat_axis=0, tiled=True)
    query_row_gradient = apply_rotation(
        query_gradient.reshape(rows, 2, KEY_VALUE_HEADS, HEAD_WIDTH), cosine_values, -sine_lookup
    )
    key_row_gradient = apply_rotation(
        local_gradient[..., :HEAD_WIDTH],
        cosine_values,
        -sine_lookup,
    )
    grad_project = low(
        jnp.concatenate(
            [
                query_row_gradient.reshape(rows, 2, width),
                key_row_gradient.reshape(rows, 1, width),
                local_gradient[..., HEAD_WIDTH:].reshape(rows, 1, width),
            ],
            1,
        )
    )
    grad_qkv_parts = [product("td,tw->dw", normed, grad_project[:, j]) for j in range(4)]
    grad_normed_first = sum(
        product("tw,dw->td", grad_project[:, j], qkv_full[j]) for j in range(4)
    )
    grad_tokens_norm, grad_gain_first = norm_backward(
        tokens, inverse_first, gain_first, grad_normed_first
    )
    input_grad = (grad_residual + grad_tokens_norm)[None]

    gains_part = jnp.stack([grad_gain_first, grad_gain_second], 0)
    gains_part = gains_part.reshape(2, device_count, shard).transpose(1, 0, 2)
    spare_part = jnp.concatenate(
        [
            jnp.pad(
                low(grad_router_part).reshape(device_count, 1, shard * E),
                ((0, 0), (0, 0), (0, width - shard * E)),
            ),
            jnp.pad(
                low(gains_part).reshape(device_count, 1, 2 * shard),
                ((0, 0), (0, shard - 2), (0, width - 2 * shard)),
            ),
        ],
        1,
    )
    parts = [as_pairs(part) for part in grad_qkv_parts + [spare_part]]
    parts[0], expert_part = lax.optimization_barrier((parts[0], expert_part))
    summed = scatter(ATTENTION_SUMS, parts, 5)
    qkv_grad, out_grad = jnp.concatenate(summed[:4], 0), jnp.concatenate(out_grad, 0)
    router_grad = summed[4][0, 0, : shard * E].reshape(shard, E)
    gain_grad = summed[4][0, 1, : 2 * shard].reshape(2, shard)
    qkv_moment_new = MOMENTUM_DECAY * query_key_value_momentum + qkv_grad
    out_moment_new = MOMENTUM_DECAY * output_momentum + out_grad
    gain_moment_new = AVERAGE_DECAY * gain_moment + (1.0 - AVERAGE_DECAY) * gain_grad
    router_moment_new = AVERAGE_DECAY * router_moment + (1.0 - AVERAGE_DECAY) * router_grad
    squares = jnp.concatenate(
        [
            jnp.sum(gain_moment_new * gain_moment_new, 1),
            jnp.sum(router_moment_new * router_moment_new)[None],
        ]
    )

    def squares_rows(count):
        upper = low(squares)
        row = jnp.concatenate([upper, low(squares - high(upper))])
        return jnp.pad(row[None], ((0, count - 1), (0, width - 6)))

    def squares_total(row):
        row = jnp.sum(high(row), 0)
        return row[:3] + row[3:6]

    attn_stack = low(jnp.concatenate([qkv_moment_new, out_moment_new], 0))
    attn_stack = jnp.pad(attn_stack, ((0, ctx_count - 6), (0, 0), (0, 0)))
    attn_stack = jnp.concatenate(
        [attn_stack, jnp.broadcast_to(squares_rows(shard)[None], attn_stack.shape)], 1
    )
    attn_rows = lax.all_to_all(attn_stack, "ctx", split_axis=0, concat_axis=0, tiled=True)
    squares = squares_total(attn_rows[:, shard, :6])
    attn_rows = attn_rows[:, :shard].reshape(ctx_count * shard, width)
    expert_part = expert_part.reshape(MODEL_WIDTH, width)
    expert_solved = orthogonal(expert_part, expert_part)
    attn_rows, expert_solved = lax.optimization_barrier((attn_rows, expert_solved))
    expert_ortho = lax.all_to_all(
        expert_solved.reshape(fsdp_count, part, width),
        "fsdp",
        split_axis=0,
        concat_axis=0,
        tiled=True,
    )
    (attn_full,) = gather(
        ATTENTION_MOMENTA, [jnp.concatenate([attn_rows, squares_rows(2 * shard)], 0)[None]], 6
    )
    attn_full, expert_ortho = lax.optimization_barrier((attn_full, expert_ortho))
    attn_full = attn_full.reshape(fsdp_count, (ctx_count + 2) * shard, width)
    squares = squares_total(attn_full[:, ctx_count * shard, :6])
    attn_full = attn_full[:, : ctx_count * shard].reshape(MODEL_WIDTH, width)
    attn_solved = orthogonal(attn_full, attn_rows)
    attn_ortho = lax.all_to_all(
        attn_solved.reshape(ctx_count, shard, width),
        "ctx",
        split_axis=0,
        concat_axis=0,
        tiled=True,
    )
    attn_ortho = high(attn_ortho[:6])
    expert_ortho = high(expert_ortho[:expert_count]).reshape(experts_here, 3, part, width)
    in_new = (
        high(expert_in) * (1.0 - RATE_EXPERT * WEIGHT_DECAY) - RATE_EXPERT * expert_ortho[:, :2]
    )
    down_new = (
        high(expert_out) * (1.0 - RATE_DOWN * WEIGHT_DECAY) - RATE_DOWN * expert_ortho[:, 2]
    )
    qkv_new = (
        high(query_key_value_weight) * (1.0 - RATE_INPUT * WEIGHT_DECAY)
        - RATE_INPUT * attn_ortho[:4]
    )
    out_new = (
        high(output_weight_matrix) * (1.0 - RATE_OUTPUT * WEIGHT_DECAY)
        - RATE_OUTPUT * attn_ortho[4:6]
    )

    gains_new = (
        high(norm_gains)
        - RATE_GAIN * gain_moment_new * lax.rsqrt(squares[:2] / MODEL_WIDTH + EPSILON)[:, None]
    )
    router_new = high(router_weights) - RATE_ROUTER * router_moment_new * lax.rsqrt(
        squares[2] / (MODEL_WIDTH * E) + EPSILON
    )
    hidden_out = low(
        residual + product("st,sd->td", own_picks, blend_returned.reshape(E * MOST, MODEL_WIDTH))
    )[None]
    return (
        hidden_out,
        input_grad,
        qkv_grad,
        out_grad,
        router_grad,
        gain_grad,
        in_grad,
        down_grad,
        qkv_moment_new,
        out_moment_new,
        router_moment_new,
        gain_moment_new,
        in_moment_new,
        down_moment_new,
        qkv_new,
        out_new,
        router_new,
        gains_new,
        in_new,
        down_new,
    )


def solution(mesh):
    placed = (
        P("fsdp", "ctx", None),
        P("fsdp", "ctx", None),
        P(),
        P("fsdp", "ctx", None),
        P(None, ("ctx", "fsdp"), None),
        P(None, ("ctx", "fsdp"), None),
        P(("ctx", "fsdp"), None),
        P(None, ("ctx", "fsdp")),
        P("ctx", None, "fsdp", None),
        P("ctx", "fsdp", None),
        P(None, ("ctx", "fsdp"), None),
        P(None, ("ctx", "fsdp"), None),
        P(("ctx", "fsdp"), None),
        P(None, ("ctx", "fsdp")),
        P("ctx", None, "fsdp", None),
        P("ctx", "fsdp", None),
    )
    return jax.shard_map(
        on_device,
        mesh=mesh,
        in_specs=placed,
        out_specs=(
            P("fsdp", "ctx", None),
            P("fsdp", "ctx", None),
            P(None, ("ctx", "fsdp"), None),
            P(None, ("ctx", "fsdp"), None),
            P(("ctx", "fsdp"), None),
            P(None, ("ctx", "fsdp")),
            P("ctx", None, "fsdp", None),
            P("ctx", "fsdp", None),
            P(None, ("ctx", "fsdp"), None),
            P(None, ("ctx", "fsdp"), None),
            P(("ctx", "fsdp"), None),
            P(None, ("ctx", "fsdp")),
            P("ctx", None, "fsdp", None),
            P("ctx", "fsdp", None),
            P(None, ("ctx", "fsdp"), None),
            P(None, ("ctx", "fsdp"), None),
            P(("ctx", "fsdp"), None),
            P(None, ("ctx", "fsdp")),
            P("ctx", None, "fsdp", None),
            P("ctx", "fsdp", None),
        ),
        check_vma=False,
    )
```

```python
import functools
import math

import jax
import jax.numpy as jnp
from jax import lax
from jax.experimental import pallas as pl
from jax.experimental.pallas import tpu as pltpu
from jax.sharding import PartitionSpec as P

MODEL_WIDTH = 1024
QUERY_HEADS = 16
KEY_VALUE_HEADS = 8
HEAD_WIDTH = 64
E = 32
TOP = 8
MOST = 40
SCHULZ_STEPS = 2


EPSILON = 1e-06
ROTARY_BASE = 10000.0
MOMENTUM_DECAY = 0.95
AVERAGE_DECAY = 0.9
SCHULZ_LINEAR = 3.4445
SCHULZ_SQUARE = -4.775
SCHULZ_CUBIC = 2.0315
WEIGHT_DECAY = 0.1
RATE_INPUT = 0.016
RATE_OUTPUT = 0.25
RATE_EXPERT = 0.031
RATE_DOWN = 0.031
RATE_GAIN = 0.5
RATE_ROUTER = 0.008
MASKED = -1e30

MESH = pl.DeviceIdType.MESH
RING = {"x": 4, "y": 4, "z": 4, "zh": 2, "zl": 2, "c": 2}
EVERY = ("y", "zh", "c", "x", "zl")
PAIRS = ("y", "zh", "c", "x")
ALONG_CTX = ("y", "zh", "c")
ALONG_FSDP = ("x", "zl")


def place():
    ctx = lax.axis_index("ctx")
    fsdp = lax.axis_index("fsdp")
    at = {"y": ctx // 4, "zh": (ctx // 2) % 2, "c": ctx % 2, "x": fsdp // 2, "zl": fsdp % 2}
    at["z"] = at["zh"] * 2 + at["zl"]
    return at


def moved(at, dim, to):
    at = dict(at)
    at[dim] = to
    if dim == "z":
        at["zh"], at["zl"] = to // 2, to % 2
    return at


def device_at(at):
    return ((at["y"] * 2 + at["zh"]) * 2 + at["c"], at["x"] * 2 + at["zl"])


def greet(peers):
    barrier = pltpu.get_barrier_semaphore()
    for peer in peers:
        pl.semaphore_signal(barrier, inc=1, device_id=peer, device_id_type=MESH)
    pl.semaphore_wait(barrier, len(peers))


def network_dims(jobs):
    found = []
    for dims, pieces in jobs:
        for piece in pieces:
            for dim in piece[-1]:
                if dim not in found:
                    found.append(dim)
    return found


def advance(live):
    while live:
        live = [f for f in live if next(f, "end") != "end"]


def gather_copies(jobs):
    total = 0
    for dims, pieces in jobs:
        for piece in pieces:
            shared = 0 if piece[-2] is None else 1
            total += shared
            for dim in piece[-1]:
                if dim != piece[-2]:
                    total += 1 + shared if RING[dim] == 2 else 4 + 3 * shared
    return total


def gather_kernel(jobs, paired, *refs):
    n = len(jobs)
    sources, targets = list(refs[:n]), refs[n : 2 * n]
    send_sems, recv_sems, local_sems = refs[2 * n : 2 * n + 3]
    me = place()
    dims_used = network_dims(jobs) + (["zl"] if paired else [])
    peers = []
    for dim in dims_used:
        size = RING[dim]
        for step in (1,) if size == 2 else (1, 3):
            peers.append(device_at(moved(me, dim, (me[dim] + step) % size)))

    def keep(j):
        dims = jobs[j][0]
        copy = pltpu.make_async_copy(
            sources[j],
            targets[j].at[(slice(None),) + tuple(me[d] for d in dims)],
            local_sems.at[j],
        )
        copy.start()
        return copy

    own = [] if paired else [keep(j) for j in range(n)]
    greet(peers)
    if paired:
        pair_sends, pair_recvs = refs[2 * n + 3 : 2 * n + 5]
        landings, joined = refs[2 * n + 5 : 3 * n + 5], refs[3 * n + 5 :]
        pairs = []
        for j in range(n):
            copy = pltpu.make_async_remote_copy(
                src_ref=sources[j],
                dst_ref=landings[j],
                send_sem=pair_sends.at[j],
                recv_sem=pair_recvs.at[j],
                device_id=device_at(moved(me, "zl", 1 - me["zl"])),
                device_id_type=MESH,
            )
            copy.start()
            pairs.append(copy)
        second = me["zl"] == 1
        for j, copy in enumerate(pairs):
            copy.wait()
            mine, other = sources[j][...], landings[j][...]
            joined[j][...] = jnp.concatenate(
                [jnp.where(second, other, mine), jnp.where(second, mine, other)], 1
            ).astype(joined[j].dtype)
            sources[j] = joined[j]
            own.append(keep(j))
    for copy in own:
        copy.wait()
    copies, shared = [], []

    def flow(j, dims, lead, leads, first, rows, share_to, order):
        target = targets[j]
        order = tuple(d for d in order if d != share_to)
        columns = target.shape[-1]

        def view(sel, half):
            place_in = (pl.ds(lead, leads),) + tuple(sel[d] for d in dims)
            if half is None:
                return target.at[place_in + (pl.ds(first, rows),)]
            if rows >= 32:
                return target.at[place_in + (pl.ds(first + half * (rows // 2), rows // 2),)]
            return target.at[
                place_in + (pl.ds(first, rows), pl.ds(half * (columns // 2), columns // 2))
            ]

        def send(sel, dim, to, half=None):
            k = len(copies)
            part = view(sel, half)
            copy = pltpu.make_async_remote_copy(
                src_ref=part,
                dst_ref=part,
                send_sem=send_sems.at[k],
                recv_sem=recv_sems.at[k],
                device_id=device_at(moved(me, dim, to)),
                device_id_type=MESH,
            )
            copy.start()
            copies.append(copy)
            return copy

        def share(sel):
            if share_to is not None:
                shared.append(send(sel, share_to, 1 - me[share_to]))

        def whole(sel, dim):
            if dim == "z":
                return dict(sel, zh=pl.ds(0, 2), zl=pl.ds(0, 2))
            return dict(sel, **{dim: pl.ds(0, RING[dim])})

        sel = dict(me)
        for at, dim in enumerate(order):
            if RING[dim] == 2:
                copy = send(sel, dim, 1 - me[dim])
                if at == 0:
                    share(sel)
                yield
                copy.wait_recv()
                share(moved(sel, dim, 1 - me[dim]))
            else:
                right, left = (me[dim] + 1) % 4, (me[dim] + 3) % 4
                up = send(sel, dim, right)
                down = send(sel, dim, left)
                if at == 0:
                    share(sel)
                yield
                up.wait_recv()
                on_up = send(moved(sel, dim, left), dim, right, 0)
                share(moved(sel, dim, left))
                down.wait_recv()
                on_down = send(moved(sel, dim, right), dim, left, 1)
                share(moved(sel, dim, right))
                yield
                on_up.wait_recv()
                on_down.wait_recv()
                share(moved(sel, dim, (me[dim] + 2) % 4))
            sel = whole(sel, dim)

    advance([flow(j, dims, *piece) for j, (dims, pieces) in enumerate(jobs) for piece in pieces])
    for copy in shared:
        copy.wait_recv()
    for copy in copies:
        copy.wait_send()


def gather(jobs, blocks, collective_id, paired=False):
    n = gather_copies(jobs)
    shapes = []
    for j, ((dims, _), b) in enumerate(zip(jobs, blocks)):
        lead, rows, columns = b.shape
        shapes.append(
            jax.ShapeDtypeStruct(
                (lead,) + tuple(RING[d] for d in dims) + (rows * 2 if paired else rows, columns),
                jnp.bfloat16 if paired else b.dtype,
            )
        )
    scratch = [
        pltpu.SemaphoreType.DMA((n,)),
        pltpu.SemaphoreType.DMA((n,)),
        pltpu.SemaphoreType.DMA((len(jobs),)),
    ]
    if paired:
        scratch += [pltpu.SemaphoreType.DMA((len(jobs),))] * 2
        scratch += [pltpu.VMEM(b.shape, jnp.float32) for b in blocks]
        scratch += [
            pltpu.VMEM((b.shape[0], b.shape[1] * 2, b.shape[2]), jnp.bfloat16) for b in blocks
        ]
    return pl.pallas_call(
        functools.partial(gather_kernel, jobs, paired),
        out_shape=shapes,
        in_specs=[pl.BlockSpec(memory_space=pltpu.VMEM)] * len(jobs),
        out_specs=[pl.BlockSpec(memory_space=pl.ANY)] * len(jobs),
        scratch_shapes=scratch,
        compiler_params=pltpu.CompilerParams(
            collective_id=collective_id, has_side_effects=True, vmem_limit_bytes=8 * 2**20
        ),
        cost_estimate=pl.CostEstimate(flops=0, bytes_accessed=60_000_000, transcendentals=0),
    )(*blocks)


def scatter_buffers(jobs, shapes):
    buffers, sems = [], 0
    for (dims, pieces), shape in zip(jobs, shapes):
        for _, leads, order in pieces:
            left = dims
            for dim in order:
                left = tuple(d for d in left if d != dim)
                block = (leads,) + tuple(RING[d] for d in left) + shape[-2:]
                buffers.append(pltpu.VMEM((RING[dim] - 1,) + block, jnp.bfloat16))
                if left:
                    buffers.append(pltpu.VMEM(block, jnp.bfloat16))
                sems += RING[dim] - 1
    return buffers, sems


def scatter_kernel(jobs, *refs):
    n = len(jobs)
    sources, targets = refs[:n], list(refs[n : 2 * n])
    buffers = list(refs[2 * n :])
    paired = [j for j in range(n) if jobs[j][0] == PAIRS]
    if paired:
        landings = {}
        for j in paired:
            targets[j], landings[j] = buffers.pop(0), buffers.pop(0)
        pair_sends, pair_recvs = buffers.pop(0), buffers.pop(0)
    send_sems, recv_sems = buffers[-2:]
    buffers = buffers[:-2]
    me = place()
    peers = []
    for dim in network_dims(jobs) + (["zl"] if paired and "zl" not in network_dims(jobs) else []):
        for step in range(1, RING[dim]):
            peers.append(device_at(moved(me, dim, (me[dim] + step) % RING[dim])))
    greet(peers)
    copies = []

    def flow(j, dims, lead, leads, order, held):
        current, left, base = sources[j], dims, lead
        for (landing, total), dim in zip(held, order):
            size = RING[dim]
            rest = tuple(d for d in left if d != dim)
            mine = []
            for step in range(1, size):
                to = (me[dim] + step) % size
                k = len(copies)
                index = tuple(to if d == dim else pl.ds(0, RING[d]) for d in left)
                copy = pltpu.make_async_remote_copy(
                    src_ref=current.at[(pl.ds(base, leads),) + index],
                    dst_ref=landing.at[step - 1],
                    send_sem=send_sems.at[k],
                    recv_sem=recv_sems.at[k],
                    device_id=device_at(moved(me, dim, to)),
                    device_id_type=MESH,
                )
                copy.start()
                copies.append(copy)
                mine.append(copy)
            yield
            for copy in mine:
                copy.wait_recv()
            to_base = 0 if rest else lead
            looped = rest[:1]
            trips = leads * math.prod(RING[d] for d in looped)

            def add(i, carry, current=current, landing=landing, total=total, left=left, base=base):
                at = i // RING[looped[0]] if looped else i
                inner = {looped[0]: i % RING[looped[0]]} if looped else {}
                inner[dim] = me[dim]
                index = tuple(inner.get(d, pl.ds(0, RING[d])) for d in left)
                value = current[(base + at,) + index].astype(jnp.float32)
                short = tuple(inner.get(d, pl.ds(0, RING[d])) for d in rest)
                for step in range(size - 1):
                    value += landing[(step, at) + short].astype(jnp.float32)
                total[(to_base + at,) + short] = value.astype(total.dtype)
                return carry

            lax.fori_loop(0, trips, add, 0)
            current, left, base = total, rest, 0

    live = []
    for j, (dims, pieces) in enumerate(jobs):
        for lead, leads, order in pieces:
            held, left = [], dims
            for dim in order:
                left = tuple(d for d in left if d != dim)
                landing = buffers.pop(0)
                held.append((landing, buffers.pop(0) if left else targets[j]))
            live.append(flow(j, dims, lead, leads, order, held))
    advance(live)
    for copy in copies:
        copy.wait_send()
    if paired:
        half = targets[paired[0]].shape[1] // 2
        theirs = pl.ds(pl.multiple_of((1 - me["zl"]) * half, half), half)
        ours = pl.ds(pl.multiple_of(me["zl"] * half, half), half)
        pairs = []
        for j in paired:
            copy = pltpu.make_async_remote_copy(
                src_ref=targets[j].at[:, theirs],
                dst_ref=landings[j],
                send_sem=pair_sends.at[j],
                recv_sem=pair_recvs.at[j],
                device_id=device_at(moved(me, "zl", 1 - me["zl"])),
                device_id_type=MESH,
            )
            copy.start()
            pairs.append(copy)
        for j, copy in zip(paired, pairs):
            copy.wait()
            refs[n + j][...] = targets[j][:, ours, :] + landings[j][...]


def scatter(jobs, blocks, collective_id):
    buffers, n = scatter_buffers(jobs, [b.shape for b in blocks])
    scratch = buffers + [pltpu.SemaphoreType.DMA((n,)), pltpu.SemaphoreType.DMA((n,))]
    shapes = [(b.shape[0],) + b.shape[-2:] for b in blocks]
    pairs = []
    for j, (dims, _) in enumerate(jobs):
        if dims == PAIRS:
            lead, rows, columns = shapes[j]
            shapes[j] = (lead, rows // 2, columns)
            pairs += [pltpu.VMEM((lead, rows, columns), jnp.float32), pltpu.VMEM(shapes[j], jnp.float32)]
    if pairs:
        scratch = pairs + [pltpu.SemaphoreType.DMA((len(jobs),))] * 2 + scratch
    return pl.pallas_call(
        functools.partial(scatter_kernel, jobs),
        out_shape=[jax.ShapeDtypeStruct(s, jnp.float32) for s in shapes],
        in_specs=[pl.BlockSpec(memory_space=pltpu.VMEM)] * len(jobs),
        out_specs=[pl.BlockSpec(memory_space=pltpu.VMEM)] * len(jobs),
        scratch_shapes=scratch,
        compiler_params=pltpu.CompilerParams(
            collective_id=collective_id, has_side_effects=True, vmem_limit_bytes=30 * 2**20
        ),
        cost_estimate=pl.CostEstimate(flops=0, bytes_accessed=60_000_000, transcendentals=0),
    )(*blocks)
CHUNK = 256


def transposed(left, right):
    return lax.dot_general(left, right, (((1,), (1,)), ((), ())), preferred_element_type=jnp.float32)


def on_rows(left, right):
    return lax.dot_general(left, right, (((0,), (0,)), ((), ())), preferred_element_type=jnp.float32)


def attend_kernel(query_ref, both_ref, key_at_ref, query_at_ref, mixed_ref, log_ref, score_ref):
    query = query_ref[0]
    query_at = query_at_ref[...]
    keys = both_ref.shape[1]
    peak = jnp.full((1, query.shape[0]), MASKED, jnp.float32)
    for start in range(0, keys, CHUNK):
        span = pl.ds(start, CHUNK)
        scores = transposed(both_ref[0, span], query)
        scores = jnp.where(key_at_ref[span] <= query_at, scores, MASKED)
        score_ref[span] = scores
        peak = jnp.maximum(peak, jnp.max(scores, 0, keepdims=True))
    total = jnp.zeros_like(peak)
    mixed = jnp.zeros((both_ref.shape[2], query.shape[0]), jnp.float32)
    for start in range(0, keys, CHUNK):
        span = pl.ds(start, CHUNK)
        weights = jnp.exp(score_ref[span] - peak)
        total += jnp.sum(weights, 0, keepdims=True)
        mixed += on_rows(both_ref[0, span], weights.astype(jnp.bfloat16))
    mixed_ref[0] = (mixed[HEAD_WIDTH:] / total).astype(mixed_ref.dtype)
    log_ref[0] = peak + jnp.log(total)


def attend_back_kernel(
    query_ref,
    both_ref,
    key_at_ref,
    query_at_ref,
    log_ref,
    upstream_ref,
    query_grad_ref,
    both_grad_ref,
    chance_ref,
    change_ref,
):
    query, upstream = query_ref[0], upstream_ref[0]
    query_at, log_total = query_at_ref[...], log_ref[0]
    keys = both_ref.shape[1]
    inner = jnp.zeros((1, query.shape[0]), jnp.float32)
    for start in range(0, keys, CHUNK):
        span = pl.ds(start, CHUNK)
        both = both_ref[0, span]
        scores = jnp.where(key_at_ref[span] <= query_at, transposed(both, query), MASKED)
        chance = jnp.exp(scores - log_total)
        change = transposed(both, upstream)
        chance_ref[span] = chance
        change_ref[span] = change
        inner += jnp.sum(chance * change, 0, keepdims=True)
    query_grad = jnp.zeros((both_ref.shape[2], query.shape[0]), jnp.float32)
    for start in range(0, keys, CHUNK):
        span = pl.ds(start, CHUNK)
        chance = chance_ref[span]
        grad_scores = (chance * (change_ref[span] - inner)).astype(jnp.bfloat16)
        both_grad_ref[0, span] = (
            jnp.dot(grad_scores, query, preferred_element_type=jnp.float32)
            + jnp.dot(
                chance.astype(jnp.bfloat16), upstream, preferred_element_type=jnp.float32
            )
        ).astype(both_grad_ref.dtype)
        query_grad += on_rows(both_ref[0, span], grad_scores)
    query_grad_ref[0] = query_grad[:HEAD_WIDTH]


def by_head(*block):
    return pl.BlockSpec((1,) + block, lambda g: (g, 0, 0))


def for_all(*block):
    return pl.BlockSpec(block, lambda g: (0, 0))


def attend(query, both, key_at, query_at):
    heads, queries, columns = query.shape
    keys = both.shape[1]
    return pl.pallas_call(
        attend_kernel,
        grid=(heads,),
        out_shape=[
            jax.ShapeDtypeStruct((heads, HEAD_WIDTH, queries), jnp.bfloat16),
            jax.ShapeDtypeStruct((heads, 1, queries), jnp.float32),
        ],
        in_specs=[
            by_head(queries, columns),
            by_head(keys, columns),
            for_all(keys, 1),
            for_all(1, queries),
        ],
        out_specs=[by_head(HEAD_WIDTH, queries), by_head(1, queries)],
        scratch_shapes=[pltpu.VMEM((keys, queries), jnp.float32)],
        compiler_params=pltpu.CompilerParams(vmem_limit_bytes=16 * 2**20),
        cost_estimate=pl.CostEstimate(
            flops=4 * heads * queries * keys * columns,
            bytes_accessed=6_000_000,
            transcendentals=heads * queries * keys,
        ),
    )(query, both, key_at, query_at)


def attend_back(query, both, key_at, query_at, log_total, upstream):
    heads, queries, columns = query.shape
    keys = both.shape[1]
    return pl.pallas_call(
        attend_back_kernel,
        grid=(heads,),
        out_shape=[
            jax.ShapeDtypeStruct((heads, HEAD_WIDTH, queries), jnp.float32),
            jax.ShapeDtypeStruct((heads, keys, columns), jnp.bfloat16),
        ],
        in_specs=[
            by_head(queries, columns),
            by_head(keys, columns),
            for_all(keys, 1),
            for_all(1, queries),
            by_head(1, queries),
            by_head(queries, columns),
        ],
        out_specs=[by_head(HEAD_WIDTH, queries), by_head(keys, columns)],
        scratch_shapes=[pltpu.VMEM((keys, queries), jnp.float32)] * 2,
        compiler_params=pltpu.CompilerParams(vmem_limit_bytes=20 * 2**20),
        cost_estimate=pl.CostEstimate(
            flops=10 * heads * queries * keys * columns,
            bytes_accessed=12_000_000,
            transcendentals=heads * queries * keys,
        ),
    )(query, both, key_at, query_at, log_total, upstream)


def project_kernel(tokens_ref, gain_ref, cosine_ref, sine_ref, *refs):
    weights, (normed_ref, query_ref, both_ref) = refs[:4], refs[4:]
    tokens = high(tokens_ref[...])
    inverse = lax.rsqrt(jnp.mean(tokens * tokens, -1, keepdims=True) + EPSILON)
    normed = low(tokens * inverse * gain_ref[...])
    normed_ref[...] = normed
    rows, width = normed.shape[0], 2 * HEAD_WIDTH
    lane = lax.broadcasted_iota(jnp.int32, (rows, width), 1)
    first_head = lane < HEAD_WIDTH
    leading = lane % HEAD_WIDTH < HEAD_WIDTH // 2
    cosine, sine = cosine_ref[...], sine_ref[...]

    def tiles(j):
        values = jnp.dot(normed, weights[j][...], preferred_element_type=jnp.float32)
        return [values[:, i * width : (i + 1) * width] for i in range(KEY_VALUE_HEADS // 2)]

    def turned(tile):
        behind = pltpu.roll(tile, HEAD_WIDTH // 2, 1)
        ahead = pltpu.roll(tile, width - HEAD_WIDTH // 2, 1)
        return tile * cosine + jnp.where(leading, -ahead, behind) * sine

    for j in range(2):
        for i, tile in enumerate(tiles(j)):
            tile = turned(tile) * (1.0 / math.sqrt(HEAD_WIDTH))
            for r, part in enumerate((tile, pltpu.roll(tile, HEAD_WIDTH, 1))):
                query_ref[j * 4 + i, pl.ds(r * rows, rows)] = low(jnp.where(first_head, part, 0.0))
    for i, (key, value) in enumerate(zip(tiles(2), tiles(3))):
        key = turned(key)
        both_ref[2 * i] = low(jnp.where(first_head, key, pltpu.roll(value, HEAD_WIDTH, 1)))
        both_ref[2 * i + 1] = low(jnp.where(first_head, pltpu.roll(key, HEAD_WIDTH, 1), value))


def project(tokens, gain, cosine, sine, weights):
    rows = tokens.shape[0]
    return pl.pallas_call(
        project_kernel,
        out_shape=[
            jax.ShapeDtypeStruct(tokens.shape, jnp.bfloat16),
            jax.ShapeDtypeStruct((KEY_VALUE_HEADS, 2 * rows, 2 * HEAD_WIDTH), jnp.bfloat16),
            jax.ShapeDtypeStruct((KEY_VALUE_HEADS, rows, 2 * HEAD_WIDTH), jnp.bfloat16),
        ],
        compiler_params=pltpu.CompilerParams(vmem_limit_bytes=16 * 2**20),
        cost_estimate=pl.CostEstimate(
            flops=540_000_000, bytes_accessed=6_000_000, transcendentals=0
        ),
    )(tokens, gain, cosine, sine, *weights)


def project_back_kernel(normed_ref, query_ref, both_ref, cosine_ref, sine_ref, *refs):
    weights, parts, grad_ref = refs[:4], refs[4:8], refs[8]
    normed = normed_ref[...]
    rows, width = normed.shape[0], 2 * HEAD_WIDTH
    lane = lax.broadcasted_iota(jnp.int32, (rows, width), 1)
    first_head = lane < HEAD_WIDTH
    leading = lane % HEAD_WIDTH < HEAD_WIDTH // 2
    cosine, sine = cosine_ref[...], sine_ref[...]
    keys, values = [], []
    for i in range(KEY_VALUE_HEADS // 2):
        even, odd = both_ref[2 * i], both_ref[2 * i + 1]
        tile = jnp.where(first_head, even, pltpu.roll(odd, HEAD_WIDTH, 1))
        behind = pltpu.roll(tile, HEAD_WIDTH // 2, 1)
        ahead = pltpu.roll(tile, width - HEAD_WIDTH // 2, 1)
        keys.append(low(tile * cosine + jnp.where(leading, ahead, -behind) * sine))
        values.append(low(jnp.where(first_head, pltpu.roll(even, HEAD_WIDTH, 1), odd)))
    total = None
    for j in range(4):
        grads = query_ref[j] if j < 2 else jnp.concatenate(keys if j == 2 else values, 1)
        parts[j][...] = low(on_rows(normed, grads))
        term = transposed(grads, weights[j][...])
        total = term if total is None else total + term
    grad_ref[...] = total


def project_back(normed, query_grads, both_grads, cosine, sine, weights):
    shape = weights[0].shape
    return pl.pallas_call(
        project_back_kernel,
        out_shape=[jax.ShapeDtypeStruct(shape, jnp.bfloat16)] * 4
        + [jax.ShapeDtypeStruct(normed.shape, jnp.float32)],
        compiler_params=pltpu.CompilerParams(vmem_limit_bytes=24 * 2**20),
        cost_estimate=pl.CostEstimate(
            flops=1_080_000_000, bytes_accessed=10_000_000, transcendentals=0
        ),
    )(normed, query_grads, both_grads, cosine, sine, *weights)


def expert_kernel(
    sent_ref,
    upstream_ref,
    picks_ref,
    gates_ref,
    inward_ref,
    outward_ref,
    rows_ref,
    grads_ref,
    hidden_ref,
    both_ref,
    back_ref,
    blend_ref,
    dgate_ref,
    found_ref,
):
    blocks, most = picks_ref.shape[1:3]

    def find(source):
        for b in range(blocks):
            found_ref[pl.ds(b * most, most)] = jnp.dot(
                picks_ref[0, b], source[b, :, :MODEL_WIDTH], preferred_element_type=jnp.float32
            )

    find(sent_ref)
    rows = found_ref[...].astype(jnp.bfloat16)
    rows_ref[0] = rows
    find(upstream_ref)
    gates = gates_ref[0]
    row_grads = (found_ref[...] * gates).astype(jnp.bfloat16)
    grads_ref[0] = row_grads
    upper = jnp.dot(rows, inward_ref[0, 0], preferred_element_type=jnp.float32)
    lower = jnp.dot(rows, inward_ref[0, 1], preferred_element_type=jnp.float32)
    sigmoid = jax.nn.sigmoid(upper)
    hidden = (upper * sigmoid * lower).astype(jnp.bfloat16)
    hidden_ref[0] = hidden
    grad_hidden = jnp.dot(row_grads, outward_ref[0], preferred_element_type=jnp.float32)
    grad_upper = (grad_hidden * lower * sigmoid * (1.0 + upper * (1.0 - sigmoid))).astype(
        jnp.bfloat16
    )
    grad_lower = (grad_hidden * (upper * sigmoid)).astype(jnp.bfloat16)
    both_ref[0, 0] = grad_upper
    both_ref[0, 1] = grad_lower
    outputs = transposed(hidden, outward_ref[0]).astype(jnp.bfloat16).astype(jnp.float32)
    dgate_ref[0] = jnp.sum(found_ref[...] * outputs, -1, keepdims=True)
    blend = outputs * gates
    for b in range(blocks):
        blend_ref[b, 0] = blend[b * most : (b + 1) * most].astype(jnp.bfloat16)
    back = transposed(grad_upper, inward_ref[0, 0]) + transposed(grad_lower, inward_ref[0, 1])
    for b in range(blocks):
        back_ref[b, 0] = back[b * most : (b + 1) * most].astype(jnp.bfloat16)


def expert_pass(sent, upstream, picks, gates, inward, outward):
    experts, blocks, most, rows = picks.shape
    capacity = blocks * most
    hidden = inward.shape[-1]

    def one(*block):
        return pl.BlockSpec((1,) + block, lambda e: (e,) + (0,) * len(block))

    def fixed(shape):
        return pl.BlockSpec(shape, lambda e: (0,) * len(shape), pipeline_mode=pl.Buffered(1))

    by_block = pl.BlockSpec((blocks, 1, most, MODEL_WIDTH), lambda e: (0, e, 0, 0))
    low_shape = functools.partial(jax.ShapeDtypeStruct, dtype=jnp.bfloat16)
    return pl.pallas_call(
        expert_kernel,
        grid=(experts,),
        out_shape=[
            low_shape((experts, capacity, MODEL_WIDTH)),
            low_shape((experts, capacity, MODEL_WIDTH)),
            low_shape((experts, capacity, hidden)),
            low_shape((experts, 2, capacity, hidden)),
            low_shape((blocks, experts, most, MODEL_WIDTH)),
            low_shape((blocks, experts, most, MODEL_WIDTH)),
            jax.ShapeDtypeStruct((experts, capacity, 1), jnp.float32),
        ],
        in_specs=[
            fixed(sent.shape),
            fixed(upstream.shape),
            one(blocks, most, rows),
            one(capacity, 1),
            one(2, MODEL_WIDTH, hidden),
            one(MODEL_WIDTH, hidden),
        ],
        out_specs=[
            one(capacity, MODEL_WIDTH),
            one(capacity, MODEL_WIDTH),
            one(capacity, hidden),
            one(2, capacity, hidden),
            by_block,
            by_block,
            one(capacity, 1),
        ],
        scratch_shapes=[pltpu.VMEM((capacity, MODEL_WIDTH), jnp.float32)],
        compiler_params=pltpu.CompilerParams(vmem_limit_bytes=48 * 2**20),
        cost_estimate=pl.CostEstimate(
            flops=16 * experts * capacity * MODEL_WIDTH * hidden,
            bytes_accessed=40_000_000,
            transcendentals=experts * capacity * hidden,
        ),
    )(sent, upstream, picks, gates, inward, outward)


def apply_rotation(tensor, cosine_values, sine_lookup):
    half_size = tensor.shape[-1] // 2
    leading = tensor[..., :half_size]
    trailing = tensor[..., half_size:]
    table_shape = (tensor.shape[0],) + (1,) * (tensor.ndim - 2) + (half_size,)
    cosine_values = cosine_values.reshape(table_shape)
    sine_lookup = sine_lookup.reshape(table_shape)
    return jnp.concatenate(
        [
            leading * cosine_values - trailing * sine_lookup,
            trailing * cosine_values + leading * sine_lookup,
        ],
        -1,
    )


def low(value):
    return value.astype(jnp.bfloat16)


def high(value):
    return value.astype(jnp.float32)


def product(spec, left, right):
    return jnp.einsum(spec, low(left), low(right), preferred_element_type=jnp.float32)


def orthogonal_kernel(matrix_ref, rows_ref, solved_ref):
    matrix = matrix_ref[...]
    norm = jnp.sqrt(jnp.sum(jnp.square(high(matrix)), keepdims=True)) + 1e-07
    scaled = high(rows_ref[...]) / norm
    gram = on_rows(matrix, matrix) / (norm * norm)

    def times(left, right):
        return jnp.dot(low(left), low(right), preferred_element_type=jnp.float32)

    for sweep_index in range(SCHULZ_STEPS):
        polynomial = SCHULZ_SQUARE * gram + SCHULZ_CUBIC * times(gram, gram)
        scaled = SCHULZ_LINEAR * scaled + times(scaled, polynomial)
        if sweep_index < SCHULZ_STEPS - 1:
            gram = SCHULZ_LINEAR * gram + times(gram, polynomial)
            gram = SCHULZ_LINEAR * gram + times(polynomial, gram)
    solved_ref[...] = (scaled * math.sqrt(MODEL_WIDTH)).astype(solved_ref.dtype)


def orthogonal(matrix, rows):
    return pl.pallas_call(
        orthogonal_kernel,
        out_shape=jax.ShapeDtypeStruct(rows.shape, jnp.bfloat16),
        compiler_params=pltpu.CompilerParams(vmem_limit_bytes=16 * 2**20),
        cost_estimate=pl.CostEstimate(
            flops=3_000_000_000, bytes_accessed=3_000_000, transcendentals=0
        ),
    )(matrix, rows)


def norm_backward(values_in, inverse, gain_row, grad_normed):
    weighted = gain_row * grad_normed
    grad_values = inverse * weighted - values_in * inverse**3 * jnp.mean(
        weighted * values_in, -1, keepdims=True
    )
    grad_gain = jnp.sum(grad_normed * values_in * inverse, 0)
    return (grad_values, grad_gain)


def two_halves(value):
    upper = low(value)
    return upper, low(value - high(upper))


def slots_of(chosen):
    rows = chosen.shape[1]
    before = jnp.tril(jnp.ones((rows, rows), jnp.bfloat16), -1)
    rank = jnp.einsum("st,bte->bes", before, low(chosen), preferred_element_type=jnp.float32)
    taken = jnp.swapaxes(chosen, 1, 2)
    slot = jnp.arange(MOST, dtype=jnp.int32)[None, None, :, None]
    filled = (rank.astype(jnp.int32)[:, :, None, :] == slot) & (taken[:, :, None, :] > 0.5)
    return filled


ONE_WAY, OTHER_WAY = ("zh", "x", "y", "c"), ("zh", "y", "x", "c")
ATTENTION_WEIGHTS = tuple(
    (PAIRS, ((0, 1, 0, 16, "c", ONE_WAY if i % 2 == 0 else OTHER_WAY),)) for i in range(7)
)


def over_fsdp(leads):
    return tuple(
        (i, 1, 0, 128) + ((None, ("zl", "x")) if i % 3 < 2 else ("zl", ("x", "zl")))
        for i in range(leads)
    )


KEYS_VALUES_EXPERTS = (
    (ALONG_CTX, tuple((i, 4, 0, 128, "c", ("zh", "y", "c")) for i in (0, 4))),
    (ALONG_FSDP, over_fsdp(4)),
)
TOKEN_ROWS = ((ALONG_CTX, tuple((0, 1, i, 64, "c", ("zh", "y", "c")) for i in (0, 64))),)
ATTENTION_MOMENTA = (
    (
        ALONG_FSDP,
        (
            (0, 1, 0, 64, None, ("zl", "x")),
            (0, 1, 64, 64, "zl", ("x", "zl")),
            (0, 1, 128, 16, None, ("zl", "x")),
        ),
    ),
)
SUM_ONE_WAY, SUM_OTHER_WAY = ("c", "x", "y", "zh"), ("c", "y", "x", "zh")
KEY_VALUE_SUMS = (
    (ALONG_CTX, ((0, 4, ("c", "y", "zh")), (4, 4, ("c", "y", "zh")))),
    (ALONG_FSDP, tuple((i, 1, ("x", "zl") if i % 2 == 0 else ("zl", "x")) for i in range(4))),
    (ALONG_FSDP, tuple((i, 1, ("x", "zl") if i % 2 == 0 else ("zl", "x")) for i in range(2))),
)
ATTENTION_SUMS = tuple(
    (PAIRS, ((0, 1, SUM_ONE_WAY if i % 2 == 0 else SUM_OTHER_WAY),)) for i in range(7)
)


def on_device(
    hidden_in,
    cotangent,
    block_deal,
    routes,
    query_key_value_weight,
    output_weight_matrix,
    router_weights,
    norm_gains,
    expert_in,
    expert_out,
    query_key_value_momentum,
    output_momentum,
    router_moment,
    gain_moment,
    in_moment,
    down_moment,
):
    ctx_count = lax.axis_size("ctx")
    fsdp_count = lax.axis_size("fsdp")
    ctx_index = lax.axis_index("ctx")
    rows = hidden_in.shape[1]
    sequence_length = rows * ctx_count
    half_rows = rows // 2
    shard = query_key_value_weight.shape[1]
    width = query_key_value_weight.shape[2]
    group_width = QUERY_HEADS // KEY_VALUE_HEADS
    score_scale = 1.0 / math.sqrt(HEAD_WIDTH)

    steps = jnp.arange(half_rows, dtype=jnp.int32)[None, :]
    token_positions = (block_deal[:, None] * half_rows + steps).reshape(sequence_length)
    local_deal = lax.dynamic_slice_in_dim(block_deal, ctx_index * 2, 2)
    local_pos = (local_deal[:, None] * half_rows + steps).reshape(rows)
    half_size = HEAD_WIDTH // 2
    powers = jnp.arange(half_size).astype(jnp.float32) * (2.0 / HEAD_WIDTH)
    frequency = jnp.exp(-math.log(ROTARY_BASE) * powers)
    angles = local_pos.astype(jnp.float32)[:, None] * frequency[None, :]
    cosine_values, sine_lookup = jnp.cos(angles), jnp.sin(angles)
    key_at = token_positions[:, None]
    query_at = jnp.tile(local_pos, group_width)[None, :]

    spare = jnp.concatenate([router_weights, norm_gains.T], 1)
    spare = jnp.pad(spare, ((0, 0), (0, width - E - 2)))
    *weights, spare_full = gather(
        ATTENTION_WEIGHTS,
        [
            high(block)[None]
            for block in [query_key_value_weight[j] for j in range(4)]
            + [output_weight_matrix[j] for j in range(2)]
            + [spare]
        ],
        1,
        paired=True,
    )
    weights = [w.reshape(MODEL_WIDTH, width) for w in weights]
    qkv_full, out_full = weights[:4], weights[4:]
    spare_full = spare_full.reshape(MODEL_WIDTH, width)
    router_full = spare_full[:, :E]
    gains_full = spare_full[:, E : E + 2].T

    part = expert_in.shape[2]
    experts_here = expert_in.shape[0]
    cotangent_all = lax.all_gather(cotangent[0], "ctx", axis=0)
    down_full = lax.all_gather(expert_out, "fsdp", axis=1, tiled=True)

    tokens = high(hidden_in[0])
    inverse_first = lax.rsqrt(jnp.mean(tokens * tokens, -1, keepdims=True) + EPSILON)
    gain_first = high(gains_full[0])
    cosine_tile = jnp.tile(cosine_values, (1, 4))
    sine_tile = jnp.tile(sine_lookup, (1, 4))
    normed, queries, keys_values = project(
        hidden_in[0], gain_first[None], cosine_tile, sine_tile, qkv_full
    )
    keys_values, gateup_full = gather(
        KEYS_VALUES_EXPERTS,
        [
            keys_values,
            expert_in.reshape(2 * experts_here, part, width),
        ],
        2,
    )
    gateup_full = gateup_full.reshape(experts_here, 2, MODEL_WIDTH, width)
    keys_values = keys_values.reshape(KEY_VALUE_HEADS, sequence_length, 2 * HEAD_WIDTH)

    def heads_first(values, before, after):
        values = values.reshape(rows, KEY_VALUE_HEADS, group_width, HEAD_WIDTH)
        values = values.transpose(1, 2, 0, 3).reshape(KEY_VALUE_HEADS, group_width * rows, HEAD_WIDTH)
        return jnp.pad(values, ((0, 0), (0, 0), (before, after)))

    def rows_first(values):
        values = values.reshape(KEY_VALUE_HEADS, HEAD_WIDTH, group_width, rows)
        return values.transpose(3, 0, 2, 1).reshape(rows, 2, width)

    mixture, log_total = attend(queries, keys_values, key_at, query_at)
    mixture_rows = rows_first(mixture)
    residual = tokens + sum(
        product("tw,dw->td", mixture_rows[:, j], out_full[j]) for j in range(2)
    )
    inverse_second = lax.rsqrt(jnp.mean(residual * residual, -1, keepdims=True) + EPSILON)
    gain_second = high(gains_full[1])
    normed_second = low(residual * inverse_second * gain_second)
    logits = product("td,de->te", normed_second, router_full)
    routed = routes[0]
    chosen = jnp.sum(
        high(routed[:, :, None] == jnp.arange(E, dtype=jnp.int32)[None, None, :]), 1
    )
    peak = jnp.max(jnp.where(chosen > 0.5, logits, MASKED), -1, keepdims=True)
    weighed = jnp.where(chosen > 0.5, jnp.exp(jnp.minimum(logits - peak, 0.0)), 0.0)
    gates = weighed / jnp.sum(weighed, -1, keepdims=True)
    upstream = high(cotangent[0])

    gate_upper, gate_lower = two_halves(gates)
    (sent,) = gather(
        TOKEN_ROWS,
        [
            jnp.concatenate(
                [normed_second, gate_upper, gate_lower, low(chosen), jnp.zeros_like(gate_upper)], 1
            )[None]
        ],
        3,
    )
    sent = sent.reshape(ctx_count, rows, MODEL_WIDTH + 4 * E)

    def mine(start):
        return lax.dynamic_slice_in_dim(
            sent, MODEL_WIDTH + start + ctx_index * experts_here, experts_here, 2
        )

    gates_mine = high(mine(0)) + high(mine(E))
    filled = slots_of(high(mine(2 * E)))
    picks = low(filled)
    capacity = ctx_count * MOST
    row_gates = jnp.sum(
        jnp.where(filled, jnp.swapaxes(gates_mine, 1, 2)[:, :, None, :], 0.0), -1
    ).transpose(1, 0, 2).reshape(experts_here, capacity, 1)

    expert_rows, row_grads, hidden, grad_both, back_rows, blend_sent, row_dgate = expert_pass(
        sent, cotangent_all, picks.transpose(1, 0, 2, 3), row_gates, gateup_full, down_full
    )
    row_dgate = row_dgate.reshape(experts_here, ctx_count, MOST).transpose(1, 0, 2)
    dgate_upper, dgate_lower = two_halves(row_dgate.reshape(ctx_count, experts_here * MOST))
    dgate_rows = jnp.stack([dgate_upper, dgate_lower], 1)
    dgate_rows = jnp.pad(
        dgate_rows, ((0, 0), (0, 6), (0, MODEL_WIDTH - experts_here * MOST))
    )
    back_rows = back_rows.reshape(ctx_count, experts_here * MOST, MODEL_WIDTH)
    back_sent = jnp.concatenate([back_rows, dgate_rows], 1)
    back_returned = lax.all_to_all(back_sent, "ctx", split_axis=0, concat_axis=0, tiled=True)
    blend_sent = blend_sent.reshape(ctx_count, experts_here * MOST, MODEL_WIDTH)
    blend_sent, back_returned = lax.optimization_barrier((blend_sent, back_returned))
    blend_returned = lax.all_to_all(blend_sent, "ctx", split_axis=0, concat_axis=0, tiled=True)

    grad_gateup = low(product("erd,ejrf->ejdf", expert_rows, grad_both))
    grad_down = low(product("erd,erf->edf", row_grads, hidden))

    own_filled = slots_of(chosen[None])[0]
    own_picks = low(own_filled).reshape(E * MOST, rows)
    back_picks = jnp.pad(
        own_picks.reshape(ctx_count, experts_here * MOST, rows), ((0, 0), (0, 8), (0, 0))
    )
    back_sum = product(
        "st,sd->td", back_picks.reshape(-1, rows), back_returned.reshape(-1, MODEL_WIDTH)
    )
    own_dgate = high(back_returned[:, experts_here * MOST, : experts_here * MOST]) + high(
        back_returned[:, experts_here * MOST + 1, : experts_here * MOST]
    )
    grad_gates = jnp.sum(
        jnp.where(own_filled, own_dgate.reshape(E, MOST, 1), 0.0), 1
    ).T
    grad_logits = low(gates * (grad_gates - jnp.sum(gates * grad_gates, -1, keepdims=True)))
    grad_router_part = product("td,te->de", normed_second, grad_logits)
    grad_normed_second = back_sum + product("te,de->td", grad_logits, router_full)
    grad_residual_norm, grad_gain_second = norm_backward(
        residual, inverse_second, gain_second, grad_normed_second
    )
    grad_residual = upstream + grad_residual_norm
    grad_attention = low(grad_residual)
    grad_out_parts = [product("td,tw->dw", grad_attention, mixture_rows[:, j]) for j in range(2)]
    mixture_gradient = low(
        jnp.stack([product("td,dw->tw", grad_attention, out_full[j]) for j in range(2)], 1)
    )
    query_gradient, grad_keys_values = attend_back(
        queries,
        keys_values,
        key_at,
        query_at,
        log_total,
        heads_first(mixture_gradient, HEAD_WIDTH, 0),
    )
    query_gradient = rows_first(query_gradient * score_scale)
    grad_keys_values, blend_returned = lax.optimization_barrier((grad_keys_values, blend_returned))

    def as_pairs(part):
        return low(part).reshape(1, 4, 2, 2, 4, 2 * shard, width)

    local_gradient, in_grad, down_grad = scatter(
        KEY_VALUE_SUMS,
        [
            grad_keys_values.reshape(KEY_VALUE_HEADS, 4, 2, 2, rows, 2 * HEAD_WIDTH),
            grad_gateup.reshape(2 * experts_here, 4, 2, part, width),
            grad_down.reshape(experts_here, 4, 2, part, width),
        ],
        4,
    )
    in_grad = in_grad.reshape(experts_here, 2, part, width)
    in_moment_new = MOMENTUM_DECAY * in_moment + in_grad
    down_moment_new = MOMENTUM_DECAY * down_moment + down_grad
    expert_count = experts_here * 3
    expert_stack = low(jnp.concatenate([in_moment_new, down_moment_new[:, None]], 1)).reshape(
        expert_count, part, width
    )
    expert_stack = jnp.pad(expert_stack, ((0, fsdp_count - expert_count), (0, 0), (0, 0)))
    expert_part = lax.all_to_all(expert_stack, "fsdp", split_axis=0, concat_axis=0, tiled=True)
    query_row_gradient = apply_rotation(
        query_gradient.reshape(rows, 2, KEY_VALUE_HEADS, HEAD_WIDTH), cosine_values, -sine_lookup
    )
    *grad_qkv_parts, grad_normed_first = project_back(
        normed,
        low(query_row_gradient.reshape(rows, 2, width)).transpose(1, 0, 2),
        local_gradient,
        cosine_tile,
        sine_tile,
        qkv_full,
    )
    grad_tokens_norm, grad_gain_first = norm_backward(
        tokens, inverse_first, gain_first, grad_normed_first
    )
    input_grad = (grad_residual + grad_tokens_norm)[None]

    gains_part = jnp.stack([grad_gain_first, grad_gain_second], 1)
    spare_part = low(jnp.concatenate([grad_router_part, gains_part], 1))
    spare_part = jnp.pad(spare_part, ((0, 0), (0, width - E - 2)))
    parts = [as_pairs(part) for part in grad_qkv_parts + grad_out_parts + [spare_part]]
    parts[0], expert_part = lax.optimization_barrier((parts[0], expert_part))
    summed = scatter(ATTENTION_SUMS, parts, 5)
    qkv_grad, out_grad = jnp.concatenate(summed[:4], 0), jnp.concatenate(summed[4:6], 0)
    router_grad = summed[6][0, :, :E]
    gain_grad = summed[6][0, :, E : E + 2].T
    qkv_moment_new = MOMENTUM_DECAY * query_key_value_momentum + qkv_grad
    out_moment_new = MOMENTUM_DECAY * output_momentum + out_grad
    gain_moment_new = AVERAGE_DECAY * gain_moment + (1.0 - AVERAGE_DECAY) * gain_grad
    router_moment_new = AVERAGE_DECAY * router_moment + (1.0 - AVERAGE_DECAY) * router_grad
    squares = jnp.concatenate(
        [
            jnp.sum(gain_moment_new * gain_moment_new, 1),
            jnp.sum(router_moment_new * router_moment_new)[None],
        ]
    )

    def squares_rows(count):
        upper = low(squares)
        row = jnp.concatenate([upper, low(squares - high(upper))])
        return jnp.pad(row[None], ((0, count - 1), (0, width - 6)))

    def squares_total(row):
        row = jnp.sum(high(row), 0)
        return row[:3] + row[3:6]

    attn_stack = low(jnp.concatenate([qkv_moment_new, out_moment_new], 0))
    attn_stack = jnp.pad(attn_stack, ((0, ctx_count - 6), (0, 0), (0, 0)))
    attn_stack = jnp.concatenate(
        [attn_stack, jnp.broadcast_to(squares_rows(shard)[None], attn_stack.shape)], 1
    )
    attn_rows = lax.all_to_all(attn_stack, "ctx", split_axis=0, concat_axis=0, tiled=True)
    squares = squares_total(attn_rows[:, shard, :6])
    attn_rows = attn_rows[:, :shard].reshape(ctx_count * shard, width)
    expert_part = expert_part.reshape(MODEL_WIDTH, width)
    expert_solved = orthogonal(expert_part, expert_part)
    attn_rows, expert_solved = lax.optimization_barrier((attn_rows, expert_solved))
    expert_ortho = lax.all_to_all(
        expert_solved.reshape(fsdp_count, part, width),
        "fsdp",
        split_axis=0,
        concat_axis=0,
        tiled=True,
    )
    (attn_full,) = gather(
        ATTENTION_MOMENTA, [jnp.concatenate([attn_rows, squares_rows(2 * shard)], 0)[None]], 6
    )
    attn_full, expert_ortho = lax.optimization_barrier((attn_full, expert_ortho))
    attn_full = attn_full.reshape(fsdp_count, (ctx_count + 2) * shard, width)
    squares = squares_total(attn_full[:, ctx_count * shard, :6])
    attn_full = attn_full[:, : ctx_count * shard].reshape(MODEL_WIDTH, width)
    attn_solved = orthogonal(attn_full, attn_rows)
    attn_ortho = lax.all_to_all(
        attn_solved.reshape(ctx_count, shard, width),
        "ctx",
        split_axis=0,
        concat_axis=0,
        tiled=True,
    )
    attn_ortho = high(attn_ortho[:6])
    expert_ortho = high(expert_ortho[:expert_count]).reshape(experts_here, 3, part, width)
    in_new = (
        high(expert_in) * (1.0 - RATE_EXPERT * WEIGHT_DECAY) - RATE_EXPERT * expert_ortho[:, :2]
    )
    down_new = (
        high(expert_out) * (1.0 - RATE_DOWN * WEIGHT_DECAY) - RATE_DOWN * expert_ortho[:, 2]
    )
    qkv_new = (
        high(query_key_value_weight) * (1.0 - RATE_INPUT * WEIGHT_DECAY)
        - RATE_INPUT * attn_ortho[:4]
    )
    out_new = (
        high(output_weight_matrix) * (1.0 - RATE_OUTPUT * WEIGHT_DECAY)
        - RATE_OUTPUT * attn_ortho[4:6]
    )

    gains_new = (
        high(norm_gains)
        - RATE_GAIN * gain_moment_new * lax.rsqrt(squares[:2] / MODEL_WIDTH + EPSILON)[:, None]
    )
    router_new = high(router_weights) - RATE_ROUTER * router_moment_new * lax.rsqrt(
        squares[2] / (MODEL_WIDTH * E) + EPSILON
    )
    hidden_out = low(
        residual + product("st,sd->td", own_picks, blend_returned.reshape(E * MOST, MODEL_WIDTH))
    )[None]
    return (
        hidden_out,
        input_grad,
        qkv_grad,
        out_grad,
        router_grad,
        gain_grad,
        in_grad,
        down_grad,
        qkv_moment_new,
        out_moment_new,
        router_moment_new,
        gain_moment_new,
        in_moment_new,
        down_moment_new,
        qkv_new,
        out_new,
        router_new,
        gains_new,
        in_new,
        down_new,
    )


def solution(mesh):
    placed = (
        P("fsdp", "ctx", None),
        P("fsdp", "ctx", None),
        P(),
        P("fsdp", "ctx", None),
        P(None, ("ctx", "fsdp"), None),
        P(None, ("ctx", "fsdp"), None),
        P(("ctx", "fsdp"), None),
        P(None, ("ctx", "fsdp")),
        P("ctx", None, "fsdp", None),
        P("ctx", "fsdp", None),
        P(None, ("ctx", "fsdp"), None),
        P(None, ("ctx", "fsdp"), None),
        P(("ctx", "fsdp"), None),
        P(None, ("ctx", "fsdp")),
        P("ctx", None, "fsdp", None),
        P("ctx", "fsdp", None),
    )
    return jax.shard_map(
        on_device,
        mesh=mesh,
        in_specs=placed,
        out_specs=(
            P("fsdp", "ctx", None),
            P("fsdp", "ctx", None),
            P(None, ("ctx", "fsdp"), None),
            P(None, ("ctx", "fsdp"), None),
            P(("ctx", "fsdp"), None),
            P(None, ("ctx", "fsdp")),
            P("ctx", None, "fsdp", None),
            P("ctx", "fsdp", None),
            P(None, ("ctx", "fsdp"), None),
            P(None, ("ctx", "fsdp"), None),
            P(("ctx", "fsdp"), None),
            P(None, ("ctx", "fsdp")),
            P("ctx", None, "fsdp", None),
            P("ctx", "fsdp", None),
            P(None, ("ctx", "fsdp"), None),
            P(None, ("ctx", "fsdp"), None),
            P(("ctx", "fsdp"), None),
            P(None, ("ctx", "fsdp")),
            P("ctx", None, "fsdp", None),
            P("ctx", "fsdp", None),
        ),
        check_vma=False,
    )
```

```python
import functools
import math

import jax
import jax.numpy as jnp
from jax import lax
from jax.experimental import pallas as pl
from jax.experimental.pallas import tpu as pltpu
from jax.sharding import PartitionSpec as P

MODEL_WIDTH = 1024
QUERY_HEADS = 16
KEY_VALUE_HEADS = 8
HEAD_WIDTH = 64
E = 32
TOP = 8
MOST = 40
SCHULZ_STEPS = 2


EPSILON = 1e-06
ROTARY_BASE = 10000.0
MOMENTUM_DECAY = 0.95
AVERAGE_DECAY = 0.9
SCHULZ_LINEAR = 3.4445
SCHULZ_SQUARE = -4.775
SCHULZ_CUBIC = 2.0315
WEIGHT_DECAY = 0.1
RATE_INPUT = 0.016
RATE_OUTPUT = 0.25
RATE_EXPERT = 0.031
RATE_DOWN = 0.031
RATE_GAIN = 0.5
RATE_ROUTER = 0.008
MASKED = -1e30

MESH = pl.DeviceIdType.MESH
RING = {"x": 4, "y": 4, "z": 4, "zh": 2, "zl": 2, "c": 2}
EVERY = ("y", "zh", "c", "x", "zl")
PAIRS = ("y", "zh", "c", "x")
ALONG_CTX = ("y", "zh", "c")
ALONG_FSDP = ("x", "zl")


def place():
    ctx = lax.axis_index("ctx")
    fsdp = lax.axis_index("fsdp")
    at = {"y": ctx // 4, "zh": (ctx // 2) % 2, "c": ctx % 2, "x": fsdp // 2, "zl": fsdp % 2}
    at["z"] = at["zh"] * 2 + at["zl"]
    return at


def moved(at, dim, to):
    at = dict(at)
    at[dim] = to
    if dim == "z":
        at["zh"], at["zl"] = to // 2, to % 2
    return at


def device_at(at):
    return ((at["y"] * 2 + at["zh"]) * 2 + at["c"], at["x"] * 2 + at["zl"])


def greet(peers):
    barrier = pltpu.get_barrier_semaphore()
    for peer in peers:
        pl.semaphore_signal(barrier, inc=1, device_id=peer, device_id_type=MESH)
    pl.semaphore_wait(barrier, len(peers))


def network_dims(jobs):
    found = []
    for dims, pieces in jobs:
        for piece in pieces:
            for dim in piece[-1]:
                if dim not in found:
                    found.append(dim)
    return found


def advance(live):
    while live:
        live = [f for f in live if next(f, "end") != "end"]


def gather_copies(jobs):
    total = 0
    for dims, pieces in jobs:
        for piece in pieces:
            shared = 0 if piece[-2] is None else 1
            total += shared
            for dim in piece[-1]:
                if dim != piece[-2]:
                    total += 1 + shared if RING[dim] == 2 else 4 + 3 * shared
    return total


def gather_kernel(jobs, paired, *refs):
    n = len(jobs)
    sources, targets = list(refs[:n]), refs[n : 2 * n]
    send_sems, recv_sems, local_sems = refs[2 * n : 2 * n + 3]
    me = place()
    dims_used = network_dims(jobs) + (["zl"] if paired else [])
    peers = []
    for dim in dims_used:
        size = RING[dim]
        for step in (1,) if size == 2 else (1, 3):
            peers.append(device_at(moved(me, dim, (me[dim] + step) % size)))

    def keep(j):
        dims = jobs[j][0]
        copy = pltpu.make_async_copy(
            sources[j],
            targets[j].at[(slice(None),) + tuple(me[d] for d in dims)],
            local_sems.at[j],
        )
        copy.start()
        return copy

    own = [] if paired else [keep(j) for j in range(n)]
    greet(peers)
    if paired:
        pair_sends, pair_recvs = refs[2 * n + 3 : 2 * n + 5]
        landings, joined = refs[2 * n + 5 : 3 * n + 5], refs[3 * n + 5 :]
        pairs = []
        for j in range(n):
            copy = pltpu.make_async_remote_copy(
                src_ref=sources[j],
                dst_ref=landings[j],
                send_sem=pair_sends.at[j],
                recv_sem=pair_recvs.at[j],
                device_id=device_at(moved(me, "zl", 1 - me["zl"])),
                device_id_type=MESH,
            )
            copy.start()
            pairs.append(copy)
        second = me["zl"] == 1
        for j, copy in enumerate(pairs):
            copy.wait()
            mine, other = sources[j][...], landings[j][...]
            joined[j][...] = jnp.concatenate(
                [jnp.where(second, other, mine), jnp.where(second, mine, other)], 1
            ).astype(joined[j].dtype)
            sources[j] = joined[j]
            own.append(keep(j))
    for copy in own:
        copy.wait()
    copies, shared = [], []

    def flow(j, dims, lead, leads, first, rows, share_to, order):
        target = targets[j]
        order = tuple(d for d in order if d != share_to)
        columns = target.shape[-1]

        def view(sel, half):
            place_in = (pl.ds(lead, leads),) + tuple(sel[d] for d in dims)
            if half is None:
                return target.at[place_in + (pl.ds(first, rows),)]
            if rows >= 32:
                return target.at[place_in + (pl.ds(first + half * (rows // 2), rows // 2),)]
            return target.at[
                place_in + (pl.ds(first, rows), pl.ds(half * (columns // 2), columns // 2))
            ]

        def send(sel, dim, to, half=None):
            k = len(copies)
            part = view(sel, half)
            copy = pltpu.make_async_remote_copy(
                src_ref=part,
                dst_ref=part,
                send_sem=send_sems.at[k],
                recv_sem=recv_sems.at[k],
                device_id=device_at(moved(me, dim, to)),
                device_id_type=MESH,
            )
            copy.start()
            copies.append(copy)
            return copy

        def share(sel):
            if share_to is not None:
                shared.append(send(sel, share_to, 1 - me[share_to]))

        def whole(sel, dim):
            if dim == "z":
                return dict(sel, zh=pl.ds(0, 2), zl=pl.ds(0, 2))
            return dict(sel, **{dim: pl.ds(0, RING[dim])})

        sel = dict(me)
        for at, dim in enumerate(order):
            if RING[dim] == 2:
                copy = send(sel, dim, 1 - me[dim])
                if at == 0:
                    share(sel)
                yield
                copy.wait_recv()
                share(moved(sel, dim, 1 - me[dim]))
            else:
                right, left = (me[dim] + 1) % 4, (me[dim] + 3) % 4
                up = send(sel, dim, right)
                down = send(sel, dim, left)
                if at == 0:
                    share(sel)
                yield
                up.wait_recv()
                on_up = send(moved(sel, dim, left), dim, right, 0)
                share(moved(sel, dim, left))
                down.wait_recv()
                on_down = send(moved(sel, dim, right), dim, left, 1)
                share(moved(sel, dim, right))
                yield
                on_up.wait_recv()
                on_down.wait_recv()
                share(moved(sel, dim, (me[dim] + 2) % 4))
            sel = whole(sel, dim)

    advance([flow(j, dims, *piece) for j, (dims, pieces) in enumerate(jobs) for piece in pieces])
    for copy in shared:
        copy.wait_recv()
    for copy in copies:
        copy.wait_send()


def gather(jobs, blocks, collective_id, paired=False):
    n = gather_copies(jobs)
    shapes = []
    for j, ((dims, _), b) in enumerate(zip(jobs, blocks)):
        lead, rows, columns = b.shape
        shapes.append(
            jax.ShapeDtypeStruct(
                (lead,) + tuple(RING[d] for d in dims) + (rows * 2 if paired else rows, columns),
                jnp.bfloat16 if paired else b.dtype,
            )
        )
    scratch = [
        pltpu.SemaphoreType.DMA((n,)),
        pltpu.SemaphoreType.DMA((n,)),
        pltpu.SemaphoreType.DMA((len(jobs),)),
    ]
    if paired:
        scratch += [pltpu.SemaphoreType.DMA((len(jobs),))] * 2
        scratch += [pltpu.VMEM(b.shape, jnp.float32) for b in blocks]
        scratch += [
            pltpu.VMEM((b.shape[0], b.shape[1] * 2, b.shape[2]), jnp.bfloat16) for b in blocks
        ]
    return pl.pallas_call(
        functools.partial(gather_kernel, jobs, paired),
        out_shape=shapes,
        in_specs=[pl.BlockSpec(memory_space=pltpu.VMEM)] * len(jobs),
        out_specs=[pl.BlockSpec(memory_space=pl.ANY)] * len(jobs),
        scratch_shapes=scratch,
        compiler_params=pltpu.CompilerParams(
            collective_id=collective_id, has_side_effects=True, vmem_limit_bytes=8 * 2**20
        ),
        cost_estimate=pl.CostEstimate(flops=0, bytes_accessed=60_000_000, transcendentals=0),
    )(*blocks)


def scatter_buffers(jobs, shapes):
    buffers, sems = [], 0
    for (dims, pieces), shape in zip(jobs, shapes):
        for _, leads, order in pieces:
            left = dims
            for dim in order:
                left = tuple(d for d in left if d != dim)
                block = (leads,) + tuple(RING[d] for d in left) + shape[-2:]
                buffers.append(pltpu.VMEM((RING[dim] - 1,) + block, jnp.bfloat16))
                if left:
                    buffers.append(pltpu.VMEM(block, jnp.bfloat16))
                sems += RING[dim] - 1
    return buffers, sems


def scatter_kernel(jobs, *refs):
    n = len(jobs)
    sources, targets = refs[:n], list(refs[n : 2 * n])
    buffers = list(refs[2 * n :])
    paired = [j for j in range(n) if jobs[j][0] == PAIRS]
    if paired:
        landings = {}
        for j in paired:
            targets[j], landings[j] = buffers.pop(0), buffers.pop(0)
        pair_sends, pair_recvs = buffers.pop(0), buffers.pop(0)
    send_sems, recv_sems = buffers[-2:]
    buffers = buffers[:-2]
    me = place()
    peers = []
    for dim in network_dims(jobs) + (["zl"] if paired and "zl" not in network_dims(jobs) else []):
        for step in range(1, RING[dim]):
            peers.append(device_at(moved(me, dim, (me[dim] + step) % RING[dim])))
    greet(peers)
    copies = []

    def flow(j, dims, lead, leads, order, held):
        current, left, base = sources[j], dims, lead
        for (landing, total), dim in zip(held, order):
            size = RING[dim]
            rest = tuple(d for d in left if d != dim)
            mine = []
            for step in range(1, size):
                to = (me[dim] + step) % size
                k = len(copies)
                index = tuple(to if d == dim else pl.ds(0, RING[d]) for d in left)
                copy = pltpu.make_async_remote_copy(
                    src_ref=current.at[(pl.ds(base, leads),) + index],
                    dst_ref=landing.at[step - 1],
                    send_sem=send_sems.at[k],
                    recv_sem=recv_sems.at[k],
                    device_id=device_at(moved(me, dim, to)),
                    device_id_type=MESH,
                )
                copy.start()
                copies.append(copy)
                mine.append(copy)
            yield
            for copy in mine:
                copy.wait_recv()
            to_base = 0 if rest else lead
            looped = rest[:1]
            trips = leads * math.prod(RING[d] for d in looped)

            def add(i, carry, current=current, landing=landing, total=total, left=left, base=base):
                at = i // RING[looped[0]] if looped else i
                inner = {looped[0]: i % RING[looped[0]]} if looped else {}
                inner[dim] = me[dim]
                index = tuple(inner.get(d, pl.ds(0, RING[d])) for d in left)
                value = current[(base + at,) + index].astype(jnp.float32)
                short = tuple(inner.get(d, pl.ds(0, RING[d])) for d in rest)
                for step in range(size - 1):
                    value += landing[(step, at) + short].astype(jnp.float32)
                total[(to_base + at,) + short] = value.astype(total.dtype)
                return carry

            lax.fori_loop(0, trips, add, 0)
            current, left, base = total, rest, 0

    live = []
    for j, (dims, pieces) in enumerate(jobs):
        for lead, leads, order in pieces:
            held, left = [], dims
            for dim in order:
                left = tuple(d for d in left if d != dim)
                landing = buffers.pop(0)
                held.append((landing, buffers.pop(0) if left else targets[j]))
            live.append(flow(j, dims, lead, leads, order, held))
    advance(live)
    for copy in copies:
        copy.wait_send()
    if paired:
        half = targets[paired[0]].shape[1] // 2
        theirs = pl.ds(pl.multiple_of((1 - me["zl"]) * half, half), half)
        ours = pl.ds(pl.multiple_of(me["zl"] * half, half), half)
        pairs = []
        for j in paired:
            copy = pltpu.make_async_remote_copy(
                src_ref=targets[j].at[:, theirs],
                dst_ref=landings[j],
                send_sem=pair_sends.at[j],
                recv_sem=pair_recvs.at[j],
                device_id=device_at(moved(me, "zl", 1 - me["zl"])),
                device_id_type=MESH,
            )
            copy.start()
            pairs.append(copy)
        for j, copy in zip(paired, pairs):
            copy.wait()
            refs[n + j][...] = targets[j][:, ours, :] + landings[j][...]


def scatter(jobs, blocks, collective_id):
    buffers, n = scatter_buffers(jobs, [b.shape for b in blocks])
    scratch = buffers + [pltpu.SemaphoreType.DMA((n,)), pltpu.SemaphoreType.DMA((n,))]
    shapes = [(b.shape[0],) + b.shape[-2:] for b in blocks]
    pairs = []
    for j, (dims, _) in enumerate(jobs):
        if dims == PAIRS:
            lead, rows, columns = shapes[j]
            shapes[j] = (lead, rows // 2, columns)
            pairs += [pltpu.VMEM((lead, rows, columns), jnp.float32), pltpu.VMEM(shapes[j], jnp.float32)]
    if pairs:
        scratch = pairs + [pltpu.SemaphoreType.DMA((len(jobs),))] * 2 + scratch
    return pl.pallas_call(
        functools.partial(scatter_kernel, jobs),
        out_shape=[jax.ShapeDtypeStruct(s, jnp.float32) for s in shapes],
        in_specs=[pl.BlockSpec(memory_space=pltpu.VMEM)] * len(jobs),
        out_specs=[pl.BlockSpec(memory_space=pltpu.VMEM)] * len(jobs),
        scratch_shapes=scratch,
        compiler_params=pltpu.CompilerParams(
            collective_id=collective_id, has_side_effects=True, vmem_limit_bytes=30 * 2**20
        ),
        cost_estimate=pl.CostEstimate(flops=0, bytes_accessed=60_000_000, transcendentals=0),
    )(*blocks)
CHUNK = 256


def transposed(left, right):
    return lax.dot_general(left, right, (((1,), (1,)), ((), ())), preferred_element_type=jnp.float32)


def on_rows(left, right):
    return lax.dot_general(left, right, (((0,), (0,)), ((), ())), preferred_element_type=jnp.float32)


def attend_kernel(query_ref, both_ref, key_at_ref, query_at_ref, mixed_ref, log_ref, score_ref):
    query = query_ref[0]
    query_at = query_at_ref[...]
    keys = both_ref.shape[1]
    peak = jnp.full((1, query.shape[0]), MASKED, jnp.float32)
    for start in range(0, keys, CHUNK):
        span = pl.ds(start, CHUNK)
        scores = transposed(both_ref[0, span], query)
        scores = jnp.where(key_at_ref[span] <= query_at, scores, MASKED)
        score_ref[span] = scores
        peak = jnp.maximum(peak, jnp.max(scores, 0, keepdims=True))
    total = jnp.zeros_like(peak)
    mixed = jnp.zeros((both_ref.shape[2], query.shape[0]), jnp.float32)
    for start in range(0, keys, CHUNK):
        span = pl.ds(start, CHUNK)
        weights = jnp.exp(score_ref[span] - peak)
        total += jnp.sum(weights, 0, keepdims=True)
        mixed += on_rows(both_ref[0, span], weights.astype(jnp.bfloat16))
    mixed_ref[0] = (mixed[HEAD_WIDTH:] / total).astype(mixed_ref.dtype)
    log_ref[0] = peak + jnp.log(total)


def attend_back_kernel(
    query_ref,
    both_ref,
    key_at_ref,
    query_at_ref,
    log_ref,
    upstream_ref,
    query_grad_ref,
    both_grad_ref,
    chance_ref,
    change_ref,
):
    query, upstream = query_ref[0], upstream_ref[0]
    query_at, log_total = query_at_ref[...], log_ref[0]
    keys = both_ref.shape[1]
    inner = jnp.zeros((1, query.shape[0]), jnp.float32)
    for start in range(0, keys, CHUNK):
        span = pl.ds(start, CHUNK)
        both = both_ref[0, span]
        scores = jnp.where(key_at_ref[span] <= query_at, transposed(both, query), MASKED)
        chance = jnp.exp(scores - log_total)
        change = transposed(both, upstream)
        chance_ref[span] = chance
        change_ref[span] = change
        inner += jnp.sum(chance * change, 0, keepdims=True)
    query_grad = jnp.zeros((both_ref.shape[2], query.shape[0]), jnp.float32)
    for start in range(0, keys, CHUNK):
        span = pl.ds(start, CHUNK)
        chance = chance_ref[span]
        grad_scores = (chance * (change_ref[span] - inner)).astype(jnp.bfloat16)
        both_grad_ref[0, span] = (
            jnp.dot(grad_scores, query, preferred_element_type=jnp.float32)
            + jnp.dot(
                chance.astype(jnp.bfloat16), upstream, preferred_element_type=jnp.float32
            )
        ).astype(both_grad_ref.dtype)
        query_grad += on_rows(both_ref[0, span], grad_scores)
    query_grad_ref[0] = query_grad[:HEAD_WIDTH]


def by_head(*block):
    return pl.BlockSpec((1,) + block, lambda g: (g, 0, 0))


def for_all(*block):
    return pl.BlockSpec(block, lambda g: (0, 0))


def attend(query, both, key_at, query_at):
    heads, queries, columns = query.shape
    keys = both.shape[1]
    return pl.pallas_call(
        attend_kernel,
        grid=(heads,),
        out_shape=[
            jax.ShapeDtypeStruct((heads, HEAD_WIDTH, queries), jnp.bfloat16),
            jax.ShapeDtypeStruct((heads, 1, queries), jnp.float32),
        ],
        in_specs=[
            by_head(queries, columns),
            by_head(keys, columns),
            for_all(keys, 1),
            for_all(1, queries),
        ],
        out_specs=[by_head(HEAD_WIDTH, queries), by_head(1, queries)],
        scratch_shapes=[pltpu.VMEM((keys, queries), jnp.float32)],
        compiler_params=pltpu.CompilerParams(vmem_limit_bytes=16 * 2**20),
        cost_estimate=pl.CostEstimate(
            flops=4 * heads * queries * keys * columns,
            bytes_accessed=6_000_000,
            transcendentals=heads * queries * keys,
        ),
    )(query, both, key_at, query_at)


def attend_back(query, both, key_at, query_at, log_total, upstream):
    heads, queries, columns = query.shape
    keys = both.shape[1]
    return pl.pallas_call(
        attend_back_kernel,
        grid=(heads,),
        out_shape=[
            jax.ShapeDtypeStruct((heads, HEAD_WIDTH, queries), jnp.float32),
            jax.ShapeDtypeStruct((heads, keys, columns), jnp.bfloat16),
        ],
        in_specs=[
            by_head(queries, columns),
            by_head(keys, columns),
            for_all(keys, 1),
            for_all(1, queries),
            by_head(1, queries),
            by_head(queries, columns),
        ],
        out_specs=[by_head(HEAD_WIDTH, queries), by_head(keys, columns)],
        scratch_shapes=[pltpu.VMEM((keys, queries), jnp.float32)] * 2,
        compiler_params=pltpu.CompilerParams(vmem_limit_bytes=20 * 2**20),
        cost_estimate=pl.CostEstimate(
            flops=10 * heads * queries * keys * columns,
            bytes_accessed=12_000_000,
            transcendentals=heads * queries * keys,
        ),
    )(query, both, key_at, query_at, log_total, upstream)


def project_kernel(tokens_ref, gain_ref, cosine_ref, sine_ref, *refs):
    weights, (normed_ref, query_ref, both_ref) = refs[:4], refs[4:]
    tokens = high(tokens_ref[...])
    inverse = lax.rsqrt(jnp.mean(tokens * tokens, -1, keepdims=True) + EPSILON)
    normed = low(tokens * inverse * gain_ref[...])
    normed_ref[...] = normed
    rows, width = normed.shape[0], 2 * HEAD_WIDTH
    lane = lax.broadcasted_iota(jnp.int32, (rows, width), 1)
    first_head = lane < HEAD_WIDTH
    leading = lane % HEAD_WIDTH < HEAD_WIDTH // 2
    cosine, sine = cosine_ref[...], sine_ref[...]

    def tiles(j):
        values = jnp.dot(normed, weights[j][...], preferred_element_type=jnp.float32)
        return [values[:, i * width : (i + 1) * width] for i in range(KEY_VALUE_HEADS // 2)]

    def turned(tile):
        behind = pltpu.roll(tile, HEAD_WIDTH // 2, 1)
        ahead = pltpu.roll(tile, width - HEAD_WIDTH // 2, 1)
        return tile * cosine + jnp.where(leading, -ahead, behind) * sine

    for j in range(2):
        for i, tile in enumerate(tiles(j)):
            tile = turned(tile) * (1.0 / math.sqrt(HEAD_WIDTH))
            for r, part in enumerate((tile, pltpu.roll(tile, HEAD_WIDTH, 1))):
                query_ref[j * 4 + i, pl.ds(r * rows, rows)] = low(jnp.where(first_head, part, 0.0))
    for i, (key, value) in enumerate(zip(tiles(2), tiles(3))):
        key = turned(key)
        both_ref[2 * i] = low(jnp.where(first_head, key, pltpu.roll(value, HEAD_WIDTH, 1)))
        both_ref[2 * i + 1] = low(jnp.where(first_head, pltpu.roll(key, HEAD_WIDTH, 1), value))


def project(tokens, gain, cosine, sine, weights):
    rows = tokens.shape[0]
    return pl.pallas_call(
        project_kernel,
        out_shape=[
            jax.ShapeDtypeStruct(tokens.shape, jnp.bfloat16),
            jax.ShapeDtypeStruct((KEY_VALUE_HEADS, 2 * rows, 2 * HEAD_WIDTH), jnp.bfloat16),
            jax.ShapeDtypeStruct((KEY_VALUE_HEADS, rows, 2 * HEAD_WIDTH), jnp.bfloat16),
        ],
        compiler_params=pltpu.CompilerParams(vmem_limit_bytes=16 * 2**20),
        cost_estimate=pl.CostEstimate(
            flops=540_000_000, bytes_accessed=6_000_000, transcendentals=0
        ),
    )(tokens, gain, cosine, sine, *weights)


def project_back_kernel(normed_ref, query_ref, both_ref, cosine_ref, sine_ref, *refs):
    weights, parts, grad_ref = refs[:4], refs[4:8], refs[8]
    normed = normed_ref[...]
    rows, width = normed.shape[0], 2 * HEAD_WIDTH
    lane = lax.broadcasted_iota(jnp.int32, (rows, width), 1)
    first_head = lane < HEAD_WIDTH
    leading = lane % HEAD_WIDTH < HEAD_WIDTH // 2
    cosine, sine = cosine_ref[...], sine_ref[...]
    keys, values = [], []
    for i in range(KEY_VALUE_HEADS // 2):
        even, odd = both_ref[2 * i], both_ref[2 * i + 1]
        tile = jnp.where(first_head, even, pltpu.roll(odd, HEAD_WIDTH, 1))
        behind = pltpu.roll(tile, HEAD_WIDTH // 2, 1)
        ahead = pltpu.roll(tile, width - HEAD_WIDTH // 2, 1)
        keys.append(low(tile * cosine + jnp.where(leading, ahead, -behind) * sine))
        values.append(low(jnp.where(first_head, pltpu.roll(even, HEAD_WIDTH, 1), odd)))
    total = None
    for j in range(4):
        grads = query_ref[j] if j < 2 else jnp.concatenate(keys if j == 2 else values, 1)
        parts[j][...] = low(on_rows(normed, grads))
        term = transposed(grads, weights[j][...])
        total = term if total is None else total + term
    grad_ref[...] = total


def project_back(normed, query_grads, both_grads, cosine, sine, weights):
    shape = weights[0].shape
    return pl.pallas_call(
        project_back_kernel,
        out_shape=[jax.ShapeDtypeStruct(shape, jnp.bfloat16)] * 4
        + [jax.ShapeDtypeStruct(normed.shape, jnp.float32)],
        compiler_params=pltpu.CompilerParams(vmem_limit_bytes=24 * 2**20),
        cost_estimate=pl.CostEstimate(
            flops=1_080_000_000, bytes_accessed=10_000_000, transcendentals=0
        ),
    )(normed, query_grads, both_grads, cosine, sine, *weights)


def expert_kernel(
    sent_ref,
    upstream_ref,
    picks_ref,
    gates_ref,
    inward_ref,
    outward_ref,
    rows_ref,
    grads_ref,
    hidden_ref,
    both_ref,
    back_ref,
    blend_ref,
    dgate_ref,
    found_ref,
):
    blocks, most = picks_ref.shape[1:3]

    def find(source):
        for b in range(blocks):
            found_ref[pl.ds(b * most, most)] = jnp.dot(
                picks_ref[0, b], source[b, :, :MODEL_WIDTH], preferred_element_type=jnp.float32
            )

    find(sent_ref)
    rows = found_ref[...].astype(jnp.bfloat16)
    rows_ref[0] = rows
    find(upstream_ref)
    gates = gates_ref[0]
    row_grads = (found_ref[...] * gates).astype(jnp.bfloat16)
    grads_ref[0] = row_grads
    upper = jnp.dot(rows, inward_ref[0, 0], preferred_element_type=jnp.float32)
    lower = jnp.dot(rows, inward_ref[0, 1], preferred_element_type=jnp.float32)
    sigmoid = jax.nn.sigmoid(upper)
    hidden = (upper * sigmoid * lower).astype(jnp.bfloat16)
    hidden_ref[0] = hidden
    grad_hidden = jnp.dot(row_grads, outward_ref[0], preferred_element_type=jnp.float32)
    grad_upper = (grad_hidden * lower * sigmoid * (1.0 + upper * (1.0 - sigmoid))).astype(
        jnp.bfloat16
    )
    grad_lower = (grad_hidden * (upper * sigmoid)).astype(jnp.bfloat16)
    both_ref[0, 0] = grad_upper
    both_ref[0, 1] = grad_lower
    outputs = transposed(hidden, outward_ref[0]).astype(jnp.bfloat16).astype(jnp.float32)
    dgate_ref[0] = jnp.sum(found_ref[...] * outputs, -1, keepdims=True)
    blend = outputs * gates
    for b in range(blocks):
        blend_ref[b, 0] = blend[b * most : (b + 1) * most].astype(jnp.bfloat16)
    back = transposed(grad_upper, inward_ref[0, 0]) + transposed(grad_lower, inward_ref[0, 1])
    for b in range(blocks):
        back_ref[b, 0] = back[b * most : (b + 1) * most].astype(jnp.bfloat16)


def expert_pass(sent, upstream, picks, gates, inward, outward):
    experts, blocks, most, rows = picks.shape
    capacity = blocks * most
    hidden = inward.shape[-1]

    def one(*block):
        return pl.BlockSpec((1,) + block, lambda e: (e,) + (0,) * len(block))

    def fixed(shape):
        return pl.BlockSpec(shape, lambda e: (0,) * len(shape), pipeline_mode=pl.Buffered(1))

    by_block = pl.BlockSpec((blocks, 1, most, MODEL_WIDTH), lambda e: (0, e, 0, 0))
    low_shape = functools.partial(jax.ShapeDtypeStruct, dtype=jnp.bfloat16)
    return pl.pallas_call(
        expert_kernel,
        grid=(experts,),
        out_shape=[
            low_shape((experts, capacity, MODEL_WIDTH)),
            low_shape((experts, capacity, MODEL_WIDTH)),
            low_shape((experts, capacity, hidden)),
            low_shape((experts, 2, capacity, hidden)),
            low_shape((blocks, experts, most, MODEL_WIDTH)),
            low_shape((blocks, experts, most, MODEL_WIDTH)),
            jax.ShapeDtypeStruct((experts, capacity, 1), jnp.float32),
        ],
        in_specs=[
            fixed(sent.shape),
            fixed(upstream.shape),
            one(blocks, most, rows),
            one(capacity, 1),
            one(2, MODEL_WIDTH, hidden),
            one(MODEL_WIDTH, hidden),
        ],
        out_specs=[
            one(capacity, MODEL_WIDTH),
            one(capacity, MODEL_WIDTH),
            one(capacity, hidden),
            one(2, capacity, hidden),
            by_block,
            by_block,
            one(capacity, 1),
        ],
        scratch_shapes=[pltpu.VMEM((capacity, MODEL_WIDTH), jnp.float32)],
        compiler_params=pltpu.CompilerParams(vmem_limit_bytes=48 * 2**20),
        cost_estimate=pl.CostEstimate(
            flops=16 * experts * capacity * MODEL_WIDTH * hidden,
            bytes_accessed=40_000_000,
            transcendentals=experts * capacity * hidden,
        ),
    )(sent, upstream, picks, gates, inward, outward)


def apply_rotation(tensor, cosine_values, sine_lookup):
    half_size = tensor.shape[-1] // 2
    leading = tensor[..., :half_size]
    trailing = tensor[..., half_size:]
    table_shape = (tensor.shape[0],) + (1,) * (tensor.ndim - 2) + (half_size,)
    cosine_values = cosine_values.reshape(table_shape)
    sine_lookup = sine_lookup.reshape(table_shape)
    return jnp.concatenate(
        [
            leading * cosine_values - trailing * sine_lookup,
            trailing * cosine_values + leading * sine_lookup,
        ],
        -1,
    )


def low(value):
    return value.astype(jnp.bfloat16)


def high(value):
    return value.astype(jnp.float32)


def product(spec, left, right):
    return jnp.einsum(spec, low(left), low(right), preferred_element_type=jnp.float32)


def orthogonal_kernel(matrix_ref, rows_ref, solved_ref):
    matrix = matrix_ref[...]
    norm = jnp.sqrt(jnp.sum(jnp.square(high(matrix)), keepdims=True)) + 1e-07
    scaled = high(rows_ref[...]) / norm
    gram = on_rows(matrix, matrix) / (norm * norm)

    def times(left, right):
        return jnp.dot(low(left), low(right), preferred_element_type=jnp.float32)

    for sweep_index in range(SCHULZ_STEPS):
        polynomial = SCHULZ_SQUARE * gram + SCHULZ_CUBIC * times(gram, gram)
        scaled = SCHULZ_LINEAR * scaled + times(scaled, polynomial)
        if sweep_index < SCHULZ_STEPS - 1:
            gram = SCHULZ_LINEAR * gram + times(gram, polynomial)
            gram = SCHULZ_LINEAR * gram + times(polynomial, gram)
    solved_ref[...] = (scaled * math.sqrt(MODEL_WIDTH)).astype(solved_ref.dtype)


def orthogonal(matrix, rows):
    return pl.pallas_call(
        orthogonal_kernel,
        out_shape=jax.ShapeDtypeStruct(rows.shape, jnp.bfloat16),
        compiler_params=pltpu.CompilerParams(vmem_limit_bytes=16 * 2**20),
        cost_estimate=pl.CostEstimate(
            flops=3_000_000_000, bytes_accessed=3_000_000, transcendentals=0
        ),
    )(matrix, rows)


def norm_backward(values_in, inverse, gain_row, grad_normed):
    weighted = gain_row * grad_normed
    grad_values = inverse * weighted - values_in * inverse**3 * jnp.mean(
        weighted * values_in, -1, keepdims=True
    )
    grad_gain = jnp.sum(grad_normed * values_in * inverse, 0)
    return (grad_values, grad_gain)


def two_halves(value):
    upper = low(value)
    return upper, low(value - high(upper))


def slots_of(chosen):
    rows = chosen.shape[1]
    before = jnp.tril(jnp.ones((rows, rows), jnp.bfloat16), -1)
    rank = jnp.einsum("st,bte->bes", before, low(chosen), preferred_element_type=jnp.float32)
    taken = jnp.swapaxes(chosen, 1, 2)
    slot = jnp.arange(MOST, dtype=jnp.int32)[None, None, :, None]
    filled = (rank.astype(jnp.int32)[:, :, None, :] == slot) & (taken[:, :, None, :] > 0.5)
    return filled


ONE_WAY, OTHER_WAY = ("zh", "x", "y", "c"), ("zh", "y", "x", "c")
ATTENTION_WEIGHTS = tuple(
    (PAIRS, ((0, 1, 0, 16, "c", ONE_WAY if i % 2 == 0 else OTHER_WAY),)) for i in range(7)
)


def over_fsdp(leads):
    return tuple(
        (i, 1, 0, 128) + ((None, ("zl", "x")) if i % 3 < 2 else ("zl", ("x", "zl")))
        for i in range(leads)
    )


KEYS_VALUES_EXPERTS = (
    (ALONG_CTX, tuple((i, 4, 0, 128, "c", ("zh", "y", "c")) for i in (0, 4))),
    (ALONG_FSDP, over_fsdp(4)),
)
TOKEN_ROWS = ((ALONG_CTX, tuple((0, 1, i, 64, "c", ("zh", "y", "c")) for i in (0, 64))),)
ATTENTION_MOMENTA = (
    (
        ALONG_FSDP,
        (
            (0, 1, 0, 64, None, ("zl", "x")),
            (0, 1, 64, 64, "zl", ("x", "zl")),
            (0, 1, 128, 16, None, ("zl", "x")),
        ),
    ),
)
SUM_ONE_WAY, SUM_OTHER_WAY = ("c", "x", "y", "zh"), ("c", "y", "x", "zh")
KEY_VALUE_SUMS = (
    (ALONG_CTX, ((0, 4, ("c", "y", "zh")), (4, 4, ("c", "y", "zh")))),
    (ALONG_FSDP, tuple((i, 1, ("x", "zl") if i % 2 == 0 else ("zl", "x")) for i in range(4))),
    (ALONG_FSDP, tuple((i, 1, ("x", "zl") if i % 2 == 0 else ("zl", "x")) for i in range(2))),
)
ATTENTION_SUMS = tuple(
    (PAIRS, ((0, 1, SUM_ONE_WAY if i % 2 == 0 else SUM_OTHER_WAY),)) for i in range(7)
)


def on_device(
    hidden_in,
    cotangent,
    block_deal,
    routes,
    query_key_value_weight,
    output_weight_matrix,
    router_weights,
    norm_gains,
    expert_in,
    expert_out,
    query_key_value_momentum,
    output_momentum,
    router_moment,
    gain_moment,
    in_moment,
    down_moment,
):
    ctx_count = lax.axis_size("ctx")
    fsdp_count = lax.axis_size("fsdp")
    ctx_index = lax.axis_index("ctx")
    rows = hidden_in.shape[1]
    sequence_length = rows * ctx_count
    half_rows = rows // 2
    shard = query_key_value_weight.shape[1]
    width = query_key_value_weight.shape[2]
    group_width = QUERY_HEADS // KEY_VALUE_HEADS
    score_scale = 1.0 / math.sqrt(HEAD_WIDTH)

    steps = jnp.arange(half_rows, dtype=jnp.int32)[None, :]
    token_positions = (block_deal[:, None] * half_rows + steps).reshape(sequence_length)
    local_deal = lax.dynamic_slice_in_dim(block_deal, ctx_index * 2, 2)
    local_pos = (local_deal[:, None] * half_rows + steps).reshape(rows)
    half_size = HEAD_WIDTH // 2
    powers = jnp.arange(half_size).astype(jnp.float32) * (2.0 / HEAD_WIDTH)
    frequency = jnp.exp(-math.log(ROTARY_BASE) * powers)
    angles = local_pos.astype(jnp.float32)[:, None] * frequency[None, :]
    cosine_values, sine_lookup = jnp.cos(angles), jnp.sin(angles)
    key_at = token_positions[:, None]
    query_at = jnp.tile(local_pos, group_width)[None, :]

    spare = jnp.concatenate([router_weights, norm_gains.T], 1)
    spare = jnp.pad(spare, ((0, 0), (0, width - E - 2)))
    *weights, spare_full = gather(
        ATTENTION_WEIGHTS,
        [
            high(block)[None]
            for block in [query_key_value_weight[j] for j in range(4)]
            + [output_weight_matrix[j] for j in range(2)]
            + [spare]
        ],
        1,
        paired=True,
    )
    weights = [w.reshape(MODEL_WIDTH, width) for w in weights]
    qkv_full, out_full = weights[:4], weights[4:]
    spare_full = spare_full.reshape(MODEL_WIDTH, width)
    router_full = spare_full[:, :E]
    gains_full = spare_full[:, E : E + 2].T

    part = expert_in.shape[2]
    experts_here = expert_in.shape[0]
    cotangent_all = lax.all_gather(cotangent[0], "ctx", axis=0)
    down_full = lax.all_gather(expert_out, "fsdp", axis=1, tiled=True)

    tokens = high(hidden_in[0])
    inverse_first = lax.rsqrt(jnp.mean(tokens * tokens, -1, keepdims=True) + EPSILON)
    gain_first = high(gains_full[0])
    cosine_tile = jnp.tile(cosine_values, (1, 4))
    sine_tile = jnp.tile(sine_lookup, (1, 4))
    normed, queries, keys_values = project(
        hidden_in[0], gain_first[None], cosine_tile, sine_tile, qkv_full
    )
    keys_values, gateup_full = gather(
        KEYS_VALUES_EXPERTS,
        [
            keys_values,
            expert_in.reshape(2 * experts_here, part, width),
        ],
        2,
    )
    gateup_full = gateup_full.reshape(experts_here, 2, MODEL_WIDTH, width)
    keys_values = keys_values.reshape(KEY_VALUE_HEADS, sequence_length, 2 * HEAD_WIDTH)

    def heads_first(values, before, after):
        values = values.reshape(rows, KEY_VALUE_HEADS, group_width, HEAD_WIDTH)
        values = values.transpose(1, 2, 0, 3).reshape(KEY_VALUE_HEADS, group_width * rows, HEAD_WIDTH)
        return jnp.pad(values, ((0, 0), (0, 0), (before, after)))

    def rows_first(values):
        values = values.reshape(KEY_VALUE_HEADS, HEAD_WIDTH, group_width, rows)
        return values.transpose(3, 0, 2, 1).reshape(rows, 2, width)

    mixture, log_total = attend(queries, keys_values, key_at, query_at)
    mixture_rows = rows_first(mixture)
    residual = tokens + sum(
        product("tw,dw->td", mixture_rows[:, j], out_full[j]) for j in range(2)
    )
    inverse_second = lax.rsqrt(jnp.mean(residual * residual, -1, keepdims=True) + EPSILON)
    gain_second = high(gains_full[1])
    normed_second = low(residual * inverse_second * gain_second)
    logits = product("td,de->te", normed_second, router_full)
    routed = routes[0]
    chosen = jnp.sum(
        high(routed[:, :, None] == jnp.arange(E, dtype=jnp.int32)[None, None, :]), 1
    )
    peak = jnp.max(jnp.where(chosen > 0.5, logits, MASKED), -1, keepdims=True)
    weighed = jnp.where(chosen > 0.5, jnp.exp(jnp.minimum(logits - peak, 0.0)), 0.0)
    gates = weighed / jnp.sum(weighed, -1, keepdims=True)
    upstream = high(cotangent[0])

    gate_upper, gate_lower = two_halves(gates)
    (sent,) = gather(
        TOKEN_ROWS,
        [
            jnp.concatenate(
                [normed_second, gate_upper, gate_lower, low(chosen), jnp.zeros_like(gate_upper)], 1
            )[None]
        ],
        3,
    )
    sent = sent.reshape(ctx_count, rows, MODEL_WIDTH + 4 * E)

    def mine(start):
        return lax.dynamic_slice_in_dim(
            sent, MODEL_WIDTH + start + ctx_index * experts_here, experts_here, 2
        )

    gates_mine = high(mine(0)) + high(mine(E))
    filled = slots_of(high(mine(2 * E)))
    picks = low(filled)
    capacity = ctx_count * MOST
    row_gates = jnp.sum(
        jnp.where(filled, jnp.swapaxes(gates_mine, 1, 2)[:, :, None, :], 0.0), -1
    ).transpose(1, 0, 2).reshape(experts_here, capacity, 1)

    expert_rows, row_grads, hidden, grad_both, back_rows, blend_sent, row_dgate = expert_pass(
        sent, cotangent_all, picks.transpose(1, 0, 2, 3), row_gates, gateup_full, down_full
    )
    row_dgate = row_dgate.reshape(experts_here, ctx_count, MOST).transpose(1, 0, 2)
    dgate_upper, dgate_lower = two_halves(row_dgate.reshape(ctx_count, experts_here * MOST))
    dgate_rows = jnp.stack([dgate_upper, dgate_lower], 1)
    dgate_rows = jnp.pad(
        dgate_rows, ((0, 0), (0, 6), (0, MODEL_WIDTH - experts_here * MOST))
    )
    back_rows = back_rows.reshape(ctx_count, experts_here * MOST, MODEL_WIDTH)
    back_sent = jnp.concatenate([back_rows, dgate_rows], 1)
    back_returned = lax.all_to_all(back_sent, "ctx", split_axis=0, concat_axis=0, tiled=True)
    blend_sent = blend_sent.reshape(ctx_count, experts_here * MOST, MODEL_WIDTH)
    blend_sent, back_returned = lax.optimization_barrier((blend_sent, back_returned))
    blend_returned = lax.all_to_all(blend_sent, "ctx", split_axis=0, concat_axis=0, tiled=True)

    grad_gateup = low(product("erd,ejrf->ejdf", expert_rows, grad_both))
    grad_down = low(product("erd,erf->edf", row_grads, hidden))

    own_filled = slots_of(chosen[None])[0]
    own_picks = low(own_filled).reshape(E * MOST, rows)
    back_picks = jnp.pad(
        own_picks.reshape(ctx_count, experts_here * MOST, rows), ((0, 0), (0, 8), (0, 0))
    )
    back_sum = product(
        "st,sd->td", back_picks.reshape(-1, rows), back_returned.reshape(-1, MODEL_WIDTH)
    )
    own_dgate = high(back_returned[:, experts_here * MOST, : experts_here * MOST]) + high(
        back_returned[:, experts_here * MOST + 1, : experts_here * MOST]
    )
    grad_gates = jnp.sum(
        jnp.where(own_filled, own_dgate.reshape(E, MOST, 1), 0.0), 1
    ).T
    grad_logits = low(gates * (grad_gates - jnp.sum(gates * grad_gates, -1, keepdims=True)))
    grad_router_part = product("td,te->de", normed_second, grad_logits)
    grad_normed_second = back_sum + product("te,de->td", grad_logits, router_full)
    grad_residual_norm, grad_gain_second = norm_backward(
        residual, inverse_second, gain_second, grad_normed_second
    )
    grad_residual = upstream + grad_residual_norm
    grad_attention = low(grad_residual)
    grad_out_parts = [product("td,tw->dw", grad_attention, mixture_rows[:, j]) for j in range(2)]
    mixture_gradient = low(
        jnp.stack([product("td,dw->tw", grad_attention, out_full[j]) for j in range(2)], 1)
    )
    query_gradient, grad_keys_values = attend_back(
        queries,
        keys_values,
        key_at,
        query_at,
        log_total,
        heads_first(mixture_gradient, HEAD_WIDTH, 0),
    )
    query_gradient = rows_first(query_gradient * score_scale)

    def as_pairs(part):
        return low(part).reshape(1, 4, 2, 2, 4, 2 * shard, width)

    local_gradient, in_grad, down_grad = scatter(
        KEY_VALUE_SUMS,
        [
            grad_keys_values.reshape(KEY_VALUE_HEADS, 4, 2, 2, rows, 2 * HEAD_WIDTH),
            grad_gateup.reshape(2 * experts_here, 4, 2, part, width),
            grad_down.reshape(experts_here, 4, 2, part, width),
        ],
        4,
    )
    in_grad = in_grad.reshape(experts_here, 2, part, width)
    in_moment_new = MOMENTUM_DECAY * in_moment + in_grad
    down_moment_new = MOMENTUM_DECAY * down_moment + down_grad
    expert_count = experts_here * 3
    expert_stack = low(jnp.concatenate([in_moment_new, down_moment_new[:, None]], 1)).reshape(
        expert_count, part, width
    )
    expert_stack = jnp.pad(expert_stack, ((0, fsdp_count - expert_count), (0, 0), (0, 0)))
    expert_part = lax.all_to_all(expert_stack, "fsdp", split_axis=0, concat_axis=0, tiled=True)
    query_row_gradient = apply_rotation(
        query_gradient.reshape(rows, 2, KEY_VALUE_HEADS, HEAD_WIDTH), cosine_values, -sine_lookup
    )
    *grad_qkv_parts, grad_normed_first = project_back(
        normed,
        low(query_row_gradient.reshape(rows, 2, width)).transpose(1, 0, 2),
        local_gradient,
        cosine_tile,
        sine_tile,
        qkv_full,
    )
    grad_tokens_norm, grad_gain_first = norm_backward(
        tokens, inverse_first, gain_first, grad_normed_first
    )
    input_grad = (grad_residual + grad_tokens_norm)[None]

    gains_part = jnp.stack([grad_gain_first, grad_gain_second], 1)
    spare_part = low(jnp.concatenate([grad_router_part, gains_part], 1))
    spare_part = jnp.pad(spare_part, ((0, 0), (0, width - E - 2)))
    parts = [as_pairs(part) for part in grad_qkv_parts + grad_out_parts + [spare_part]]
    parts[0], expert_part, blend_returned = lax.optimization_barrier(
        (parts[0], expert_part, blend_returned)
    )
    summed = scatter(ATTENTION_SUMS, parts, 5)
    qkv_grad, out_grad = jnp.concatenate(summed[:4], 0), jnp.concatenate(summed[4:6], 0)
    router_grad = summed[6][0, :, :E]
    gain_grad = summed[6][0, :, E : E + 2].T
    qkv_moment_new = MOMENTUM_DECAY * query_key_value_momentum + qkv_grad
    out_moment_new = MOMENTUM_DECAY * output_momentum + out_grad
    gain_moment_new = AVERAGE_DECAY * gain_moment + (1.0 - AVERAGE_DECAY) * gain_grad
    router_moment_new = AVERAGE_DECAY * router_moment + (1.0 - AVERAGE_DECAY) * router_grad
    squares = jnp.concatenate(
        [
            jnp.sum(gain_moment_new * gain_moment_new, 1),
            jnp.sum(router_moment_new * router_moment_new)[None],
        ]
    )

    def squares_rows(count):
        upper = low(squares)
        row = jnp.concatenate([upper, low(squares - high(upper))])
        return jnp.pad(row[None], ((0, count - 1), (0, width - 6)))

    def squares_total(row):
        row = jnp.sum(high(row), 0)
        return row[:3] + row[3:6]

    attn_stack = low(jnp.concatenate([qkv_moment_new, out_moment_new], 0))
    attn_stack = jnp.pad(attn_stack, ((0, ctx_count - 6), (0, 0), (0, 0)))
    attn_stack = jnp.concatenate(
        [attn_stack, jnp.broadcast_to(squares_rows(shard)[None], attn_stack.shape)], 1
    )
    attn_rows = lax.all_to_all(attn_stack, "ctx", split_axis=0, concat_axis=0, tiled=True)
    squares = squares_total(attn_rows[:, shard, :6])
    attn_rows = attn_rows[:, :shard].reshape(ctx_count * shard, width)
    expert_part = expert_part.reshape(MODEL_WIDTH, width)
    expert_solved = orthogonal(expert_part, expert_part)
    attn_rows, expert_solved = lax.optimization_barrier((attn_rows, expert_solved))
    expert_ortho = lax.all_to_all(
        expert_solved.reshape(fsdp_count, part, width),
        "fsdp",
        split_axis=0,
        concat_axis=0,
        tiled=True,
    )
    (attn_full,) = gather(
        ATTENTION_MOMENTA, [jnp.concatenate([attn_rows, squares_rows(2 * shard)], 0)[None]], 6
    )
    attn_full, expert_ortho = lax.optimization_barrier((attn_full, expert_ortho))
    attn_full = attn_full.reshape(fsdp_count, (ctx_count + 2) * shard, width)
    squares = squares_total(attn_full[:, ctx_count * shard, :6])
    attn_full = attn_full[:, : ctx_count * shard].reshape(MODEL_WIDTH, width)
    attn_solved = orthogonal(attn_full, attn_rows)
    attn_ortho = lax.all_to_all(
        attn_solved.reshape(ctx_count, shard, width),
        "ctx",
        split_axis=0,
        concat_axis=0,
        tiled=True,
    )
    attn_ortho = high(attn_ortho[:6])
    expert_ortho = high(expert_ortho[:expert_count]).reshape(experts_here, 3, part, width)
    in_new = (
        high(expert_in) * (1.0 - RATE_EXPERT * WEIGHT_DECAY) - RATE_EXPERT * expert_ortho[:, :2]
    )
    down_new = (
        high(expert_out) * (1.0 - RATE_DOWN * WEIGHT_DECAY) - RATE_DOWN * expert_ortho[:, 2]
    )
    qkv_new = (
        high(query_key_value_weight) * (1.0 - RATE_INPUT * WEIGHT_DECAY)
        - RATE_INPUT * attn_ortho[:4]
    )
    out_new = (
        high(output_weight_matrix) * (1.0 - RATE_OUTPUT * WEIGHT_DECAY)
        - RATE_OUTPUT * attn_ortho[4:6]
    )

    gains_new = (
        high(norm_gains)
        - RATE_GAIN * gain_moment_new * lax.rsqrt(squares[:2] / MODEL_WIDTH + EPSILON)[:, None]
    )
    router_new = high(router_weights) - RATE_ROUTER * router_moment_new * lax.rsqrt(
        squares[2] / (MODEL_WIDTH * E) + EPSILON
    )
    hidden_out = low(
        residual + product("st,sd->td", own_picks, blend_returned.reshape(E * MOST, MODEL_WIDTH))
    )[None]
    return (
        hidden_out,
        input_grad,
        qkv_grad,
        out_grad,
        router_grad,
        gain_grad,
        in_grad,
        down_grad,
        qkv_moment_new,
        out_moment_new,
        router_moment_new,
        gain_moment_new,
        in_moment_new,
        down_moment_new,
        qkv_new,
        out_new,
        router_new,
        gains_new,
        in_new,
        down_new,
    )


def solution(mesh):
    placed = (
        P("fsdp", "ctx", None),
        P("fsdp", "ctx", None),
        P(),
        P("fsdp", "ctx", None),
        P(None, ("ctx", "fsdp"), None),
        P(None, ("ctx", "fsdp"), None),
        P(("ctx", "fsdp"), None),
        P(None, ("ctx", "fsdp")),
        P("ctx", None, "fsdp", None),
        P("ctx", "fsdp", None),
        P(None, ("ctx", "fsdp"), None),
        P(None, ("ctx", "fsdp"), None),
        P(("ctx", "fsdp"), None),
        P(None, ("ctx", "fsdp")),
        P("ctx", None, "fsdp", None),
        P("ctx", "fsdp", None),
    )
    return jax.shard_map(
        on_device,
        mesh=mesh,
        in_specs=placed,
        out_specs=(
            P("fsdp", "ctx", None),
            P("fsdp", "ctx", None),
            P(None, ("ctx", "fsdp"), None),
            P(None, ("ctx", "fsdp"), None),
            P(("ctx", "fsdp"), None),
            P(None, ("ctx", "fsdp")),
            P("ctx", None, "fsdp", None),
            P("ctx", "fsdp", None),
            P(None, ("ctx", "fsdp"), None),
            P(None, ("ctx", "fsdp"), None),
            P(("ctx", "fsdp"), None),
            P(None, ("ctx", "fsdp")),
            P("ctx", None, "fsdp", None),
            P("ctx", "fsdp", None),
            P(None, ("ctx", "fsdp"), None),
            P(None, ("ctx", "fsdp"), None),
            P(("ctx", "fsdp"), None),
            P(None, ("ctx", "fsdp")),
            P("ctx", None, "fsdp", None),
            P("ctx", "fsdp", None),
        ),
        check_vma=False,
    )
```
